32 devices in a mesh: fsdp: 16 (over z, y, x), tp: 2 (over core).
Axes of the slice: x: 2, y: 2, z: 4, core: 2. Of those that a mesh axis runs over, the one named last changes fastest.
Arguments:
- hidden_in: bfloat16 [4096, 2048], P(('fsdp', 'tp')), may hold values from -6 to 6
- routes: int32 [4096, 6], P('fsdp'), may hold values from 0 to 15, all different within a row; in each aligned block of 256 rows (0 to 255, 256 to 511, ...) at most 128 rows name the same one
- cotangent: bfloat16 [4096, 2048], P('fsdp'), may hold values from -6 to 6
- norm_attn: bfloat16 [2048], P('fsdp'), may hold values from 0.5 to 1.5
- query_proj: bfloat16 [2048, 3072], P('fsdp', 'tp'), may hold values from -0.25 to 0.25
- kv_down: bfloat16 [2048, 576], P('fsdp'), may hold values from -0.125 to 0.125
- kv_norm: bfloat16 [512], P('fsdp'), may hold values from 0.5 to 1.5
- kv_up: bfloat16 [512, 4096], P('fsdp', 'tp'), may hold values from -0.25 to 0.25
- out_proj: bfloat16 [2048, 2048], P('tp', 'fsdp'), may hold values from -0.75 to 0.75
- norm_ffn: bfloat16 [2048], P('fsdp'), may hold values from 0.5 to 1.5
- router_proj: bfloat16 [2048, 16], P('fsdp'), may hold values from -0.0625 to 0.0625
- shared_gate: bfloat16 [2048, 2816], P('fsdp', 'tp'), may hold values from -0.125 to 0.125
- shared_up: bfloat16 [2048, 2816], P('fsdp', 'tp'), may hold values from -0.125 to 0.125
- shared_down: bfloat16 [2816, 2048], P('tp', 'fsdp'), may hold values from -0.109375 to 0.109375
- expert_gate: bfloat16 [16, 2048, 1408], P('fsdp', None, 'tp'), may hold values from -0.125 to 0.125
- expert_up_weight: bfloat16 [16, 2048, 1408], P('fsdp', None, 'tp'), may hold values from -0.125 to 0.125
- expert_down: bfloat16 [16, 1408, 2048], P('fsdp', 'tp'), may hold values from -0.15625 to 0.15625
Outputs:
- hidden_out: bfloat16 [4096, 2048], P(('fsdp', 'tp'))
- grad_in: bfloat16 [4096, 2048], P(('fsdp', 'tp'))
- grad_norm_attn: float32 [2048], P(('fsdp', 'tp'))
- grad_query_proj: float32 [2048, 3072], P('fsdp', 'tp')
- grad_kv_down: float32 [2048, 576], P(('fsdp', 'tp'))
- grad_kv_norm: float32 [512], P(('fsdp', 'tp'))
- grad_kv_up: float32 [512, 4096], P('fsdp', 'tp')
- grad_out_proj: float32 [2048, 2048], P('tp', 'fsdp')
- grad_norm_ffn: float32 [2048], P(('fsdp', 'tp'))
- grad_router: float32 [2048, 16], P(('fsdp', 'tp'))
- grad_shared_gate: float32 [2048, 2816], P('fsdp', 'tp')
- grad_shared_up: float32 [2048, 2816], P('fsdp', 'tp')
- grad_shared_down: float32 [2816, 2048], P('tp', 'fsdp')
- grad_expert_gate: float32 [16, 2048, 1408], P('fsdp', None, 'tp')
- grad_expert_up: float32 [16, 2048, 1408], P('fsdp', None, 'tp')
- grad_expert_down: float32 [16, 1408, 2048], P('fsdp', 'tp')
The draws below stay inside these ranges and needn't reach their ends.
Inputs may be any that keep to these rules, and one draw needn't show every extreme that they name: `routes`: each row names 6 different experts; in the rows of one sequence no expert is named more than 128 times, a bound that some block reaches.
All inputs are finite; a program needn't handle non-finite values.
Results may differ from the reference program's by a relative error of at most 0.02.
Values may be sent and summed in bfloat16 or wider, within the bound.
A program may use at most 256 MiB of HBM per device.

```python
import math
from functools import partial
import jax
import jax.numpy as jnp
import numpy as np
from jax import lax

MODEL_WIDTH = 2048
H = 16
DN = 128
DR = 64
DV = 128
KVR = 512
FFE = 1408
TOP = 6
SFF = 2816
EXPERTS = 16
SEQ = 256
TOKENS = 4096
CAP = 128
N_TP = 2


def levels(key, shape, cuts, least, high):
    loudness, own = 1.0, jax.random.fold_in(key, 6)
    for dim, parts in cuts:
        heights = jnp.exp(jax.random.uniform(jax.random.fold_in(own, dim), (parts,), jnp.float32, least / len(cuts), high / len(cuts)))
        loudness = loudness * jnp.repeat(heights, shape[dim] // parts).reshape([-1 if axis == dim else 1 for axis in range(len(shape))])
    return loudness


def routed_block(own_key, own, number, rows, amount, top, reach, skew):
    order = jax.random.permutation(own_key, amount)
    heavy_load, common = load_shares(amount, rows * top, reach, skew, True), load_shares(amount, rows * top, reach, skew, False)
    places = jnp.arange(amount)

    def named(lengths, rotation):
        used = int((lengths > 0).sum())
        fixed = max(1, used // 4)
        shifted = fixed + (places - fixed + rotation * (used - fixed)) % max(1, amount - fixed)
        return jnp.zeros((amount,), jnp.int32).at[order[jnp.where(places < fixed, places, shifted)]].set(jnp.asarray(lengths, jnp.int32))

    lengths = jnp.where(number % 4 == 0, named(heavy_load, number // 4), named(common, number - number // 4 - 1))
    mixed = jax.random.permutation(jax.random.fold_in(own, 3), amount)
    giver, sink = mixed[0:amount // 2 * 2:2], mixed[1:amount // 2 * 2:2]
    slack = jnp.minimum(lengths[giver] - 1, reach - lengths[sink]) // 2
    slack = jnp.where((giver == order[0]) | (sink == order[0]) | (lengths[sink] == 0), 0, jnp.maximum(slack, 0))
    shifted = jax.random.randint(jax.random.fold_in(own, 4), (amount // 2,), 0, 1 << 20) % (slack + 1)
    lengths = lengths.at[giver].add(-shifted).at[sink].add(shifted)
    labels = jnp.searchsorted(jnp.cumsum(lengths), jnp.arange(rows * top), side="right").astype(jnp.int32)
    table = labels.reshape(top, rows).T
    table = table[jax.random.permutation(jax.random.fold_in(own, 1), rows)]
    rotation = jax.random.randint(jax.random.fold_in(own, 2), (rows, 1), 0, top)
    return jnp.take_along_axis(table, (jnp.arange(top)[None, :] + rotation) % top, axis=1)


def load_shares(number_of, total, most, lean, full):
    weights = [(1 << 20) // math.isqrt(rank ** lean) + 1 for rank in range(1, number_of + 1)]
    largest = most if full else min(most, max(-(-total // number_of), total * weights[0] // sum(weights)))
    least = 1 if total - largest >= number_of - 1 else 0
    counts, spare = [largest] + [least] * (number_of - 1), total - largest - least * (number_of - 1)
    while spare > 0:
        candidates = [i for i in range(1, number_of) if counts[i] < largest] or [i for i in range(1, number_of) if counts[i] < most]
        whole, budget = sum([weights[i] for i in candidates]), spare
        for i in candidates:
            addition = min(most - counts[i], max(1, budget * weights[i] // whole), spare)
            counts[i] = counts[i] + addition
            spare = spare - addition
    return np.array(counts)


def normal_values(rng, shape, deviation, most, split=(), kind=jnp.bfloat16):
    array = deviation * jax.random.normal(rng, shape, jnp.float32)
    if split:
        array = array * levels(rng, shape, split, -0.22, 0.18)
    return jnp.clip(array, -most, most).astype(kind)


def setup_inputs(seed: int = 0) -> dict:
    streams_of = jax.random.split(jax.random.key(seed), 18)
    hidden_in = normal_values(streams_of[0], (TOKENS, MODEL_WIDTH), 1.0, 6.0, ((0, 32),))
    routes_keys = jax.random.split(jax.random.fold_in(streams_of[1], 1), TOKENS // SEQ)
    routes_turns = jax.random.permutation(jax.random.fold_in(streams_of[1], 3), TOKENS // SEQ)
    routes = jax.vmap(lambda own, number: routed_block(jax.random.fold_in(streams_of[1], 2), own, number, SEQ, EXPERTS, TOP, CAP, 1))(routes_keys, routes_turns).reshape((TOKENS, TOP))
    cotangent = normal_values(streams_of[2], (TOKENS, MODEL_WIDTH), 1.0, 6.0, ((0, 16),))
    norm_attn = jnp.clip(1.0 + 0.1 * jax.random.normal(streams_of[3], (MODEL_WIDTH,), jnp.float32), 0.5, 1.5).astype(jnp.bfloat16)
    query_proj = normal_values(streams_of[4], (MODEL_WIDTH, H * (DN + DR)), (MODEL_WIDTH // 4) ** -0.5, 0.25, ((0, 16), (1, 2)))
    kv_down = normal_values(streams_of[5], (MODEL_WIDTH, KVR + DR), MODEL_WIDTH ** -0.5, 0.125, ((0, 16),))
    kv_norm = jnp.clip(1.0 + 0.1 * jax.random.normal(streams_of[6], (KVR,), jnp.float32), 0.5, 1.5).astype(jnp.bfloat16)
    kv_up = normal_values(streams_of[7], (KVR, H * (DN + DV)), KVR ** -0.5, 0.25, ((0, 16), (1, 2)))
    out_proj = normal_values(streams_of[8], (H * DV, MODEL_WIDTH), (max(H * DV // 32, 16)) ** -0.5, 0.75, ((0, 2), (1, 16)))
    norm_ffn = jnp.clip(1.0 + 0.1 * jax.random.normal(streams_of[9], (MODEL_WIDTH,), jnp.float32), 0.5, 1.5).astype(jnp.bfloat16)
    router_proj = normal_values(streams_of[10], (MODEL_WIDTH, EXPERTS), (4 * MODEL_WIDTH) ** -0.5, 0.0625, ((0, 16),))
    shared_gate = normal_values(streams_of[11], (MODEL_WIDTH, SFF), MODEL_WIDTH ** -0.5, 0.125, ((0, 16), (1, 2)))
    shared_up = normal_values(streams_of[12], (MODEL_WIDTH, SFF), MODEL_WIDTH ** -0.5, 0.125, ((0, 16), (1, 2)))
    shared_down = normal_values(streams_of[13], (SFF, MODEL_WIDTH), SFF ** -0.5, 0.109375, ((0, 2), (1, 16)))
    expert_gate = normal_values(streams_of[14], (EXPERTS, MODEL_WIDTH, FFE), MODEL_WIDTH ** -0.5, 0.125, ((0, 16), (2, 2)))
    expert_up_weight = normal_values(streams_of[15], (EXPERTS, MODEL_WIDTH, FFE), MODEL_WIDTH ** -0.5, 0.125, ((0, 16), (2, 2)))
    expert_down = normal_values(streams_of[16], (EXPERTS, FFE, MODEL_WIDTH), FFE ** -0.5, 0.15625, ((0, 16), (1, 2)))
    return dict(hidden_in=hidden_in, routes=routes, cotangent=cotangent, norm_attn=norm_attn, query_proj=query_proj, kv_down=kv_down, kv_norm=kv_norm, kv_up=kv_up, out_proj=out_proj, norm_ffn=norm_ffn, router_proj=router_proj, shared_gate=shared_gate, shared_up=shared_up, shared_down=shared_down, expert_gate=expert_gate, expert_up_weight=expert_up_weight, expert_down=expert_down)


NORM_EPS = 1e-06
ROPE_THETA = 50000.0
ROUTE_SCALE = 2.446

@jax.custom_vjp
def low(v):
    return lax.optimization_barrier(v.astype(jnp.bfloat16)).astype(jnp.float32)

@jax.custom_vjp
def low_back(v):
    return v

def low_keep(v):
    return (low(v), None)

def low_pass(kept, grad):
    return (grad,)

def back_keep(v):
    return (v, None)

def back_low(kept, grad):
    return (low(grad),)
low.defvjp(low_keep, low_pass)
low_back.defvjp(back_keep, back_low)

def low_both(value):
    return low(low_back(value))

def matmul(left, right):
    return jnp.dot(left, right, precision=lax.Precision.HIGHEST, preferred_element_type=jnp.float32)

def normed(value, gain):
    return value * lax.rsqrt(lax.optimization_barrier(jnp.mean(value * value, axis=-1, keepdims=True)) + NORM_EPS) * gain

def rope_tables():
    half_width = DR // 2
    freq = ROPE_THETA ** (-(jnp.arange(half_width, dtype=jnp.float32) * 2.0 / DR))
    angle = jnp.arange(SEQ, dtype=jnp.float32)[:, None] * freq[None, :]
    return (jnp.cos(angle), jnp.sin(angle))

def rotate(value, cos_table, sin_table):
    half_width = value.shape[-1] // 2
    first, second = (value[..., :half_width], value[..., half_width:])
    return jnp.concatenate([first * cos_table - second * sin_table, second * cos_table + first * sin_table], -1)

def attend(query, keys, values):
    length = query.shape[0]
    scores = jnp.einsum('qhd,khd->hqk', query, keys, precision=lax.Precision.HIGHEST) * (1.0 / math.sqrt(DN + DR))
    scores = low_back(scores)
    causal = jnp.arange(length)[:, None] >= jnp.arange(length)[None, :]
    weights = jax.nn.softmax(jnp.where(causal[None], scores, -1e+30), axis=-1)
    weights = low(weights)
    return jnp.einsum('hqk,khd->qhd', weights, values, precision=lax.Precision.HIGHEST)

def attention_block(seq_rows, norm_attn, query_proj, kv_down, kv_norm, kv_up, out_proj):
    cos_table, sin_table = rope_tables()
    normed_in = low(normed(seq_rows, norm_attn))
    query_raw = low_back(matmul(normed_in, query_proj)).reshape(SEQ, H, DN + DR)
    query = low(jnp.concatenate([query_raw[..., :DN], rotate(query_raw[..., DN:], cos_table[:, None], sin_table[:, None])], -1))
    kv_first = matmul(normed_in, kv_down)
    latent_normed = low(normed(kv_first[:, :KVR], kv_norm))
    key_rope = low(rotate(kv_first[:, KVR:], cos_table, sin_table))
    kv_full = low_both(matmul(latent_normed, kv_up)).reshape(SEQ, H, DN + DV)
    keys = jnp.concatenate([kv_full[..., :DN], jnp.broadcast_to(key_rope[:, None, :], (SEQ, H, DR))], -1)
    context = attend(query, keys, kv_full[..., DN:])
    context = low_both(context.reshape(SEQ, H * DV))
    return low_back(matmul(context, out_proj))

def slot_tables(routes):
    groups = routes.reshape(TOKENS // SEQ, SEQ * TOP)
    one_hot = (groups[..., None] == jnp.arange(EXPERTS, dtype=jnp.int32)[None, None, :]).astype(jnp.int32)
    earlier = jnp.cumsum(one_hot, axis=1) - one_hot
    slot_num = lax.optimization_barrier(jnp.sum(earlier * one_hot, axis=-1))
    column = jnp.arange(TOKENS // SEQ, dtype=jnp.int32)[:, None] * CAP + slot_num
    pair_ids = jnp.arange(TOKENS * TOP, dtype=jnp.int32).reshape(TOKENS // SEQ, SEQ * TOP)
    empty = jnp.full((EXPERTS, TOKENS // SEQ * CAP), TOKENS * TOP, jnp.int32)
    return empty.at[groups, column].set(pair_ids)

def routed(normed_rows, gate_values, table, expert_gate, expert_up_weight, expert_down):
    padded = jnp.concatenate([normed_rows, jnp.zeros((1, MODEL_WIDTH), jnp.float32)], 0)
    flattened_gate = jnp.concatenate([gate_values.reshape(-1), jnp.zeros((1,), jnp.float32)], 0)
    part_width = FFE // N_TP

    def expert_step(accum, item):
        w_gate, w_up, w_down, pair_ids = item
        token_ids = pair_ids // TOP
        picked_rows = padded[token_ids]
        pre_gate = low_back(matmul(picked_rows, w_gate))
        up_projected = low_back(matmul(picked_rows, w_up))
        activ = low(jax.nn.silu(pre_gate) * up_projected)
        output = jnp.zeros((picked_rows.shape[0], MODEL_WIDTH), jnp.float32)
        for part_index in range(N_TP):
            lower_edge = part_index * part_width
            output = output + low_both(matmul(activ[:, lower_edge:lower_edge + part_width], w_down[lower_edge:lower_edge + part_width]))
        return (accum.at[token_ids].add(flattened_gate[pair_ids][:, None] * output), None)
    start = jnp.zeros((TOKENS + 1, MODEL_WIDTH), jnp.float32)
    accum, unused = lax.scan(jax.checkpoint(expert_step), start, (expert_gate, expert_up_weight, expert_down, table))
    return accum[:TOKENS]

def forward(table, routes, hidden_in, norm_attn, query_proj, kv_down, kv_norm, kv_up, out_proj, norm_ffn, router_proj, shared_gate, shared_up, shared_down, expert_gate, expert_up_weight, expert_down):

    def one_sequence(seq_rows):
        return attention_block(seq_rows, norm_attn, query_proj, kv_down, kv_norm, kv_up, out_proj)
    sequences = hidden_in.reshape(TOKENS // SEQ, SEQ, MODEL_WIDTH)
    attn_rows = lax.map(jax.checkpoint(one_sequence), sequences).reshape(TOKENS, MODEL_WIDTH)
    resid = hidden_in + attn_rows
    normed_ffn = low(normed(resid, norm_ffn))
    logits = low_back(matmul(normed_ffn, router_proj))
    sigmoids = jax.nn.sigmoid(logits)
    chosen = jnp.take_along_axis(sigmoids, routes, axis=1)
    gate_values = ROUTE_SCALE * chosen / lax.optimization_barrier(jnp.sum(chosen, axis=-1, keepdims=True))
    shared_act = low(jax.nn.silu(low_back(matmul(normed_ffn, shared_gate))) * low_back(matmul(normed_ffn, shared_up)))
    shared_rows = matmul(shared_act, shared_down)
    return resid + shared_rows + routed(normed_ffn, gate_values, table, expert_gate, expert_up_weight, expert_down)

def reference(hidden_in, routes, cotangent, norm_attn, query_proj, kv_down, kv_norm, kv_up, out_proj, norm_ffn, router_proj, shared_gate, shared_up, shared_down, expert_gate, expert_up_weight, expert_down):
    table = slot_tables(routes)
    params = tuple((arr.astype(jnp.float32) for arr in (hidden_in, norm_attn, query_proj, kv_down, kv_norm, kv_up, out_proj, norm_ffn, router_proj, shared_gate, shared_up, shared_down, expert_gate, expert_up_weight, expert_down)))
    output, pullback = jax.vjp(partial(forward, table, routes), *params)
    grads = pullback(cotangent.astype(jnp.float32))
    return (output.astype(jnp.bfloat16), grads[0].astype(jnp.bfloat16), grads[1], grads[2], grads[3], grads[4], grads[5], grads[6], grads[7], grads[8], grads[9], grads[10], grads[11], grads[12], grads[13], grads[14])
```

```python
import math

import jax
import jax.numpy as jnp
from jax import lax
from jax.experimental import pallas as pl
from jax.experimental.pallas import tpu as pltpu
from jax.sharding import PartitionSpec as P

MODEL_WIDTH = 2048
DN = 128
DR = 64
DV = 128
KVR = 512
TOP = 6


NORM_EPS = 1e-06
ROPE_THETA = 50000.0
ROUTE_SCALE = 2.446


def dot_single_float(left, right):
    return jnp.dot(left, right, preferred_element_type=jnp.float32)


def dot_high(left, right):
    return jnp.dot(left, right, precision=lax.Precision.HIGHEST, preferred_element_type=jnp.float32)


def inv_rms(value):
    return lax.rsqrt(jnp.mean(value * value, axis=-1, keepdims=True) + NORM_EPS)


def norm_back(value, factor, gain, grad):
    scaled = grad * gain
    return factor * scaled - value * factor**3 * jnp.mean(scaled * value, axis=-1, keepdims=True)


def silu_grad(value):
    sigm = jax.nn.sigmoid(value)
    return sigm * (1.0 + value * (1.0 - sigm))


def rope_tables(length, width):
    half_width = width // 2
    freq = ROPE_THETA ** (-(jnp.arange(half_width, dtype=jnp.float32) * 2.0 / width))
    angle = jnp.arange(length, dtype=jnp.float32)[:, None] * freq[None, :]
    return (jnp.cos(angle), jnp.sin(angle))


def rotate(value, cos_table, sin_table):
    half_width = value.shape[-1] // 2
    first, second = (value[..., :half_width], value[..., half_width:])
    return jnp.concatenate(
        [first * cos_table - second * sin_table, second * cos_table + first * sin_table], -1
    )


def unrotate(grad, cos_table, sin_table):
    half_width = grad.shape[-1] // 2
    first, second = (grad[..., :half_width], grad[..., half_width:])
    return jnp.concatenate(
        [first * cos_table + second * sin_table, second * cos_table - first * sin_table], -1
    )


def scores_of(query, keys, factor):
    length = query.shape[0]
    raw_scores = (
        jnp.einsum("qhd,khd->hqk", query, keys, preferred_element_type=jnp.float32) * factor
    )
    causal = jnp.arange(length)[:, None] >= jnp.arange(length)[None, :]
    return jnp.where(causal[None], raw_scores, -1e30)


def plain(
    hidden_in,
    routes,
    cotangent,
    norm_attn,
    query_proj,
    kv_down,
    kv_norm,
    kv_up,
    out_proj,
    norm_ffn,
    router_proj,
    shared_gate,
    shared_up,
    shared_down,
    expert_gate,
    expert_up_weight,
    expert_down,
):
    n_tp = lax.axis_size("tp")
    sharded_parts_count = lax.axis_size("fsdp")
    own_rows = hidden_in.shape[0]
    seq_len = own_rows * n_tp
    head_width = DN + DR
    heads_here = query_proj.shape[1] // head_width
    expert_capacity = 4 * seq_len * TOP // (3 * sharded_parts_count)
    tp_index = lax.axis_index("tp")
    factor = 1.0 / math.sqrt(head_width)
    cos_table, sin_table = rope_tables(seq_len, DR)

    def arrange(grad):
        rest = grad.shape[1:]
        block = grad.shape[0] // (sharded_parts_count * n_tp)
        split = grad.reshape((sharded_parts_count, n_tp, block) + rest)
        return jnp.swapaxes(split, 0, 1).reshape((grad.shape[0],) + rest)

    x_group = lax.all_gather(hidden_in, "tp", axis=0, tiled=True).astype(jnp.float32)
    full_g1, full_wq, full_wkva, full_gkv, full_wkvb, full_wo = (
        lax.all_gather(norm_attn, "fsdp", axis=0, tiled=True),
        lax.all_gather(query_proj, "fsdp", axis=0, tiled=True),
        lax.all_gather(kv_down, "fsdp", axis=0, tiled=True),
        lax.all_gather(kv_norm, "fsdp", axis=0, tiled=True),
        lax.all_gather(kv_up, "fsdp", axis=0, tiled=True),
        lax.all_gather(out_proj, "fsdp", axis=1, tiled=True),
    )
    factor_one = inv_rms(x_group)
    x_normed = x_group * factor_one
    normed_in = (x_normed * full_g1.astype(jnp.float32)).astype(jnp.bfloat16)
    query_raw = dot_single_float(normed_in, full_wq).reshape(seq_len, heads_here, head_width)
    query = jnp.concatenate(
        [query_raw[..., :DN], rotate(query_raw[..., DN:], cos_table[:, None], sin_table[:, None])],
        -1,
    ).astype(jnp.bfloat16)
    kv_first = dot_single_float(normed_in, full_wkva)
    latent = kv_first[:, :KVR]
    latent_factor = inv_rms(latent)
    latent_normed = (latent * latent_factor * full_gkv.astype(jnp.float32)).astype(jnp.bfloat16)
    key_rope = rotate(kv_first[:, KVR:], cos_table, sin_table).astype(jnp.bfloat16)
    kv_full = (
        dot_single_float(latent_normed, full_wkvb)
        .astype(jnp.bfloat16)
        .reshape(seq_len, heads_here, DN + DV)
    )
    keys = jnp.concatenate(
        [kv_full[..., :DN], jnp.broadcast_to(key_rope[:, None, :], (seq_len, heads_here, DR))], -1
    )
    values = kv_full[..., DN:]
    scores = scores_of(query, keys, factor)
    top_score = jnp.max(scores, axis=-1, keepdims=True)
    log_total = top_score + jnp.log(jnp.sum(jnp.exp(scores - top_score), axis=-1, keepdims=True))
    weights_bf = jnp.exp(scores - log_total).astype(jnp.bfloat16)
    context = jnp.einsum("hqk,khd->qhd", weights_bf, values, preferred_element_type=jnp.float32)
    context = context.reshape(seq_len, heads_here * DV).astype(jnp.bfloat16)
    attn_own = lax.psum_scatter(
        dot_single_float(context, full_wo), "tp", scatter_dimension=0, tiled=True
    )
    x_own = hidden_in.astype(jnp.float32)
    resid = x_own + attn_own
    full_g2, full_wr, full_sg, full_su, full_sd = (
        lax.all_gather(norm_ffn, "fsdp", axis=0, tiled=True),
        lax.all_gather(router_proj, "fsdp", axis=0, tiled=True),
        lax.all_gather(shared_gate, "fsdp", axis=0, tiled=True),
        lax.all_gather(shared_up, "fsdp", axis=0, tiled=True),
        lax.all_gather(shared_down, "fsdp", axis=1, tiled=True),
    )
    factor_two = inv_rms(resid)
    resid_normed = resid * factor_two
    normed_own = (resid_normed * full_g2.astype(jnp.float32)).astype(jnp.bfloat16)
    normed_ffn = lax.all_gather(normed_own, "tp", axis=0, tiled=True)
    logits = dot_single_float(normed_ffn, full_wr)
    sigmoids = jax.nn.sigmoid(logits)
    chosen = jnp.take_along_axis(sigmoids, routes, axis=1)
    chosen_sum = jnp.sum(chosen, axis=-1, keepdims=True)
    gate_values = ROUTE_SCALE * chosen / chosen_sum
    flat_routes = routes.reshape(-1)
    one_hot = (
        flat_routes[:, None] == jnp.arange(sharded_parts_count, dtype=jnp.int32)[None, :]
    ).astype(jnp.int32)
    slot_num = jnp.sum((jnp.cumsum(one_hot, axis=0) - one_hot) * one_hot, axis=-1)
    target = flat_routes * expert_capacity + slot_num
    token_of = jnp.arange(seq_len * TOP, dtype=jnp.int32) // TOP
    send_rows = (
        jnp.zeros((sharded_parts_count * expert_capacity, MODEL_WIDTH), jnp.bfloat16)
        .at[target]
        .set(normed_ffn[token_of])
    )
    send_rows = send_rows.reshape(sharded_parts_count, expert_capacity, MODEL_WIDTH)
    expert_gate_weight = expert_gate[0]
    routed_up_weight = expert_up_weight[0]
    w_edown = expert_down[0]
    arrived = lax.all_to_all(send_rows, "fsdp", split_axis=0, concat_axis=0, tiled=True)
    sources = arrived.shape[0]
    items = arrived.shape[1]
    flattened_input = arrived.reshape(sources * items, MODEL_WIDTH)
    pre_gate = dot_single_float(flattened_input, expert_gate_weight)
    up_projected = dot_single_float(flattened_input, routed_up_weight)
    activ = (jax.nn.silu(pre_gate) * up_projected).astype(jnp.bfloat16)
    output = (
        dot_single_float(activ, w_edown).astype(jnp.bfloat16).reshape(sources, items, MODEL_WIDTH)
    )
    returned = lax.all_to_all(output, "fsdp", split_axis=0, concat_axis=0, tiled=True)
    hidden_shape = (sources, items, pre_gate.shape[-1])
    returned, arrived, pre_gate, up_projected, activ = (
        returned,
        arrived,
        pre_gate.reshape(hidden_shape),
        up_projected.reshape(hidden_shape),
        activ.reshape(hidden_shape),
    )
    pair_rows = returned.reshape(sharded_parts_count * expert_capacity, MODEL_WIDTH)[
        target
    ].reshape(seq_len, TOP, MODEL_WIDTH)
    routed_rows = jnp.sum(gate_values[..., None] * pair_rows, axis=1)
    shared_pre_gate = dot_single_float(normed_ffn, full_sg)
    shared_pre_up = dot_single_float(normed_ffn, full_su)
    shared_act = (jax.nn.silu(shared_pre_gate) * shared_pre_up).astype(jnp.bfloat16)
    ffn_own = lax.psum_scatter(
        (routed_rows + dot_single_float(shared_act, full_sd)).astype(jnp.bfloat16),
        "tp",
        scatter_dimension=0,
        tiled=True,
    ).astype(jnp.float32)
    hidden_out = (resid + ffn_own).astype(jnp.bfloat16)
    grad_own = lax.dynamic_slice_in_dim(cotangent, tp_index * own_rows, own_rows, 0).astype(
        jnp.float32
    )
    d_shared = dot_single_float(cotangent, full_sd.T)
    d_sgate = (d_shared * shared_pre_up * silu_grad(shared_pre_gate)).astype(jnp.bfloat16)
    d_sup = (d_shared * jax.nn.silu(shared_pre_gate)).astype(jnp.bfloat16)
    dh2_part = dot_single_float(d_sgate, full_sg.T) + dot_single_float(d_sup, full_su.T)
    grad_sdown = dot_single_float(shared_act.T, cotangent)
    grad_sgate = dot_single_float(normed_ffn.T, d_sgate)
    grad_sup = dot_single_float(normed_ffn.T, d_sup)
    cot_pairs = cotangent[token_of]
    d_output = (gate_values.reshape(-1)[:, None] * cot_pairs).astype(jnp.bfloat16)
    d_gate_part = jnp.einsum("td,tkd->tk", cotangent, pair_rows, preferred_element_type=jnp.float32)
    grad_send = (
        jnp.zeros((sharded_parts_count * expert_capacity, MODEL_WIDTH), jnp.bfloat16)
        .at[target]
        .set(d_output)
    )
    grad_arrived = lax.all_to_all(
        grad_send.reshape(sharded_parts_count, expert_capacity, MODEL_WIDTH),
        "fsdp",
        split_axis=0,
        concat_axis=0,
        tiled=True,
    )
    grad_flat = grad_arrived.reshape(-1, MODEL_WIDTH)
    flattened_gate = pre_gate.reshape(grad_flat.shape[0], -1)
    up_flat = up_projected.reshape(grad_flat.shape[0], -1)
    activ_flat = activ.reshape(grad_flat.shape[0], -1)
    flattened_rows = arrived.reshape(-1, MODEL_WIDTH)
    activation_gradient = dot_single_float(grad_flat, w_edown.T)
    expert_gate_gradient = (activation_gradient * up_flat * silu_grad(flattened_gate)).astype(
        jnp.bfloat16
    )
    expert_up_gradient = (activation_gradient * jax.nn.silu(flattened_gate)).astype(jnp.bfloat16)
    grad_edown = dot_single_float(activ_flat.T, grad_flat)
    grad_egate = dot_single_float(flattened_rows.T, expert_gate_gradient)
    expert_up_weight_gradient = dot_single_float(flattened_rows.T, expert_up_gradient)
    row_gradients = (
        dot_single_float(expert_gate_gradient, expert_gate_weight.T)
        + dot_single_float(expert_up_gradient, routed_up_weight.T)
    ).reshape(sharded_parts_count, expert_capacity, MODEL_WIDTH)
    d_back = lax.all_to_all(
        row_gradients.astype(jnp.bfloat16), "fsdp", split_axis=0, concat_axis=0, tiled=True
    ).astype(row_gradients.dtype)
    dh2_part = dh2_part + jnp.sum(
        d_back.reshape(sharded_parts_count * expert_capacity, MODEL_WIDTH)[target].reshape(
            seq_len, TOP, MODEL_WIDTH
        ),
        axis=1,
    )
    dh2_own, dgate_own = (
        lax.psum_scatter(
            dh2_part.astype(jnp.bfloat16), "tp", scatter_dimension=0, tiled=True
        ).astype(jnp.float32),
        lax.psum_scatter(
            d_gate_part.astype(jnp.bfloat16), "tp", scatter_dimension=0, tiled=True
        ).astype(jnp.float32),
    )
    own_routes = lax.dynamic_slice_in_dim(routes, tp_index * own_rows, own_rows, 0)
    own_chosen = lax.dynamic_slice_in_dim(chosen, tp_index * own_rows, own_rows, 0)
    own_sum = lax.dynamic_slice_in_dim(chosen_sum, tp_index * own_rows, own_rows, 0)
    d_chosen = ROUTE_SCALE * (
        dgate_own / own_sum
        - jnp.sum(dgate_own * own_chosen, axis=-1, keepdims=True) / (own_sum * own_sum)
    )
    d_select = d_chosen * own_chosen * (1.0 - own_chosen)
    expert_ids = jnp.arange(sharded_parts_count, dtype=jnp.int32)
    d_logits = jnp.sum(
        jnp.where(own_routes[..., None] == expert_ids, d_select[..., None], 0.0), axis=1
    ).astype(jnp.bfloat16)
    dh2_own = dh2_own + dot_single_float(d_logits, full_wr.T)
    grad_wr = dot_single_float(normed_own.T, d_logits)
    grad_g2 = jnp.sum(dh2_own * resid_normed, axis=0)
    d_resid = grad_own + norm_back(resid, factor_two, full_g2.astype(jnp.float32), dh2_own)
    d_attn = lax.all_gather(d_resid.astype(jnp.bfloat16), "tp", axis=0, tiled=True)
    grad_wo = dot_single_float(context.T, d_attn)
    d_context = (
        dot_single_float(d_attn, full_wo.T).astype(jnp.bfloat16).reshape(seq_len, heads_here, DV)
    )
    weights_f = jnp.exp(scores_of(query, keys, factor) - log_total)
    d_weights = jnp.einsum("qhd,khd->hqk", d_context, values, preferred_element_type=jnp.float32)
    d_scores = (
        weights_f * (d_weights - jnp.sum(weights_f * d_weights, axis=-1, keepdims=True))
    ).astype(jnp.bfloat16)
    d_query = (
        jnp.einsum("hqk,khd->qhd", d_scores, keys, preferred_element_type=jnp.float32) * factor
    )
    d_keys = (
        jnp.einsum("hqk,qhd->khd", d_scores, query, preferred_element_type=jnp.float32) * factor
    )
    d_values = jnp.einsum(
        "hqk,qhd->khd",
        weights_f.astype(jnp.bfloat16),
        d_context,
        preferred_element_type=jnp.float32,
    )
    d_qraw = jnp.concatenate(
        [d_query[..., :DN], unrotate(d_query[..., DN:], cos_table[:, None], sin_table[:, None])], -1
    )
    d_qraw = d_qraw.reshape(seq_len, heads_here * head_width).astype(jnp.bfloat16)
    d_kv = (
        jnp.concatenate([d_keys[..., :DN], d_values], -1)
        .reshape(seq_len, heads_here * (DN + DV))
        .astype(jnp.bfloat16)
    )
    d_krope = unrotate(jnp.sum(d_keys[..., DN:], axis=1), cos_table, sin_table)
    grad_wq = dot_single_float(normed_in.T, d_qraw)
    grad_wkvb = dot_single_float(latent_normed.T, d_kv)
    d_latent_normed = dot_single_float(d_kv, full_wkvb.T)
    gkv_f = full_gkv.astype(jnp.float32)
    grad_gkv = jnp.sum(d_latent_normed * latent * latent_factor, axis=0)
    d_latent = norm_back(latent, latent_factor, gkv_f, d_latent_normed)
    d_kvfirst = jnp.concatenate([d_latent, d_krope], -1)
    grad_wkva = dot_high(normed_in.astype(jnp.float32).T, d_kvfirst)
    dh1_part = dot_single_float(d_qraw, full_wq.T) + dot_high(
        d_kvfirst, full_wkva.astype(jnp.float32).T
    )
    grad_g1 = jnp.sum(dh1_part * x_normed, axis=0)
    dh1_own, sum_g1, sum_wkva, sum_gkv, sum_g2, sum_wr = (
        lax.psum_scatter(
            dh1_part.astype(jnp.bfloat16), "tp", scatter_dimension=0, tiled=True
        ).astype(jnp.float32),
        lax.psum_scatter(
            arrange(grad_g1).astype(jnp.bfloat16), "tp", scatter_dimension=0, tiled=True
        ).astype(jnp.float32),
        lax.psum_scatter(
            arrange(grad_wkva).astype(jnp.bfloat16), "tp", scatter_dimension=0, tiled=True
        ).astype(jnp.float32),
        lax.psum_scatter(
            arrange(grad_gkv).astype(jnp.bfloat16), "tp", scatter_dimension=0, tiled=True
        ).astype(jnp.float32),
        lax.psum_scatter(
            arrange(grad_g2).astype(jnp.bfloat16), "tp", scatter_dimension=0, tiled=True
        ).astype(jnp.float32),
        lax.psum_scatter(
            arrange(grad_wr).astype(jnp.bfloat16), "tp", scatter_dimension=0, tiled=True
        ).astype(jnp.float32),
    )
    g1_f = full_g1.astype(jnp.float32)
    grad_in = (d_resid + norm_back(x_own, inv_rms(x_own), g1_f, dh1_own)).astype(jnp.bfloat16)
    summed = (
        lax.psum_scatter(grad_wq, "fsdp", scatter_dimension=0, tiled=True),
        lax.psum_scatter(grad_wkvb, "fsdp", scatter_dimension=0, tiled=True),
        lax.psum_scatter(grad_wo, "fsdp", scatter_dimension=1, tiled=True),
        lax.psum_scatter(grad_sgate, "fsdp", scatter_dimension=0, tiled=True),
        lax.psum_scatter(grad_sup, "fsdp", scatter_dimension=0, tiled=True),
        lax.psum_scatter(grad_sdown, "fsdp", scatter_dimension=1, tiled=True),
        lax.psum_scatter(sum_g1, "fsdp", scatter_dimension=0, tiled=True),
        lax.psum_scatter(sum_wkva, "fsdp", scatter_dimension=0, tiled=True),
        lax.psum_scatter(sum_gkv, "fsdp", scatter_dimension=0, tiled=True),
        lax.psum_scatter(sum_g2, "fsdp", scatter_dimension=0, tiled=True),
        lax.psum_scatter(sum_wr, "fsdp", scatter_dimension=0, tiled=True),
    )
    (
        out_wq,
        out_wkvb,
        out_wo,
        out_sgate,
        out_sup,
        out_sdown,
        out_g1,
        out_wkva,
        out_gkv,
        out_g2,
        out_wr,
    ) = summed
    return (
        hidden_out,
        grad_in,
        out_g1,
        out_wq,
        out_wkva,
        out_gkv,
        out_wkvb,
        out_wo,
        out_g2,
        out_wr,
        out_sgate,
        out_sup,
        out_sdown,
        grad_egate[None],
        expert_up_weight_gradient[None],
        grad_edown[None],
    )


RINGS_16 = (
    (0, 1, 3, 2, 6, 7, 5, 9, 13, 12, 14, 15, 11, 10, 8, 4),
    (0, 1, 5, 4, 6, 10, 14, 15, 13, 12, 8, 9, 11, 7, 3, 2),
    (0, 2, 6, 7, 3, 1, 5, 9, 13, 15, 11, 10, 14, 12, 8, 4),
)
VMEM_BYTES = 60 * 2**20
BF16 = jnp.bfloat16
F32 = jnp.float32
SLOTS = 3


def ring_orders(n):
    return RINGS_16 if n == 16 else (tuple(range(n)),) * 3


def lookup(values, index):
    words = []
    for k in range(0, len(values), 8):
        word = sum(v << (4 * j) for j, v in enumerate(values[k : k + 8]))
        words.append(word - (1 << 32) if word >= 1 << 31 else word)
    word = jnp.int32(words[0])
    for k in range(1, len(words)):
        word = jnp.where(index >= 8 * k, jnp.int32(words[k]), word)
    return lax.shift_right_logical(word, 4 * (index & 7)) & 15


def remote(src, dst, send, recv, device):
    return pltpu.make_async_remote_copy(
        src_ref=src,
        dst_ref=dst,
        send_sem=send,
        recv_sem=recv,
        device_id=device,
        device_id_type=pl.DeviceIdType.MESH,
    )


class Place:
    def __init__(self, n):
        self.n, self.half = n, n // 2
        self.me, self.t = lax.axis_index("fsdp"), lax.axis_index("tp")
        self.orders = ring_orders(n)
        self.spot = [
            lookup([order.index(k) for k in range(n)], self.me) for order in self.orders
        ]
        self.near = [[self.owner(r, 1), self.owner(r, n - 1)] for r in range(len(self.orders))]
        self.twin = (self.me, 1 - self.t)

    def owner(self, ring, offset):
        return lookup(self.orders[ring], lax.rem(self.spot[ring] + offset + self.n, self.n))

    def next(self, ring, way):
        return (self.near[ring][way], self.t)

    def enter(self, everyone=False):
        barrier = pltpu.get_barrier_semaphore()
        if everyone:

            def greet(k, _):
                there = lax.rem(self.me + k, self.n)
                pl.semaphore_signal(
                    barrier, 1, device_id=(there, self.t), device_id_type=pl.DeviceIdType.MESH
                )
                return 0

            lax.fori_loop(1, self.n, greet, 0)
            count = self.n - 1
        else:
            count = 0
            for ring in range(len(self.orders)):
                for way in range(2):
                    pl.semaphore_signal(
                        barrier,
                        1,
                        device_id=self.next(ring, way),
                        device_id_type=pl.DeviceIdType.MESH,
                    )
                    count += 1
        pl.semaphore_signal(barrier, 1, device_id=self.twin, device_id_type=pl.DeviceIdType.MESH)
        pl.semaphore_wait(barrier, count + 1)


def gather_sems(n):
    return pltpu.SemaphoreType.DMA((4, 2, n // 2 + 1))


class Gather:
    def __init__(self, place, ring, rows, source, target, sems, shared):
        self.place, self.ring, self.rows = place, ring, rows
        self.source, self.target, self.sems, self.shared = source, target, sems, shared

    def part(self, way, last):
        if not last:
            return 0, self.rows
        half = self.rows // 2
        return (0, half) if way == 0 else (half, self.rows - half)

    def offset(self, way, s):
        return -s if way == 0 else s

    def hop(self, way, s, last=False, first=False, owner=None):
        lo, rows = self.part(way, last)
        place = self.place
        if owner is None:
            owner = place.owner(self.ring, self.offset(way, s - 1))
        there = self.target(owner, lo, rows, place.t)
        here = self.source(lo, rows) if first else there
        return remote(
            here, there, self.sems.at[0, way, s], self.sems.at[1, way, s], place.next(self.ring, way)
        )

    def landed(self, way, s, last=False, owner=None):
        lo, rows = self.part(way, last)
        place = self.place
        if owner is None:
            owner = place.owner(self.ring, self.offset(way, s))
        there = self.target(owner, lo, rows, place.t)
        return remote(
            there, there, self.sems.at[0, way, s], self.sems.at[1, way, s], place.next(self.ring, way)
        )

    def across(self, way, s, t, last=False, first=False, owner=None):
        lo, rows = (0, self.rows) if first else self.part(way, last)
        place = self.place
        if owner is None:
            owner = place.me if first else place.owner(self.ring, self.offset(way, s))
        there = self.target(owner, lo, rows, t)
        here = self.source(lo, rows) if first else there
        return remote(here, there, self.sems.at[2, way, s], self.sems.at[3, way, s], place.twin)

    def own(self):
        return pltpu.make_async_copy(
            self.source(0, self.rows),
            self.target(self.place.me, 0, self.rows, self.place.t),
            self.sems.at[0, 0, 0],
        )

    def begin(self):
        for way in range(2):
            self.hop(way, 1, first=True).start()
        self.own().start()
        if self.shared:
            self.across(0, 0, self.place.t, first=True).start()

    def step(self, s, final=False):
        for way in range(2):
            owner = self.place.owner(self.ring, self.offset(way, s))
            self.landed(way, s, owner=owner).wait_recv()
            self.hop(way, s + 1, last=final, owner=owner).start()
            if self.shared:
                self.across(way, s, self.place.t, owner=owner).start()

    def close(self):
        half = self.place.half
        for way in range(2):
            self.landed(way, half, last=True).wait_recv()
            if self.shared:
                self.across(way, half, self.place.t, last=True).start()

    def settle(self):
        half = self.place.half
        self.own().wait()
        t = self.place.t
        if self.shared:
            self.across(0, 0, t, first=True).wait_send()
            self.across(0, 0, 1 - t, first=True).wait_recv()

        def each(s, _):
            for way in range(2):
                self.hop(way, s).wait_send()
                if self.shared:
                    self.across(way, s, t).wait_send()
                    self.across(way, s, 1 - t).wait_recv()
            return 0

        lax.fori_loop(1, half, each, 0)
        for way in range(2):
            self.hop(way, half, last=True).wait_send()
            if self.shared:
                self.across(way, half, t, last=True).wait_send()
                self.across(way, half, 1 - t, last=True).wait_recv()


def pump_gathers(gathers, half, s):
    if isinstance(s, int):
        s = jnp.int32(s)

    @pl.when(s < half - 1)
    def _():
        for g in gathers:
            g.step(s)

    @pl.when(s == half - 1)
    def _():
        for g in gathers:
            g.step(half - 1, final=True)

    @pl.when(s == half)
    def _():
        for g in gathers:
            g.close()


def pump_all(place, gathers, beside=()):
    for s, work in enumerate(beside):
        pump_gathers(gathers, place.half, s + 1)
        work()

    def each(s, _):
        for g in gathers:
            g.step(s)
        return 0

    lax.fori_loop(1 + len(beside), place.half - 1, each, 0)
    for g in gathers:
        g.step(place.half - 1, final=True)
    for g in gathers:
        g.close()


class Bring:
    def __init__(self, pairs, sems):
        self.copies = [
            pltpu.make_async_copy(src, dst, sems.at[k]) for k, (src, dst) in enumerate(pairs)
        ]

    def begin(self):
        for copy in self.copies:
            copy.start()

    def wait(self):
        for copy in self.copies:
            copy.wait()


def room_for(arrays):
    return [pltpu.VMEM(a.shape, a.dtype) for a in arrays] + [
        pltpu.SemaphoreType.DMA((len(arrays),))
    ]


def scatter_scratch(n, rows, cols):
    return [
        pltpu.SemaphoreType.DMA((2, 2, n // 2 + 1)),
        pltpu.SemaphoreType.DMA((2, 2, n // 2 + 1)),
        pltpu.SemaphoreType.DMA((2, n)),
        pltpu.VMEM((2, SLOTS, rows, cols), BF16),
        pltpu.VMEM((2, SLOTS, rows, cols), BF16),
        pltpu.VMEM((2, n // 2, rows, cols), BF16),
    ]


def add_rows(target, sources, lo, rows, cols):
    most = max(16, (32768 // cols) // 16 * 16)
    size = min(most, rows)
    while rows % size:
        size -= 16

    def each(i, _):
        at = pl.ds(pl.multiple_of(lo + i * size, 16), size)
        total = sources[0][at, :].astype(F32)
        for source in sources[1:]:
            total = total + source[at, :].astype(F32)
        target[at, :] = total.astype(target.dtype)
        return 0

    lax.fori_loop(0, rows // size, each, 0)


class Scatter:
    def __init__(self, place, ring, shape, source, scratch, heap=None):
        self.place, self.ring, self.source, self.heap = place, ring, source, heap
        self.rows, self.cols = shape
        self.sems, self.load_sems, self.give_sems, self.term, self.other, self.land = scratch

    def owner(self, way, s):
        half = self.place.half
        return self.place.owner(self.ring, half - s if way == 0 else half + s)

    def loads(self, way, s):
        slot = lax.rem(s, SLOTS)
        owner = self.owner(way, s)
        out = [
            pltpu.make_async_copy(
                self.source(owner, self.place.t),
                self.term.at[way, slot],
                self.load_sems.at[0, way, s],
            )
        ]
        if self.heap is not None:
            out.append(
                pltpu.make_async_copy(
                    self.heap(owner), self.other.at[way, slot], self.load_sems.at[1, way, s]
                )
            )
        return out

    def give(self, owner):
        return remote(
            self.source(owner, 1 - self.place.t),
            self.heap(owner),
            self.give_sems.at[0, owner],
            self.give_sems.at[1, owner],
            self.place.twin,
        )

    def push(self, s):
        if self.heap is not None:
            for way in range(2):

                @pl.when((s <= self.place.half) if way == 0 else ((s > 0) & (s < self.place.half)))
                def _(way=way):
                    self.give(self.owner(way, s)).start()

    def fetch(self, s, ways=(0, 1), fresh=True):
        for way in ways:
            if self.heap is not None and fresh:
                self.give(self.owner(way, s)).wait_recv()
            for copy in self.loads(way, s):
                copy.start()

    def part(self, way, first):
        if not first:
            return 0, self.rows
        half = self.rows // 2
        return (0, half) if way == 0 else (half, self.rows - half)

    def hop(self, way, s, first=False):
        lo, rows = self.part(way, first)
        at = pl.ds(lo, rows)
        return remote(
            self.term.at[way, lax.rem(s - 1, SLOTS), at, :],
            self.land.at[way, s - 1, at, :],
            self.sems.at[0, way, s],
            self.sems.at[1, way, s],
            self.place.next(self.ring, way),
        )

    def sources(self, way, s, *more):
        slot = lax.rem(s, SLOTS)
        out = [self.term.at[way, slot]]
        if self.heap is not None:
            out.append(self.other.at[way, slot])
        return out + list(more)

    def begin(self):
        self.push(0)
        self.push(1)
        self.fetch(0, ways=(0,))
        self.fetch(0, ways=(1,), fresh=False)

    def open(self):
        for way in range(2):
            for copy in self.loads(way, 0):
                copy.wait()
            if self.heap is not None:
                lo, rows = self.part(way, True)
                add_rows(self.term.at[way, 0], self.sources(way, 0), lo, rows, self.cols)
            self.hop(way, 1, first=True).start()

    def follow(self):
        if self.heap is not None:

            def each(s, _):
                self.push(s)
                return 0

            lax.fori_loop(2, self.place.half + 1, each, 0)
        self.fetch(1)

    def step(self, s, first=False, second=False, final=False):
        for way in range(2):
            for copy in self.loads(way, s):
                copy.wait()
            self.hop(way, s, first=first).wait_recv()
            lo, rows = self.part(way, first)
            target = self.term.at[way, lax.rem(s, SLOTS)]
            landed = self.land.at[way, s - 1]
            add_rows(target, self.sources(way, s, landed), lo, rows, self.cols)
            if first and self.heap is not None:
                lo, rows = self.part(1 - way, first)
                add_rows(target, self.sources(way, s), lo, rows, self.cols)
            self.hop(way, s + 1).start()
        for way in range(2):
            if not first:
                self.hop(way, s - 1, first=second).wait_send()
            if not final or way == 0:
                self.fetch(s + 1, ways=(way,))

    def middle(self, s):
        half = self.place.half

        @pl.when(s == 2)
        def _():
            self.step(s, second=True)

        @pl.when((s > 2) & (s < half - 1))
        def _():
            self.step(s)

        @pl.when(s == half - 1)
        def _():
            self.step(s, final=True)

    def close(self, out):
        half = self.place.half
        for copy in self.loads(0, half):
            copy.wait()
        for way in range(2):
            self.hop(way, half).wait_recv()
        last = [self.land.at[way, half - 1] for way in range(2)]
        add_rows(out, self.sources(0, half, *last), 0, self.rows, self.cols)
        for way in range(2):
            self.hop(way, half - 1).wait_send()
            self.hop(way, half).wait_send()
        if self.heap is not None:

            def given(k, _):
                self.give(k).wait_send()
                return 0

            lax.fori_loop(0, self.place.n, given, 0)


def open_scatters(scatters):
    for s in scatters:
        s.begin()
    for s in scatters:
        s.open()
    for s in scatters:
        s.follow()


def step_scatters(place, scatters, s):
    if isinstance(s, int):
        s = jnp.int32(s)

    @pl.when(s == 1)
    def _():
        for one in scatters:
            one.step(1, first=True)

    @pl.when((s > 1) & (s < place.half))
    def _():
        for one in scatters:
            one.middle(s)


def run_scatters(place, scatters, outs, beside=()):
    open_scatters(scatters)
    for s, work in enumerate(beside):
        step_scatters(place, scatters, s + 1)
        work()

    def each(s, _):
        step_scatters(place, scatters, s)
        return 0

    lax.fori_loop(1 + len(beside), place.half, each, 0)
    for s, out in zip(scatters, outs):
        s.close(out)


class Trade:
    def __init__(self, place, sources, targets, sems):
        self.place, self.sources, self.targets, self.sems = place, sources, targets, sems

    def copies(self, k, coming=False):
        place = self.place
        there = lax.rem(place.me + k, place.n)
        back = lax.rem(place.me + place.n - k, place.n)
        return [
            remote(
                source(there),
                target(back if coming else place.me),
                self.sems.at[0, k, j],
                self.sems.at[1, k, j],
                (there, place.t),
            )
            for j, (source, target) in enumerate(zip(self.sources, self.targets))
        ]

    def own(self):
        me = self.place.me
        return [
            pltpu.make_async_copy(source(me), target(me), self.sems.at[0, 0, j])
            for j, (source, target) in enumerate(zip(self.sources, self.targets))
        ]

    def begin(self):
        def each(k, _):
            for copy in self.copies(k):
                copy.start()
            return 0

        lax.fori_loop(1, self.place.n, each, 0)
        for copy in self.own():
            copy.start()

    def settle(self):
        def each(k, _):
            for copy in self.copies(k):
                copy.wait_send()
            for copy in self.copies(k, coming=True):
                copy.wait_recv()
            return 0

        lax.fori_loop(1, self.place.n, each, 0)
        for copy in self.own():
            copy.wait()


def comm_call(kernel, out_shape, out_specs, in_specs, scratch, ident, name):
    return pl.pallas_call(
        kernel,
        out_shape=out_shape,
        in_specs=in_specs,
        out_specs=out_specs,
        scratch_shapes=scratch,
        compiler_params=pltpu.CompilerParams(
            collective_id=ident, has_side_effects=True, vmem_limit_bytes=VMEM_BYTES
        ),
        name=name,
    )


IN_HBM = pl.BlockSpec(memory_space=pl.ANY)
IN_VMEM = pl.BlockSpec(memory_space=pltpu.VMEM)


def thirds(width):
    tiles = width // 128
    cuts = [0, tiles // 3, 2 * tiles // 3, tiles]
    return [(128 * lo, 128 * (hi - lo)) for lo, hi in zip(cuts, cuts[1:])]


def pick(flat):
    flat = list(flat)

    def take(count):
        head, flat[:] = flat[:count], flat[count:]
        return head

    return take


def dot_tn(left, right):
    return lax.dot_general(left, right, (((0,), (0,)), ((), ())), preferred_element_type=F32)


def dot_nt(left, right):
    return lax.dot_general(left, right, (((1,), (1,)), ((), ())), preferred_element_type=F32)


def whole(array):
    zeros = (0,) * array.ndim
    return pl.BlockSpec(array.shape, lambda i: zeros, pipeline_mode=pl.Buffered(1))


def by_cols(rows, cols):
    return pl.BlockSpec((rows, cols), lambda i: (0, i))


def by_rows(rows, cols):
    return pl.BlockSpec((rows, cols), lambda i: (i, 0))


def by_seq(*block):
    rest = (0,) * (len(block) - 1)
    return pl.BlockSpec(block, lambda i: (i,) + rest)


def eye(size):
    same = lax.broadcasted_iota(jnp.int32, (size, size), 0) == lax.broadcasted_iota(
        jnp.int32, (size, size), 1
    )
    return same.astype(F32).astype(BF16)


def sds(shape, dtype):
    return jax.ShapeDtypeStruct(shape, dtype)


def grid_call(kernel, steps, in_specs, out, scratch, ident, name):
    return pl.pallas_call(
        kernel,
        grid=(steps,),
        in_specs=in_specs,
        out_specs=tuple(spec for spec, _, _ in out),
        out_shape=tuple(sds(shape, dtype) for _, shape, dtype in out),
        scratch_shapes=scratch,
        compiler_params=pltpu.CompilerParams(
            collective_id=ident, has_side_effects=True, vmem_limit_bytes=63 * 2**20
        ),
        name=name,
    )


GAIN_ATTN, GAIN_FFN, GAIN_KV, TABLES = 16, 17, 18, 32


def row_gathers(place, chunks, sems, source, target, own):
    t = place.t
    return [
        Gather(
            place, ring, rows,
            lambda lo, r, b=b, c0=c0, w=w: source(pl.ds(b + lo, r), pl.ds(c0, w)),
            lambda o, lo, r, u, b=b, c0=c0, w=w: target(
                o, pl.ds(u * own + b + lo, r), pl.ds(c0, w)
            ),
            sems[k], True,
        )
        for k, (ring, b, rows, c0, w) in enumerate(chunks)
    ]


def row_scatters(place, chunks, scratch, parts, heap, own):
    return [
        Scatter(
            place, ring, (rows, w),
            lambda o, u, b=b, rows=rows, c0=c0, w=w: parts.at[
                o, pl.ds(u * own + b, rows), pl.ds(c0, w)
            ],
            scratch[k],
            lambda o, b=b, rows=rows, c0=c0, w=w: heap.at[o, pl.ds(b, rows), pl.ds(c0, w)],
        )
        for k, (ring, b, rows, c0, w) in enumerate(chunks)
    ]


def row_cuts(rows, width):
    return [(ring, 0, rows, c0, w) for ring, (c0, w) in enumerate(thirds(width))]


def collect_inputs(
    n, query, kvd, kvu, outp, x, norm_attn, norm_ffn, kv_norm, router, routes, s_gate, s_up, s_down
):
    own, width = x.shape
    seq = 2 * own
    q_rows, q_cols = query.shape
    cut = q_cols // 4 * 3
    d_rows, cols = kvd.shape[0] // 2, kvd.shape[1]
    o_rows = outp.shape[0]
    u_rows = kvu.shape[0]
    hidden = s_down.shape[0] // n
    padded = -(-hidden // 16) * 16
    small_rows = TABLES + 2 * n

    def kernel(*refs):
        take = pick(refs)
        q, kd, ku, wo, xin, na, nf, nk, ro, rt, sg, su, sd = take(13)
        q_all, kd_all, ku_all, wo_all, sm_all, x_all, blocks = take(7)
        sems = take(6)
        x_sems, sm, turned = take(3)
        place = Place(n)
        t = place.t
        place.enter()

        def of_q(ring, c0, w):
            return Gather(
                place, ring, q_rows,
                lambda lo, r: q.at[pl.ds(lo, r), pl.ds(c0, w)],
                lambda o, lo, r, _: q_all.at[pl.ds(o * q_rows + lo, r), pl.ds(c0, w)],
                sems[ring], False,
            )

        gathers = [
            of_q(0, 0, cut),
            of_q(1, cut, q_cols - cut),
            Gather(
                place, 2, o_rows,
                lambda lo, r: wo.at[pl.ds(lo, r)],
                lambda o, lo, r, _: wo_all.at[pl.ds(lo, r), pl.ds(o * cols, cols)],
                sems[5], False,
            ),
            Gather(
                place, 1, u_rows,
                lambda lo, r: ku.at[pl.ds(lo, r)],
                lambda o, lo, r, _: ku_all.at[pl.ds(o * u_rows + lo, r)],
                sems[2], False,
            ),
            Gather(
                place, 1, d_rows,
                lambda lo, r: kd.at[pl.ds(t * d_rows + lo, r)],
                lambda o, lo, r, u: kd_all.at[pl.ds(u * d_rows + lo, r), pl.ds(o * cols, cols)],
                sems[3], True,
            ),
            Gather(
                place, 2, small_rows,
                lambda lo, r: sm.at[pl.ds(lo, r)],
                lambda o, lo, r, _: sm_all.at[o, pl.ds(lo, r)],
                sems[4], False,
            ),
        ]
        for g in gathers[:-1]:
            g.begin()
        mine = x_all.at[pl.ds(t * own, own)]
        x_own = pltpu.make_async_copy(xin, mine, x_sems.at[0])
        x_give = remote(xin, mine, x_sems.at[1], x_sems.at[2], place.twin)
        theirs = x_all.at[pl.ds((1 - t) * own, own)]
        x_take = remote(xin, theirs, x_sems.at[1], x_sems.at[2], place.twin)
        x_own.start()
        x_give.start()

        sm[...] = jnp.zeros_like(sm)
        sm[0:n, :] = ro[...]
        gains = jnp.concatenate(
            [
                na[...].astype(F32),
                nf[...].astype(F32),
                nk[...].astype(F32),
                jnp.zeros((TABLES - GAIN_KV - 1, cols), F32),
            ],
            0,
        )
        sm[GAIN_ATTN:TABLES, :] = gains.astype(BF16)
        ids = lax.broadcasted_iota(jnp.int32, (n, seq), 0)
        chosen = jnp.zeros((n, seq), F32)
        for k in range(TOP):
            chosen = jnp.where(ids == rt[k : k + 1, :], 1.0, chosen)
        table = chosen.astype(BF16)
        sm[TABLES : TABLES + n, :] = table[:, :own]
        sm[TABLES + n : TABLES + 2 * n, :] = table[:, own:]
        gathers[-1].begin()

        def cut_slices(j, w):
            if j < 2:
                turned[...] = dot_tn(w[...], eye(cols))
            else:
                turned[...] = w[...].astype(F32)
            for k in range(n):
                blocks[k, j, 0:hidden, :] = turned[k * hidden : (k + 1) * hidden, :].astype(BF16)
                if padded > hidden:
                    blocks[k, j, hidden:padded, :] = jnp.zeros((padded - hidden, cols), BF16)

        beside = [lambda j=j, w=w: cut_slices(j, w) for j, w in enumerate((sg, su, sd))]
        pump_all(place, gathers, beside)
        x_own.wait()
        x_give.wait_send()
        x_take.wait_recv()
        for g in gathers:
            g.settle()

    return comm_call(
        kernel,
        (
            sds((n * q_rows, q_cols), BF16),
            sds((kvd.shape[0], n * cols), BF16),
            sds((n * u_rows, kvu.shape[1]), BF16),
            sds((o_rows, n * cols), BF16),
            sds((n, small_rows, cols), BF16),
            sds((seq, width), BF16),
            sds((n, 3, padded, cols), BF16),
        ),
        (IN_HBM,) * 6 + (IN_VMEM,),
        [IN_HBM] * 5 + [IN_VMEM] * 8,
        [gather_sems(n)] * 6
        + [
            pltpu.SemaphoreType.DMA((3,)),
            pltpu.VMEM((small_rows, cols), BF16),
            pltpu.VMEM((n * hidden, cols), F32),
        ],
        1,
        "collect_inputs",
    )(query, kvd, kvu, outp, x, norm_attn, norm_ffn, kv_norm, router, routes, s_gate, s_up, s_down)


def swapped(v):
    half_width = v.shape[1] // 2
    return jnp.concatenate([v[:, half_width:], v[:, :half_width]], 1)


def causal_weights(q_n, q_r, k_n, k_r, factor):
    raw = (dot_nt(q_n, k_n) + dot_nt(q_r, k_r)) * factor
    length = raw.shape[0]
    ahead = lax.broadcasted_iota(jnp.int32, (length, length), 0) >= lax.broadcasted_iota(
        jnp.int32, (length, length), 1
    )
    raw = jnp.where(ahead, raw, -1e30)
    top = jnp.max(raw, axis=1, keepdims=True)
    up = jnp.exp(raw - top)
    return up / jnp.sum(up, axis=1, keepdims=True)


def attend(n, x_seq, small_all, w_kvd, cos2, sin2, w_q, w_kvu, w_out, blocks):
    seq, width = x_seq.shape
    head = DN + DR
    pairs = w_q.shape[1] // (2 * head)
    factor = 1.0 / math.sqrt(head)
    cols = width // n
    padded = blocks.shape[2]
    kv_cols = KVR // n
    part_rows = 128

    def kernel(*refs):
        take = pick(refs)
        x, sm, wd, co, si, wq, wu, wo, bl = take(9)
        part, h1, g1, gk, lat, cn, kpe, sw, qn, qr, kv, ctx = take(12)
        trade_sems, got = take(2)
        place = Place(n)
        i = pl.program_id(0)
        trade = Trade(place, [lambda k: bl.at[k]], [lambda k: got.at[k]], trade_sems)

        @pl.when(i == 0)
        def _():
            place.enter(everyone=True)
            trade.begin()
            for o in range(n):
                at = slice(o * cols, (o + 1) * cols)
                g1[:, at] = sm[o, GAIN_ATTN : GAIN_ATTN + 1, :].astype(F32)
                gk[:, o * kv_cols : (o + 1) * kv_cols] = sm[
                    o, GAIN_KV : GAIN_KV + 1, 0:kv_cols
                ].astype(F32)
            size = 16

            def norm_rows(j, _):
                at = pl.ds(pl.multiple_of(j * size, size), size)
                v = x[at, :].astype(F32)
                h1[at, :] = (v * inv_rms(v) * g1[...]).astype(BF16)
                return 0

            lax.fori_loop(0, seq // size, norm_rows, 0)
            first = dot_nt(h1[...], wd[...])
            latent = first[:, :KVR]
            lat[...] = latent
            cn[...] = (latent * inv_rms(latent) * gk[...]).astype(BF16)
            rope = first[:, KVR:]
            kpe[...] = (rope * co[...] + swapped(rope) * si[...]).astype(BF16)

        q_raw = dot_single_float(h1[...], wq[...])
        kv[...] = dot_single_float(cn[...], wu[...]).astype(BF16)
        for k in range(2):
            q_n = q_raw[:, k * head : k * head + DN].astype(BF16)
            rope = q_raw[:, k * head + DN : (k + 1) * head]
            q_r = (rope * co[...] + swapped(rope) * si[...]).astype(BF16)
            qn[:, k * DN : (k + 1) * DN] = q_n
            qr[:, k * DR : (k + 1) * DR] = q_r
            base = k * (DN + DV)
            weights = causal_weights(q_n, q_r, kv[:, base : base + DN], kpe[...], factor)
            one = dot_single_float(weights.astype(BF16), kv[:, base + DN : base + DN + DV])
            ctx[:, k * DV : (k + 1) * DV] = one.astype(BF16)
        more = dot_single_float(ctx[...], wo[...])

        @pl.when(i == 0)
        def _():
            part[...] = more

        @pl.when(i > 0)
        def _():
            part[...] += more

        @pl.when(i == pairs - 1)
        def _():
            trade.settle()
            sw[...] = jnp.zeros_like(sw)
            for o in range(n):
                for j in range(3):
                    sw[j * part_rows : j * part_rows + padded, o * cols : (o + 1) * cols] = got[o, j]

    heads = 2 * pairs
    return grid_call(
        kernel,
        pairs,
        [whole(a) for a in (x_seq, small_all, w_kvd, cos2, sin2)]
        + [by_cols(width, 2 * head), by_cols(KVR, 2 * (DN + DV)), by_rows(2 * DV, width), IN_HBM],
        (
            (IN_VMEM, (seq, width), F32),
            (IN_VMEM, (seq, width), BF16),
            (IN_VMEM, (1, width), F32),
            (IN_VMEM, (1, KVR), F32),
            (IN_VMEM, (seq, KVR), F32),
            (IN_VMEM, (seq, KVR), BF16),
            (IN_VMEM, (seq, DR), BF16),
            (IN_VMEM, (3 * part_rows, width), BF16),
            (by_cols(seq, 2 * DN), (seq, heads * DN), BF16),
            (by_cols(seq, 2 * DR), (seq, heads * DR), BF16),
            (by_cols(seq, 2 * (DN + DV)), (seq, heads * (DN + DV)), BF16),
            (by_cols(seq, 2 * DV), (seq, heads * DV), BF16),
        ),
        [pltpu.SemaphoreType.DMA((2, n, 1)), pltpu.VMEM(blocks.shape, BF16)],
        2,
        "attend",
    )(x_seq, small_all, w_kvd, cos2, sin2, w_q, w_kvu, w_out, blocks)


def spread_rows(n, attn_part, x_own, small_all, cap):
    own, width = x_own.shape
    seq = 2 * own
    cols = width // n
    chunks = row_cuts(own, width)

    def kernel(*refs):
        take = pick(refs)
        part, x, sm = take(3)
        resid, sel_out, g2, wr, h_own, table, h_all, gate_all = take(8)
        got, gate_buf, named = take(3)
        sems = take(1 + len(chunks))
        (swap_sems,) = take(1)
        place = Place(n)
        t, me = place.t, place.me
        place.enter()
        swap = remote(
            part.at[pl.ds((1 - t) * own, own)], got, swap_sems.at[0], swap_sems.at[1], place.twin
        )
        swap.start()
        for o in range(n):
            at = slice(o * cols, (o + 1) * cols)
            g2[:, at] = sm[o, GAIN_FFN : GAIN_FFN + 1, :].astype(F32)
            wr[:, at] = sm[o, 0:n, :]
        swap.wait_recv()
        size = 16

        def norm_rows(i, _):
            at = pl.ds(pl.multiple_of(i * size, size), size)
            mine = pl.ds(pl.multiple_of(t * own + i * size, size), size)
            v = x[at, :].astype(F32) + (part[mine, :] + got[at, :])
            resid[at, :] = v
            h_own[at, :] = (v * inv_rms(v) * g2[...]).astype(BF16)
            return 0

        lax.fori_loop(0, own // size, norm_rows, 0)
        gathers = row_gathers(
            place, chunks, sems,
            lambda r, c: h_own.at[r, c], lambda o, r, c: h_all.at[o, r, c], own,
        )
        gathers.append(
            Gather(
                place, 0, 2 * n,
                lambda lo, r: gate_buf.at[pl.ds(lo, r)],
                lambda o, lo, r, u: gate_all.at[o, u, pl.ds(lo, r)],
                sems[len(chunks)], True,
            )
        )
        for one in gathers[:-1]:
            one.begin()
        logits = dot_nt(wr[...], h_own[...])
        chosen = sm[me, pl.ds(pl.multiple_of(TABLES + t * n, 16), n), :].astype(F32)
        sel = jnp.where(chosen > 0.5, 1.0 / (1.0 + jnp.exp(-logits)), 0.0)
        sel_out[...] = sel
        gate = ROUTE_SCALE * sel / jnp.sum(sel, axis=0, keepdims=True)
        high = gate.astype(BF16)
        gate_buf[0:n, :] = high
        gate_buf[n : 2 * n, :] = (gate - high.astype(F32)).astype(BF16)
        gathers[-1].begin()

        mine = lax.broadcasted_iota(jnp.int32, (n, own), 0) == me
        for s in range(n):
            for u in range(2):
                one = sm[s, TABLES + u * n : TABLES + (u + 1) * n, :].astype(F32)
                one = jnp.sum(jnp.where(mine, one, 0.0), axis=0, keepdims=True)
                named[s : s + 1, u * own : (u + 1) * own] = one
        below = lax.broadcasted_iota(jnp.int32, (seq, seq), 0) <= lax.broadcasted_iota(
            jnp.int32, (seq, seq), 1
        )
        count = dot_single_float(named[...].astype(BF16), below.astype(F32).astype(BF16)) - 1.0
        slots = lax.broadcasted_iota(jnp.int32, (cap, seq), 0).astype(F32)
        for s in range(n):
            here = (count[s : s + 1, :] == slots) & (named[s : s + 1, :] > 0.5)
            table[s] = here.astype(F32).astype(BF16)

        pump_all(place, gathers)
        swap.wait_send()
        for one in gathers:
            one.settle()

    return comm_call(
        kernel,
        (
            sds((own, width), F32),
            sds((n, own), F32),
            sds((1, width), F32),
            sds((n, width), BF16),
            sds((own, width), BF16),
            sds((n, cap, seq), BF16),
            sds((n, seq, width), BF16),
            sds((n, 2, 2 * n, own), BF16),
        ),
        (IN_VMEM,) * 6 + (IN_HBM,) * 2,
        [IN_VMEM] * 3,
        [
            pltpu.VMEM((own, width), F32),
            pltpu.VMEM((2 * n, own), BF16),
            pltpu.VMEM((n, seq), F32),
        ]
        + [gather_sems(n)] * (1 + len(chunks))
        + [pltpu.SemaphoreType.DMA((2,))],
        3,
        "spread_rows",
    )(attn_part, x_own, small_all)


PAIR = 2


def expert_forward(h_all, place_table, gates_all, w_gate, w_up, w_down, shared_w, cot):
    n, seq, width = h_all.shape
    own = seq // 2
    cap, hidden, part = place_table.shape[1], w_gate.shape[0], shared_w.shape[0] // 3
    steps = n // PAIR
    chunks = row_cuts(own, width)

    def kernel(*refs):
        take = pick(refs)
        h, pm, ga, *far, ct = take(8)
        gate, rows, act, on_up, on_gate, s_act, s_on, out_part, ct_all = take(9)
        sems = take(len(chunks))
        orows, *near, bring_sems = take(6)
        wg, wu, wd, sw = near
        place = Place(n)
        t, me = place.t, place.me
        i = pl.program_id(0)
        gathers = row_gathers(
            place, chunks, sems,
            lambda r, c: ct.at[pl.ds(t * own + r.start, r.size), c],
            lambda o, r, c: ct_all.at[o, r, c], own,
        )

        bring = Bring(list(zip(far, near)), bring_sems)

        @pl.when(i == 0)
        def _():
            place.enter()
            for one in gathers:
                one.begin()
            bring.begin()

        @pl.when(i > 0)
        def _():
            pump_gathers(gathers, place.half, i)

        slots = []
        line = lax.broadcasted_iota(jnp.int32, (2 * n, own), 0)
        mine = (line == me) | (line == me + n)
        for k in range(PAIR):
            halves = [
                jnp.sum(jnp.where(mine, ga[k, u].astype(F32), 0.0), axis=0, keepdims=True)
                for u in range(2)
            ]
            gate[k] = jnp.concatenate(halves, 1)
            rows[pl.ds(k * cap, cap), :] = dot_single_float(pm[k], h[k]).astype(BF16)
            slots.append(jnp.sum(pm[k].astype(F32) * gate[k], axis=1, keepdims=True))
        pl.when(i == 0)(bring.wait)
        pre = dot_nt(rows[...], wg[...])
        up = dot_nt(rows[...], wu[...])
        sigm = jax.nn.sigmoid(pre)
        silu = pre * sigm
        act[...] = (silu * up).astype(BF16)
        on_up[...] = silu.astype(BF16)
        on_gate[...] = (up * (sigm * (1.0 + pre * (1.0 - sigm)))).astype(BF16)
        orows[...] = (dot_single_float(act[...], wd[...]) * jnp.concatenate(slots, 0)).astype(BF16)
        for k in range(PAIR):
            at = pl.ds(k * seq, seq)
            both = dot_nt(h[k], sw[0 : 2 * part, :])
            s_pre, s_up = both[:, :part], both[:, part:]
            sigm = jax.nn.sigmoid(s_pre)
            silu = s_pre * sigm
            s_act[at, :] = (silu * s_up).astype(BF16)
            s_on[at, 0:part] = (s_up * (sigm * (1.0 + s_pre * (1.0 - sigm)))).astype(BF16)
            s_on[at, part:] = silu.astype(BF16)
            out_part[k] = (
                dot_tn(pm[k], orows[pl.ds(k * cap, cap), :])
                + dot_single_float(s_act[at, :], sw[2 * part :, :])
            ).astype(BF16)

        @pl.when(i == steps - 1)
        def _():
            for one in gathers:
                one.close()
            for one in gathers:
                one.settle()

    return grid_call(
        kernel,
        steps,
        [by_seq(PAIR, seq, width), by_seq(PAIR, cap, seq), by_seq(PAIR, 2, 2 * n, own)]
        + [IN_HBM] * 5,
        (
            (by_seq(PAIR, 1, seq), (n, 1, seq), F32),
            (by_rows(PAIR * cap, width), (n * cap, width), BF16),
            (by_rows(PAIR * cap, hidden), (n * cap, hidden), BF16),
            (by_rows(PAIR * cap, hidden), (n * cap, hidden), BF16),
            (by_rows(PAIR * cap, hidden), (n * cap, hidden), BF16),
            (by_rows(PAIR * seq, part), (n * seq, part), BF16),
            (by_rows(PAIR * seq, 2 * part), (n * seq, 2 * part), BF16),
            (by_seq(PAIR, seq, width), (n, seq, width), BF16),
            (IN_HBM, (n, seq, width), BF16),
        ),
        [gather_sems(n)] * len(chunks)
        + [pltpu.VMEM((PAIR * cap, width), BF16)]
        + room_for((w_gate, w_up, w_down, shared_w)),
        4,
        "expert_forward",
    )(h_all, place_table, gates_all, w_gate, w_up, w_down, shared_w, cot)


def expert_back(
    out_part, resid, cot_all, place_table, gate, act, on_up, on_gate, s_on,
    w_gate, w_up, w_down, shared_w,
):
    n, seq, width = cot_all.shape
    own = seq // 2
    cap, hidden, part = place_table.shape[1], w_gate.shape[0], shared_w.shape[0] // 3
    steps = n // PAIR
    chunks = row_cuts(own, width)

    def kernel(*refs):
        take = pick(refs)
        p, res, ct, pm, gt, ac, ou, og, so, *far = take(13)
        out, heap, dy, dge, due, d_spre, dh, dgt = take(8)
        scratch = [take(6) for _ in chunks]
        total, cr, dr, *near, bring_sems = take(8)
        wg, wu, wd, sw = near
        place = Place(n)
        me = place.me
        i = pl.program_id(0)
        scatters = row_scatters(place, chunks, scratch, p, heap, own)
        bring = Bring(list(zip(far, near)), bring_sems)

        @pl.when(i == 0)
        def _():
            place.enter()
            bring.begin()
            open_scatters(scatters)

        @pl.when(i > 0)
        def _():
            step_scatters(place, scatters, i)

        slots = []
        for k in range(PAIR):
            cr[pl.ds(k * cap, cap), :] = dot_single_float(pm[k], ct[k]).astype(BF16)
            slots.append(jnp.sum(pm[k].astype(F32) * gt[k], axis=1, keepdims=True))
        gs = jnp.concatenate(slots, 0)
        pl.when(i == 0)(bring.wait)
        plain_da = dot_nt(cr[...], wd[...])
        dgs = jnp.sum(plain_da * ac[...].astype(F32), axis=1, keepdims=True)
        da = plain_da * gs
        dge[...] = (da * og[...].astype(F32)).astype(BF16)
        due[...] = (da * ou[...].astype(F32)).astype(BF16)
        dy[...] = (cr[...].astype(F32) * gs).astype(BF16)

        dr[...] = (
            dot_single_float(dge[...], wg[...]) + dot_single_float(due[...], wu[...])
        ).astype(BF16)
        line = lax.broadcasted_iota(jnp.int32, (2 * n, own), 0)
        for k in range(PAIR):
            at = pl.ds(k * cap, cap)
            s_at = pl.ds(k * seq, seq)
            ds = dot_nt(ct[k], sw[2 * part :, :])
            d_spre[s_at, 0:part] = (ds * so[s_at, 0:part].astype(F32)).astype(BF16)
            d_spre[s_at, part:] = (ds * so[s_at, part:].astype(F32)).astype(BF16)
            dh[k] = (
                dot_tn(pm[k], dr[at, :])
                + dot_single_float(d_spre[s_at, :], sw[0 : 2 * part, :])
            ).astype(BF16)
            dg = jnp.sum(pm[k].astype(F32) * dgs[k * cap : (k + 1) * cap], axis=0, keepdims=True)
            for u in range(2):
                one = dg[:, u * own : (u + 1) * own]
                high = one.astype(BF16).astype(F32)
                both = jnp.where(line == me, high, jnp.where(line == me + n, one - high, 0.0))
                dgt[k, u] = both.astype(BF16)

        @pl.when(i == steps - 1)
        def _():
            for s, (_, b, rows, c0, w) in zip(scatters, chunks):
                s.close(total.at[pl.ds(b, rows), pl.ds(c0, w)])
            add_rows(out, [total, res], 0, own, width)

    scratch = []
    for _, _, size, _, w in chunks:
        scratch += scatter_scratch(n, size, w)
    scratch += [
        pltpu.VMEM((own, width), F32),
        pltpu.VMEM((PAIR * cap, width), BF16),
        pltpu.VMEM((PAIR * cap, width), BF16),
    ] + room_for((w_gate, w_up, w_down, shared_w))
    return grid_call(
        kernel,
        steps,
        [IN_HBM, whole(resid), by_seq(PAIR, seq, width), by_seq(PAIR, cap, seq)]
        + [by_seq(PAIR, 1, seq)]
        + [by_rows(PAIR * cap, hidden)] * 3
        + [by_rows(PAIR * seq, 2 * part)]
        + [IN_HBM] * 4,
        (
            (IN_VMEM, (own, width), BF16),
            (IN_HBM, (n, own, width), BF16),
            (by_rows(PAIR * cap, width), (n * cap, width), BF16),
            (by_rows(PAIR * cap, hidden), (n * cap, hidden), BF16),
            (by_rows(PAIR * cap, hidden), (n * cap, hidden), BF16),
            (by_rows(PAIR * seq, 2 * part), (n * seq, 2 * part), BF16),
            (by_seq(PAIR, seq, width), (n, seq, width), BF16),
            (by_seq(PAIR, 2, 2 * n, own), (n, 2, 2 * n, own), BF16),
        ),
        scratch,
        5,
        "expert_back",
    )(
        out_part, resid, cot_all, place_table, gate, act, on_up, on_gate, s_on,
        w_gate, w_up, w_down, shared_w,
    )


def sum_rows(
    parts, gate_parts, sel, router_t, resid, gain, cot, normed_own,
    rows, dy, act, dge, due, s_act, d_spre, h_all, cot_all,
):
    n, seq, width = parts.shape
    own = seq // 2
    chunks = row_cuts(own, width)
    hidden, part = act.shape[1], s_act.shape[1]
    steps = n // 2
    cols = width // steps
    slots = rows.shape[0]

    def kernel(*refs):
        take = pick(refs)
        p, gp, se, wr, res, g, gr, hn = take(8)
        r_in, y_in, *far, h_in, c_in = take(9)
        g2_out, wr_out, d_resid, d_attn, heap, gate_heap = take(6)
        g_gate, g_up, g_down, g_shared = take(4)
        scratch = [take(6) for _ in range(len(chunks) + 1)]
        dg, ex_sems, dh, swap, gr_own, hn_own, *near, bring_sems = take(12)
        a_in, ge_in, ue_in, sa_in, sp_in = near
        place = Place(n)
        t = place.t
        i = pl.program_id(0)
        scatters = row_scatters(place, chunks, scratch, p, heap, own)
        gates = Scatter(
            place, 0, (2 * n, own), lambda o, u: gp.at[o, u], scratch[-1],
            lambda o: gate_heap.at[o],
        )
        bring = Bring(
            list(zip(far, near)) + [(gr.at[pl.ds(t * own, own)], gr_own), (hn, hn_own)], bring_sems
        )

        @pl.when(i == 0)
        def _():
            place.enter()
            bring.begin()
            open_scatters(scatters + [gates])
            bring.wait()

        @pl.when(i > 0)
        def _():
            step_scatters(place, scatters + [gates], i)

        g_gate[...] = dot_tn(ge_in[...], r_in[...]).astype(g_gate.dtype)
        g_up[...] = dot_tn(ue_in[...], r_in[...]).astype(g_up.dtype)

        g_down[...] = dot_tn(a_in[...], y_in[...]).astype(g_down.dtype)
        g_shared[0 : 2 * part, :] = dot_tn(sp_in[...], h_in[...]).astype(BF16)
        g_shared[2 * part :, :] = dot_tn(sa_in[...], c_in[...]).astype(BF16)

        @pl.when(i == steps - 1)
        def _():
            for s, (_, b, r, c0, w) in zip(scatters, chunks):
                s.close(dh.at[pl.ds(b, r), pl.ds(c0, w)])
            gates.close(dg)
            dgate = dg[0:n, :] + dg[n : 2 * n, :]
            s = se[...]
            total = jnp.sum(s, axis=0, keepdims=True)
            dsel = ROUTE_SCALE * (
                dgate / total - jnp.sum(dgate * s, axis=0, keepdims=True) / (total * total)
            )
            dl = (dsel * s * (1.0 - s)).astype(BF16)
            wr_out[...] = dot_single_float(dl, hn_own[...])
            dh[...] += dot_tn(dl, wr[...])
            size = 16

            def rows_back(j, acc):
                at = pl.ds(pl.multiple_of(j * size, size), size)
                mine = pl.ds(pl.multiple_of(t * own + j * size, size), size)
                v = res[at, :]
                r, one = inv_rms(v), dh[at, :]
                out = gr_own[at, :].astype(F32) + norm_back(v, r, g[...], one)
                d_resid[at, :] = out
                d_attn[mine, :] = out.astype(BF16)
                swap[0, at, :] = out.astype(BF16)
                return acc + jnp.sum(one * (v * r), axis=0, keepdims=True)

            g2_out[...] = lax.fori_loop(0, own // size, rows_back, jnp.zeros((1, width), F32))
            give = remote(swap.at[0], swap.at[1], ex_sems.at[0], ex_sems.at[1], place.twin)
            give.start()
            give.wait_recv()
            d_attn[pl.ds(pl.multiple_of((1 - t) * own, own), own), :] = swap[1]
            give.wait_send()

    scratch = []
    for _, _, size, _, w in chunks:
        scratch += scatter_scratch(n, size, w)
    scratch += scatter_scratch(n, 2 * n, own)
    scratch += [
        pltpu.VMEM((2 * n, own), F32),
        pltpu.SemaphoreType.DMA((2,)),
        pltpu.VMEM((own, width), F32),
        pltpu.VMEM((2, own, width), BF16),
        pltpu.VMEM((own, width), BF16),
        pltpu.VMEM((own, width), BF16),
        *[pltpu.VMEM(a.shape, a.dtype) for a in (act, dge, due, s_act, d_spre)],
        pltpu.SemaphoreType.DMA((7,)),
    ]
    return grid_call(
        kernel,
        steps,
        [IN_HBM, IN_HBM]
        + [whole(a) for a in (sel, router_t, resid, gain)]
        + [IN_HBM] * 2
        + [by_cols(slots, cols)] * 2
        + [IN_HBM] * 5
        + [by_cols(n * seq, cols)] * 2,
        (
            (IN_VMEM, (1, width), F32),
            (IN_VMEM, (n, width), F32),
            (IN_VMEM, (own, width), F32),
            (IN_VMEM, (seq, width), BF16),
            (IN_HBM, (n, own, width), BF16),
            (IN_HBM, (n, 2 * n, own), BF16),
            (by_cols(hidden, cols), (hidden, width), EXPERT_GRADS),
            (by_cols(hidden, cols), (hidden, width), EXPERT_GRADS),
            (by_cols(hidden, cols), (hidden, width), EXPERT_GRADS),
            (by_cols(3 * part, cols), (3 * part, width), BF16),
        ),
        scratch,
        6,
        "sum_row_gradients",
    )(
        parts, gate_parts, sel, router_t, resid, gain, cot, normed_own,
        rows, dy, act, dge, due, s_act, d_spre,
        h_all.reshape(n * seq, width), cot_all.reshape(n * seq, width),
    )


EXPERT_GRADS = BF16


def attend_back(
    n, d_attn, x_seq, h1, latent, cn, gain_kv, k_rope, cos2, sin2, w_kvd,
    q_n, q_r, kv, ctx, w_q, w_kvu, w_out, g2_small, wr_small, g_shared, padded,
):
    seq, width = x_seq.shape
    head = DN + DR
    pairs = w_q.shape[1] // (2 * head)
    factor = 1.0 / math.sqrt(head)
    cols = width // n
    part_rows = g_shared.shape[0] // 3

    def kernel(*refs):
        take = pick(refs)
        da, x, h, lat, c_n, gk, kpe, co, si, wd, g2s, wrs = take(12)
        gsh, qn, qr, kvb, cx, wq, wu, wo = take(8)
        dh_out, g_kvd, small, sh_got = take(4)
        g_wq, g_wu, g_wo = take(3)
        trade_sems, dh, dcn, dkr, dq, dkv, dctx = take(7)
        place = Place(n)
        i = pl.program_id(0)
        trade = Trade(
            place,
            [
                lambda k, j=j: gsh.at[pl.ds(j * part_rows, padded), pl.ds(k * cols, cols)]
                for j in range(3)
            ],
            [lambda k, j=j: sh_got.at[k, j] for j in range(3)],
            trade_sems,
        )

        @pl.when(i == 0)
        def _():
            place.enter(everyone=True)
            trade.begin()
            dh[...] = jnp.zeros_like(dh)
            dcn[...] = jnp.zeros_like(dcn)
            dkr[...] = jnp.zeros_like(dkr)

        dctx[...] = dot_nt(da[...], wo[...]).astype(BF16)
        g_wo[...] = dot_tn(cx[...], da[...]).astype(BF16)
        for k in range(2):
            base = k * (DN + DV)
            keys, values = kvb[:, base : base + DN], kvb[:, base + DN : base + DN + DV]
            one_n, one_r = qn[:, k * DN : (k + 1) * DN], qr[:, k * DR : (k + 1) * DR]
            d_one = dctx[:, k * DV : (k + 1) * DV]
            weights = causal_weights(one_n, one_r, keys, kpe[...], factor)
            dw = dot_nt(d_one, values)
            ds = (weights * (dw - jnp.sum(weights * dw, axis=1, keepdims=True))).astype(BF16)
            dq[:, k * head : k * head + DN] = (dot_single_float(ds, keys) * factor).astype(BF16)
            d_rope = dot_single_float(ds, kpe[...]) * factor
            dq[:, k * head + DN : (k + 1) * head] = (
                d_rope * co[...] - swapped(d_rope) * si[...]
            ).astype(BF16)
            dkv[:, base : base + DN] = (dot_tn(ds, one_n) * factor).astype(BF16)
            dkr[...] += dot_tn(ds, one_r) * factor
            dkv[:, base + DN : base + DN + DV] = dot_tn(weights.astype(BF16), d_one).astype(BF16)
        g_wq[...] = dot_tn(h[...], dq[...]).astype(BF16)
        g_wu[...] = dot_tn(c_n[...], dkv[...]).astype(BF16)
        dcn[...] += dot_nt(dkv[...], wu[...])
        dh[...] += dot_nt(dq[...], wq[...])

        @pl.when(i == pairs - 1)
        def _():
            lt = lat[...]
            factor_kv = inv_rms(lt)
            back = dcn[...]
            g_gain = jnp.sum(back * lt * factor_kv, axis=0, keepdims=True)
            d_lat = norm_back(lt, factor_kv, gk[...], back)
            d_rope = dkr[...]
            d_rope = d_rope * co[...] - swapped(d_rope) * si[...]
            d_first = jnp.concatenate([d_lat, d_rope], 1).astype(BF16)
            g_kvd[...] = dot_tn(h[...], d_first).astype(BF16)
            dh[...] += dot_single_float(d_first, wd[...])
            size = 16

            def finish(j, acc):
                at = pl.ds(pl.multiple_of(j * size, size), size)
                v = x[at, :].astype(F32)
                one = dh[at, :]
                dh_out[at, :] = one.astype(BF16)
                return acc + jnp.sum(one * (v * inv_rms(v)), axis=0, keepdims=True)

            g_one = lax.fori_loop(0, seq // size, finish, jnp.zeros((1, width), F32))
            small[...] = jnp.zeros_like(small)
            kv_cols = KVR // n
            for o in range(n):
                at = slice(o * cols, (o + 1) * cols)
                small[o, 0:1, :] = g_one[:, at].astype(BF16)
                small[o, 1:2, :] = g2s[:, at].astype(BF16)
                small[o, 2:3, 0:kv_cols] = g_gain[:, o * kv_cols : (o + 1) * kv_cols].astype(BF16)
                small[o, 16 : 16 + n, :] = wrs[:, at].astype(BF16)
            trade.settle()

    scratch = [
        pltpu.SemaphoreType.DMA((2, n, 3)),
        pltpu.VMEM((seq, width), F32),
        pltpu.VMEM((seq, KVR), F32),
        pltpu.VMEM((seq, DR), F32),
        pltpu.VMEM((seq, 2 * head), BF16),
        pltpu.VMEM((seq, 2 * (DN + DV)), BF16),
        pltpu.VMEM((seq, 2 * DV), BF16),
    ]
    resident = (
        d_attn, x_seq, h1, latent, cn, gain_kv, k_rope, cos2, sin2, w_kvd, g2_small, wr_small,
    )
    return grid_call(
        kernel,
        pairs,
        [whole(a) for a in resident]
        + [
            IN_HBM,
            by_cols(seq, 2 * DN),
            by_cols(seq, 2 * DR),
            by_cols(seq, 2 * (DN + DV)),
            by_cols(seq, 2 * DV),
            by_cols(width, 2 * head),
            by_cols(KVR, 2 * (DN + DV)),
            by_rows(2 * DV, width),
        ],
        (
            (IN_VMEM, (seq, width), BF16),
            (IN_VMEM, (width, KVR + DR), BF16),
            (IN_VMEM, (n, 32, cols), BF16),
            (IN_HBM, (n, 3, padded, cols), BF16),
            (by_cols(width, 2 * head), w_q.shape, BF16),
            (by_cols(KVR, 2 * (DN + DV)), w_kvu.shape, BF16),
            (by_rows(2 * DV, width), w_out.shape, BF16),
        ),
        scratch,
        7,
        "attend_back",
    )(*resident, g_shared, q_n, q_r, kv, ctx, w_q, w_kvu, w_out)


def sum_weights(n, g_query, g_kvu, g_out, g_kvd, g_small, dh1, x_own, d_resid, gain, g_shared, hidden):
    q_rows, q_cols = g_query.shape[0] // n, g_query.shape[1]
    cut = q_cols // 4 * 3
    o_rows, o_cols = g_out.shape[0], g_out.shape[1] // n
    u_rows, u_cols = g_kvu.shape[0] // n, g_kvu.shape[1]
    d_rows, d_cols = g_kvd.shape[0] // (2 * n), g_kvd.shape[1]
    s_rows, s_cols = g_small.shape[1:]
    seq, width = dh1.shape
    own = seq // 2
    specs = [
        (0, (q_rows, cut)),
        (1, (q_rows, q_cols - cut)),
        (2, (o_rows, o_cols)),
        (1, (u_rows, u_cols)),
        (1, (d_rows, d_cols)),
        (2, (s_rows, s_cols)),
    ]

    def kernel(*refs):
        take = pick(refs)
        q, ku, wo, kd, sm, dh, x, dr, g, sh = take(10)
        q_out, ku_out, wo_out, kd_out, sm_out, in_out, sg_out, su_out, sd_out = take(9)
        kd_heap, sm_heap = take(2)
        scratch = [take(6) for _ in specs]
        got, swap_sems, turned = take(3)
        place = Place(n)
        t = place.t
        place.enter()
        swap = remote(
            dh.at[pl.ds((1 - t) * own, own)], got, swap_sems.at[0], swap_sems.at[1], place.twin
        )
        swap.start()
        views = [
            lambda o, u: q.at[pl.ds(o * q_rows, q_rows), pl.ds(0, cut)],
            lambda o, u: q.at[pl.ds(o * q_rows, q_rows), pl.ds(cut, q_cols - cut)],
            lambda o, u: wo.at[:, pl.ds(o * o_cols, o_cols)],
            lambda o, u: ku.at[pl.ds(o * u_rows, u_rows)],
            lambda o, u: kd.at[pl.ds((o * 2 + u) * d_rows, d_rows)],
            lambda o, u: sm.at[o],
        ]
        heaps = [None] * 4 + [lambda o: kd_heap.at[o], lambda o: sm_heap.at[o]]
        scatters = [
            Scatter(place, ring, shape, view, more, heap)
            for (ring, shape), view, more, heap in zip(specs, views, scratch, heaps)
        ]
        outs = [
            q_out.at[:, pl.ds(0, cut)],
            q_out.at[:, pl.ds(cut, q_cols - cut)],
            wo_out,
            ku_out,
            kd_out,
            sm_out,
        ]

        def grad_in():
            swap.wait_recv()
            size = 16

            def rows_back(j, _):
                at = pl.ds(pl.multiple_of(j * size, size), size)
                mine = pl.ds(pl.multiple_of(t * own + j * size, size), size)
                v = x[at, :].astype(F32)
                one = dh[mine, :].astype(F32) + got[at, :].astype(F32)
                in_out[at, :] = (dr[at, :] + norm_back(v, inv_rms(v), g[...], one)).astype(BF16)
                return 0

            lax.fori_loop(0, own // size, rows_back, 0)

        def put_together(j, out):
            for k in range(n):
                turned[k * hidden : (k + 1) * hidden, :] = sh[k, j, 0:hidden, :].astype(F32)
            if j < 2:
                out[...] = dot_nt(eye(q_rows), turned[...].astype(BF16))
            else:
                out[...] = turned[...]

        beside = [grad_in] + [
            lambda j=j, out=out: put_together(j, out)
            for j, out in enumerate((sg_out, su_out, sd_out))
        ]
        run_scatters(place, scatters, outs, beside)
        swap.wait_send()

    scratch = []
    for _, shape in specs:
        scratch += scatter_scratch(n, *shape)
    scratch += [
        pltpu.VMEM((own, width), BF16),
        pltpu.SemaphoreType.DMA((2,)),
        pltpu.VMEM((n * hidden, q_rows), F32),
    ]
    return comm_call(
        kernel,
        (
            sds((q_rows, q_cols), F32),
            sds((u_rows, u_cols), F32),
            sds((o_rows, o_cols), F32),
            sds((d_rows, d_cols), F32),
            sds((s_rows, s_cols), F32),
            sds((own, width), BF16),
            sds((q_rows, n * hidden), F32),
            sds((q_rows, n * hidden), F32),
            sds((n * hidden, q_rows), F32),
            sds((n, d_rows, d_cols), BF16),
            sds((n, s_rows, s_cols), BF16),
        ),
        (IN_VMEM,) * 9 + (IN_HBM,) * 2,
        [IN_HBM] * 5 + [IN_VMEM] * 5,
        scratch,
        8,
        "sum_weights",
    )(g_query, g_kvu, g_out, g_kvd, g_small, dh1, x_own, d_resid, gain, g_shared)[:9]


def fast(
    hidden_in,
    routes,
    cotangent,
    norm_attn,
    query_proj,
    kv_down,
    kv_norm,
    kv_up,
    out_proj,
    norm_ffn,
    router_proj,
    shared_gate,
    shared_up,
    shared_down,
    expert_gate,
    expert_up_weight,
    expert_down,
):
    n = lax.axis_size("fsdp")
    own, width = hidden_in.shape
    seq = 2 * own
    cap = 4 * seq * TOP // (3 * n)
    t = lax.axis_index("tp")
    cos_table, sin_table = rope_tables(seq, DR)
    cos2 = jnp.concatenate([cos_table, cos_table], 1)
    sin2 = jnp.concatenate([-sin_table, sin_table], 1)
    model_rows, latent_rows = norm_attn.shape[0], kv_norm.shape[0]
    hidden = shared_gate.shape[1] // n

    full_wq, full_wkva, full_wkvb, full_wo, small_all, x_seq, blocks = collect_inputs(
        n,
        query_proj,
        kv_down.T,
        kv_up,
        out_proj,
        hidden_in,
        norm_attn[None],
        norm_ffn[None],
        jnp.pad(kv_norm, (0, model_rows - latent_rows))[None],
        router_proj.T,
        routes.T,
        shared_gate,
        shared_up,
        shared_down,
    )
    (
        attn_part, h1, full_g1, full_gkv, latent, latent_normed, key_rope, shared_w,
        q_n, q_r, kv, context,
    ) = attend(
        n, x_seq, small_all, full_wkva, cos2, sin2, full_wq, full_wkvb, full_wo, blocks
    )
    resid, sel, full_g2, router_t, normed_own, place_table, h_all, gates_all = spread_rows(
        n, attn_part, hidden_in, small_all, cap
    )
    w_gate, w_up, w_down = expert_gate[0].T, expert_up_weight[0].T, expert_down[0]
    gate, rows, act, on_up, on_gate, sh_act, sh_on, out_part, cot_all = expert_forward(
        h_all, place_table, gates_all, w_gate, w_up, w_down, shared_w, cotangent
    )
    hidden_out, _, d_out_rows, d_pre_gate, d_pre_up, d_sh_pre, dh2_part, d_gates = expert_back(
        out_part, resid, cot_all, place_table, gate, act, on_up, on_gate, sh_on,
        w_gate, w_up, w_down, shared_w,
    )
    (
        grad_g2, grad_wr, d_resid, d_attn, _, _, grad_egate, grad_eup, grad_edown, grad_shared,
    ) = sum_rows(
        dh2_part, d_gates, sel, router_t, resid, full_g2, cotangent, normed_own,
        rows, d_out_rows, act, d_pre_gate, d_pre_up, sh_act, d_sh_pre, h_all, cot_all,
    )
    dh1_part, grad_wkva, grad_small, out_shared, grad_wq, grad_wkvb, grad_wo = attend_back(
        n, d_attn, x_seq, h1, latent, latent_normed, full_gkv, key_rope, cos2, sin2, full_wkva,
        q_n, q_r, kv, context, full_wq, full_wkvb, full_wo, grad_g2, grad_wr, grad_shared,
        blocks.shape[2],
    )
    (
        out_wq, out_wkvb, out_wo, out_wkva, out_small, grad_in, out_sgate, out_sup, out_sdown,
    ) = sum_weights(
        n, grad_wq, grad_wkvb, grad_wo, grad_wkva, grad_small, dh1_part, hidden_in, d_resid,
        full_g1, out_shared, hidden,
    )
    keep, keep_kv = model_rows // 2, latent_rows // 2
    kv_small = lax.dynamic_slice_in_dim(out_small[2], t * keep_kv, keep_kv, 0)
    out_small = lax.dynamic_slice_in_dim(out_small, t * keep, keep, 1)
    return (
        hidden_out,
        grad_in,
        out_small[0],
        out_wq,
        out_wkva,
        kv_small,
        out_wkvb,
        out_wo,
        out_small[1],
        out_small[16 : 16 + n].T,
        out_sgate,
        out_sup,
        out_sdown,
        grad_egate.T[None].astype(F32),
        grad_eup.T[None].astype(F32),
        grad_edown[None].astype(F32),
    )


def suits(mesh):
    return mesh.shape["tp"] == 2 and mesh.shape["fsdp"] * 128 == MODEL_WIDTH


def solution(mesh):
    return jax.shard_map(
        fast if suits(mesh) else plain,
        mesh=mesh,
        in_specs=(
            P(("fsdp", "tp"), None),
            P("fsdp", None),
            P("fsdp", None),
            P("fsdp"),
            P("fsdp", "tp"),
            P("fsdp", None),
            P("fsdp"),
            P("fsdp", "tp"),
            P("tp", "fsdp"),
            P("fsdp"),
            P("fsdp", None),
            P("fsdp", "tp"),
            P("fsdp", "tp"),
            P("tp", "fsdp"),
            P("fsdp", None, "tp"),
            P("fsdp", None, "tp"),
            P("fsdp", "tp", None),
        ),
        out_specs=(
            P(("fsdp", "tp"), None),
            P(("fsdp", "tp"), None),
            P(("fsdp", "tp")),
            P("fsdp", "tp"),
            P(("fsdp", "tp"), None),
            P(("fsdp", "tp")),
            P("fsdp", "tp"),
            P("tp", "fsdp"),
            P(("fsdp", "tp")),
            P(("fsdp", "tp"), None),
            P("fsdp", "tp"),
            P("fsdp", "tp"),
            P("tp", "fsdp"),
            P("fsdp", None, "tp"),
            P("fsdp", None, "tp"),
            P("fsdp", "tp", None),
        ),
        check_vma=False,
    )
```

```python
import math

import jax
import jax.numpy as jnp
from jax import lax
from jax.experimental import pallas as pl
from jax.experimental.pallas import tpu as pltpu
from jax.sharding import PartitionSpec as P

MODEL_WIDTH = 2048
DN = 128
DR = 64
DV = 128
KVR = 512
TOP = 6


NORM_EPS = 1e-06
ROPE_THETA = 50000.0
ROUTE_SCALE = 2.446


def dot_single_float(left, right):
    return jnp.dot(left, right, preferred_element_type=jnp.float32)


def dot_high(left, right):
    return jnp.dot(left, right, precision=lax.Precision.HIGHEST, preferred_element_type=jnp.float32)


def inv_rms(value):
    return lax.rsqrt(jnp.mean(value * value, axis=-1, keepdims=True) + NORM_EPS)


def norm_back(value, factor, gain, grad):
    scaled = grad * gain
    return factor * scaled - value * factor**3 * jnp.mean(scaled * value, axis=-1, keepdims=True)


def silu_grad(value):
    sigm = jax.nn.sigmoid(value)
    return sigm * (1.0 + value * (1.0 - sigm))


def rope_tables(length, width):
    half_width = width // 2
    freq = ROPE_THETA ** (-(jnp.arange(half_width, dtype=jnp.float32) * 2.0 / width))
    angle = jnp.arange(length, dtype=jnp.float32)[:, None] * freq[None, :]
    return (jnp.cos(angle), jnp.sin(angle))


def rotate(value, cos_table, sin_table):
    half_width = value.shape[-1] // 2
    first, second = (value[..., :half_width], value[..., half_width:])
    return jnp.concatenate(
        [first * cos_table - second * sin_table, second * cos_table + first * sin_table], -1
    )


def unrotate(grad, cos_table, sin_table):
    half_width = grad.shape[-1] // 2
    first, second = (grad[..., :half_width], grad[..., half_width:])
    return jnp.concatenate(
        [first * cos_table + second * sin_table, second * cos_table - first * sin_table], -1
    )


def scores_of(query, keys, factor):
    length = query.shape[0]
    raw_scores = (
        jnp.einsum("qhd,khd->hqk", query, keys, preferred_element_type=jnp.float32) * factor
    )
    causal = jnp.arange(length)[:, None] >= jnp.arange(length)[None, :]
    return jnp.where(causal[None], raw_scores, -1e30)


def plain(
    hidden_in,
    routes,
    cotangent,
    norm_attn,
    query_proj,
    kv_down,
    kv_norm,
    kv_up,
    out_proj,
    norm_ffn,
    router_proj,
    shared_gate,
    shared_up,
    shared_down,
    expert_gate,
    expert_up_weight,
    expert_down,
):
    n_tp = lax.axis_size("tp")
    sharded_parts_count = lax.axis_size("fsdp")
    own_rows = hidden_in.shape[0]
    seq_len = own_rows * n_tp
    head_width = DN + DR
    heads_here = query_proj.shape[1] // head_width
    expert_capacity = 4 * seq_len * TOP // (3 * sharded_parts_count)
    tp_index = lax.axis_index("tp")
    factor = 1.0 / math.sqrt(head_width)
    cos_table, sin_table = rope_tables(seq_len, DR)

    def arrange(grad):
        rest = grad.shape[1:]
        block = grad.shape[0] // (sharded_parts_count * n_tp)
        split = grad.reshape((sharded_parts_count, n_tp, block) + rest)
        return jnp.swapaxes(split, 0, 1).reshape((grad.shape[0],) + rest)

    x_group = lax.all_gather(hidden_in, "tp", axis=0, tiled=True).astype(jnp.float32)
    full_g1, full_wq, full_wkva, full_gkv, full_wkvb, full_wo = (
        lax.all_gather(norm_attn, "fsdp", axis=0, tiled=True),
        lax.all_gather(query_proj, "fsdp", axis=0, tiled=True),
        lax.all_gather(kv_down, "fsdp", axis=0, tiled=True),
        lax.all_gather(kv_norm, "fsdp", axis=0, tiled=True),
        lax.all_gather(kv_up, "fsdp", axis=0, tiled=True),
        lax.all_gather(out_proj, "fsdp", axis=1, tiled=True),
    )
    factor_one = inv_rms(x_group)
    x_normed = x_group * factor_one
    normed_in = (x_normed * full_g1.astype(jnp.float32)).astype(jnp.bfloat16)
    query_raw = dot_single_float(normed_in, full_wq).reshape(seq_len, heads_here, head_width)
    query = jnp.concatenate(
        [query_raw[..., :DN], rotate(query_raw[..., DN:], cos_table[:, None], sin_table[:, None])],
        -1,
    ).astype(jnp.bfloat16)
    kv_first = dot_single_float(normed_in, full_wkva)
    latent = kv_first[:, :KVR]
    latent_factor = inv_rms(latent)
    latent_normed = (latent * latent_factor * full_gkv.astype(jnp.float32)).astype(jnp.bfloat16)
    key_rope = rotate(kv_first[:, KVR:], cos_table, sin_table).astype(jnp.bfloat16)
    kv_full = (
        dot_single_float(latent_normed, full_wkvb)
        .astype(jnp.bfloat16)
        .reshape(seq_len, heads_here, DN + DV)
    )
    keys = jnp.concatenate(
        [kv_full[..., :DN], jnp.broadcast_to(key_rope[:, None, :], (seq_len, heads_here, DR))], -1
    )
    values = kv_full[..., DN:]
    scores = scores_of(query, keys, factor)
    top_score = jnp.max(scores, axis=-1, keepdims=True)
    log_total = top_score + jnp.log(jnp.sum(jnp.exp(scores - top_score), axis=-1, keepdims=True))
    weights_bf = jnp.exp(scores - log_total).astype(jnp.bfloat16)
    context = jnp.einsum("hqk,khd->qhd", weights_bf, values, preferred_element_type=jnp.float32)
    context = context.reshape(seq_len, heads_here * DV).astype(jnp.bfloat16)
    attn_own = lax.psum_scatter(
        dot_single_float(context, full_wo), "tp", scatter_dimension=0, tiled=True
    )
    x_own = hidden_in.astype(jnp.float32)
    resid = x_own + attn_own
    full_g2, full_wr, full_sg, full_su, full_sd = (
        lax.all_gather(norm_ffn, "fsdp", axis=0, tiled=True),
        lax.all_gather(router_proj, "fsdp", axis=0, tiled=True),
        lax.all_gather(shared_gate, "fsdp", axis=0, tiled=True),
        lax.all_gather(shared_up, "fsdp", axis=0, tiled=True),
        lax.all_gather(shared_down, "fsdp", axis=1, tiled=True),
    )
    factor_two = inv_rms(resid)
    resid_normed = resid * factor_two
    normed_own = (resid_normed * full_g2.astype(jnp.float32)).astype(jnp.bfloat16)
    normed_ffn = lax.all_gather(normed_own, "tp", axis=0, tiled=True)
    logits = dot_single_float(normed_ffn, full_wr)
    sigmoids = jax.nn.sigmoid(logits)
    chosen = jnp.take_along_axis(sigmoids, routes, axis=1)
    chosen_sum = jnp.sum(chosen, axis=-1, keepdims=True)
    gate_values = ROUTE_SCALE * chosen / chosen_sum
    flat_routes = routes.reshape(-1)
    one_hot = (
        flat_routes[:, None] == jnp.arange(sharded_parts_count, dtype=jnp.int32)[None, :]
    ).astype(jnp.int32)
    slot_num = jnp.sum((jnp.cumsum(one_hot, axis=0) - one_hot) * one_hot, axis=-1)
    target = flat_routes * expert_capacity + slot_num
    token_of = jnp.arange(seq_len * TOP, dtype=jnp.int32) // TOP
    send_rows = (
        jnp.zeros((sharded_parts_count * expert_capacity, MODEL_WIDTH), jnp.bfloat16)
        .at[target]
        .set(normed_ffn[token_of])
    )
    send_rows = send_rows.reshape(sharded_parts_count, expert_capacity, MODEL_WIDTH)
    expert_gate_weight = expert_gate[0]
    routed_up_weight = expert_up_weight[0]
    w_edown = expert_down[0]
    arrived = lax.all_to_all(send_rows, "fsdp", split_axis=0, concat_axis=0, tiled=True)
    sources = arrived.shape[0]
    items = arrived.shape[1]
    flattened_input = arrived.reshape(sources * items, MODEL_WIDTH)
    pre_gate = dot_single_float(flattened_input, expert_gate_weight)
    up_projected = dot_single_float(flattened_input, routed_up_weight)
    activ = (jax.nn.silu(pre_gate) * up_projected).astype(jnp.bfloat16)
    output = (
        dot_single_float(activ, w_edown).astype(jnp.bfloat16).reshape(sources, items, MODEL_WIDTH)
    )
    returned = lax.all_to_all(output, "fsdp", split_axis=0, concat_axis=0, tiled=True)
    hidden_shape = (sources, items, pre_gate.shape[-1])
    returned, arrived, pre_gate, up_projected, activ = (
        returned,
        arrived,
        pre_gate.reshape(hidden_shape),
        up_projected.reshape(hidden_shape),
        activ.reshape(hidden_shape),
    )
    pair_rows = returned.reshape(sharded_parts_count * expert_capacity, MODEL_WIDTH)[
        target
    ].reshape(seq_len, TOP, MODEL_WIDTH)
    routed_rows = jnp.sum(gate_values[..., None] * pair_rows, axis=1)
    shared_pre_gate = dot_single_float(normed_ffn, full_sg)
    shared_pre_up = dot_single_float(normed_ffn, full_su)
    shared_act = (jax.nn.silu(shared_pre_gate) * shared_pre_up).astype(jnp.bfloat16)
    ffn_own = lax.psum_scatter(
        (routed_rows + dot_single_float(shared_act, full_sd)).astype(jnp.bfloat16),
        "tp",
        scatter_dimension=0,
        tiled=True,
    ).astype(jnp.float32)
    hidden_out = (resid + ffn_own).astype(jnp.bfloat16)
    grad_own = lax.dynamic_slice_in_dim(cotangent, tp_index * own_rows, own_rows, 0).astype(
        jnp.float32
    )
    d_shared = dot_single_float(cotangent, full_sd.T)
    d_sgate = (d_shared * shared_pre_up * silu_grad(shared_pre_gate)).astype(jnp.bfloat16)
    d_sup = (d_shared * jax.nn.silu(shared_pre_gate)).astype(jnp.bfloat16)
    dh2_part = dot_single_float(d_sgate, full_sg.T) + dot_single_float(d_sup, full_su.T)
    grad_sdown = dot_single_float(shared_act.T, cotangent)
    grad_sgate = dot_single_float(normed_ffn.T, d_sgate)
    grad_sup = dot_single_float(normed_ffn.T, d_sup)
    cot_pairs = cotangent[token_of]
    d_output = (gate_values.reshape(-1)[:, None] * cot_pairs).astype(jnp.bfloat16)
    d_gate_part = jnp.einsum("td,tkd->tk", cotangent, pair_rows, preferred_element_type=jnp.float32)
    grad_send = (
        jnp.zeros((sharded_parts_count * expert_capacity, MODEL_WIDTH), jnp.bfloat16)
        .at[target]
        .set(d_output)
    )
    grad_arrived = lax.all_to_all(
        grad_send.reshape(sharded_parts_count, expert_capacity, MODEL_WIDTH),
        "fsdp",
        split_axis=0,
        concat_axis=0,
        tiled=True,
    )
    grad_flat = grad_arrived.reshape(-1, MODEL_WIDTH)
    flattened_gate = pre_gate.reshape(grad_flat.shape[0], -1)
    up_flat = up_projected.reshape(grad_flat.shape[0], -1)
    activ_flat = activ.reshape(grad_flat.shape[0], -1)
    flattened_rows = arrived.reshape(-1, MODEL_WIDTH)
    activation_gradient = dot_single_float(grad_flat, w_edown.T)
    expert_gate_gradient = (activation_gradient * up_flat * silu_grad(flattened_gate)).astype(
        jnp.bfloat16
    )
    expert_up_gradient = (activation_gradient * jax.nn.silu(flattened_gate)).astype(jnp.bfloat16)
    grad_edown = dot_single_float(activ_flat.T, grad_flat)
    grad_egate = dot_single_float(flattened_rows.T, expert_gate_gradient)
    expert_up_weight_gradient = dot_single_float(flattened_rows.T, expert_up_gradient)
    row_gradients = (
        dot_single_float(expert_gate_gradient, expert_gate_weight.T)
        + dot_single_float(expert_up_gradient, routed_up_weight.T)
    ).reshape(sharded_parts_count, expert_capacity, MODEL_WIDTH)
    d_back = lax.all_to_all(
        row_gradients.astype(jnp.bfloat16), "fsdp", split_axis=0, concat_axis=0, tiled=True
    ).astype(row_gradients.dtype)
    dh2_part = dh2_part + jnp.sum(
        d_back.reshape(sharded_parts_count * expert_capacity, MODEL_WIDTH)[target].reshape(
            seq_len, TOP, MODEL_WIDTH
        ),
        axis=1,
    )
    dh2_own, dgate_own = (
        lax.psum_scatter(
            dh2_part.astype(jnp.bfloat16), "tp", scatter_dimension=0, tiled=True
        ).astype(jnp.float32),
        lax.psum_scatter(
            d_gate_part.astype(jnp.bfloat16), "tp", scatter_dimension=0, tiled=True
        ).astype(jnp.float32),
    )
    own_routes = lax.dynamic_slice_in_dim(routes, tp_index * own_rows, own_rows, 0)
    own_chosen = lax.dynamic_slice_in_dim(chosen, tp_index * own_rows, own_rows, 0)
    own_sum = lax.dynamic_slice_in_dim(chosen_sum, tp_index * own_rows, own_rows, 0)
    d_chosen = ROUTE_SCALE * (
        dgate_own / own_sum
        - jnp.sum(dgate_own * own_chosen, axis=-1, keepdims=True) / (own_sum * own_sum)
    )
    d_select = d_chosen * own_chosen * (1.0 - own_chosen)
    expert_ids = jnp.arange(sharded_parts_count, dtype=jnp.int32)
    d_logits = jnp.sum(
        jnp.where(own_routes[..., None] == expert_ids, d_select[..., None], 0.0), axis=1
    ).astype(jnp.bfloat16)
    dh2_own = dh2_own + dot_single_float(d_logits, full_wr.T)
    grad_wr = dot_single_float(normed_own.T, d_logits)
    grad_g2 = jnp.sum(dh2_own * resid_normed, axis=0)
    d_resid = grad_own + norm_back(resid, factor_two, full_g2.astype(jnp.float32), dh2_own)
    d_attn = lax.all_gather(d_resid.astype(jnp.bfloat16), "tp", axis=0, tiled=True)
    grad_wo = dot_single_float(context.T, d_attn)
    d_context = (
        dot_single_float(d_attn, full_wo.T).astype(jnp.bfloat16).reshape(seq_len, heads_here, DV)
    )
    weights_f = jnp.exp(scores_of(query, keys, factor) - log_total)
    d_weights = jnp.einsum("qhd,khd->hqk", d_context, values, preferred_element_type=jnp.float32)
    d_scores = (
        weights_f * (d_weights - jnp.sum(weights_f * d_weights, axis=-1, keepdims=True))
    ).astype(jnp.bfloat16)
    d_query = (
        jnp.einsum("hqk,khd->qhd", d_scores, keys, preferred_element_type=jnp.float32) * factor
    )
    d_keys = (
        jnp.einsum("hqk,qhd->khd", d_scores, query, preferred_element_type=jnp.float32) * factor
    )
    d_values = jnp.einsum(
        "hqk,qhd->khd",
        weights_f.astype(jnp.bfloat16),
        d_context,
        preferred_element_type=jnp.float32,
    )
    d_qraw = jnp.concatenate(
        [d_query[..., :DN], unrotate(d_query[..., DN:], cos_table[:, None], sin_table[:, None])], -1
    )
    d_qraw = d_qraw.reshape(seq_len, heads_here * head_width).astype(jnp.bfloat16)
    d_kv = (
        jnp.concatenate([d_keys[..., :DN], d_values], -1)
        .reshape(seq_len, heads_here * (DN + DV))
        .astype(jnp.bfloat16)
    )
    d_krope = unrotate(jnp.sum(d_keys[..., DN:], axis=1), cos_table, sin_table)
    grad_wq = dot_single_float(normed_in.T, d_qraw)
    grad_wkvb = dot_single_float(latent_normed.T, d_kv)
    d_latent_normed = dot_single_float(d_kv, full_wkvb.T)
    gkv_f = full_gkv.astype(jnp.float32)
    grad_gkv = jnp.sum(d_latent_normed * latent * latent_factor, axis=0)
    d_latent = norm_back(latent, latent_factor, gkv_f, d_latent_normed)
    d_kvfirst = jnp.concatenate([d_latent, d_krope], -1)
    grad_wkva = dot_high(normed_in.astype(jnp.float32).T, d_kvfirst)
    dh1_part = dot_single_float(d_qraw, full_wq.T) + dot_high(
        d_kvfirst, full_wkva.astype(jnp.float32).T
    )
    grad_g1 = jnp.sum(dh1_part * x_normed, axis=0)
    dh1_own, sum_g1, sum_wkva, sum_gkv, sum_g2, sum_wr = (
        lax.psum_scatter(
            dh1_part.astype(jnp.bfloat16), "tp", scatter_dimension=0, tiled=True
        ).astype(jnp.float32),
        lax.psum_scatter(
            arrange(grad_g1).astype(jnp.bfloat16), "tp", scatter_dimension=0, tiled=True
        ).astype(jnp.float32),
        lax.psum_scatter(
            arrange(grad_wkva).astype(jnp.bfloat16), "tp", scatter_dimension=0, tiled=True
        ).astype(jnp.float32),
        lax.psum_scatter(
            arrange(grad_gkv).astype(jnp.bfloat16), "tp", scatter_dimension=0, tiled=True
        ).astype(jnp.float32),
        lax.psum_scatter(
            arrange(grad_g2).astype(jnp.bfloat16), "tp", scatter_dimension=0, tiled=True
        ).astype(jnp.float32),
        lax.psum_scatter(
            arrange(grad_wr).astype(jnp.bfloat16), "tp", scatter_dimension=0, tiled=True
        ).astype(jnp.float32),
    )
    g1_f = full_g1.astype(jnp.float32)
    grad_in = (d_resid + norm_back(x_own, inv_rms(x_own), g1_f, dh1_own)).astype(jnp.bfloat16)
    summed = (
        lax.psum_scatter(grad_wq, "fsdp", scatter_dimension=0, tiled=True),
        lax.psum_scatter(grad_wkvb, "fsdp", scatter_dimension=0, tiled=True),
        lax.psum_scatter(grad_wo, "fsdp", scatter_dimension=1, tiled=True),
        lax.psum_scatter(grad_sgate, "fsdp", scatter_dimension=0, tiled=True),
        lax.psum_scatter(grad_sup, "fsdp", scatter_dimension=0, tiled=True),
        lax.psum_scatter(grad_sdown, "fsdp", scatter_dimension=1, tiled=True),
        lax.psum_scatter(sum_g1, "fsdp", scatter_dimension=0, tiled=True),
        lax.psum_scatter(sum_wkva, "fsdp", scatter_dimension=0, tiled=True),
        lax.psum_scatter(sum_gkv, "fsdp", scatter_dimension=0, tiled=True),
        lax.psum_scatter(sum_g2, "fsdp", scatter_dimension=0, tiled=True),
        lax.psum_scatter(sum_wr, "fsdp", scatter_dimension=0, tiled=True),
    )
    (
        out_wq,
        out_wkvb,
        out_wo,
        out_sgate,
        out_sup,
        out_sdown,
        out_g1,
        out_wkva,
        out_gkv,
        out_g2,
        out_wr,
    ) = summed
    return (
        hidden_out,
        grad_in,
        out_g1,
        out_wq,
        out_wkva,
        out_gkv,
        out_wkvb,
        out_wo,
        out_g2,
        out_wr,
        out_sgate,
        out_sup,
        out_sdown,
        grad_egate[None],
        expert_up_weight_gradient[None],
        grad_edown[None],
    )


RINGS_16 = (
    (0, 1, 3, 2, 6, 7, 5, 9, 13, 12, 14, 15, 11, 10, 8, 4),
    (0, 1, 5, 4, 6, 10, 14, 15, 13, 12, 8, 9, 11, 7, 3, 2),
    (0, 2, 6, 7, 3, 1, 5, 9, 13, 15, 11, 10, 14, 12, 8, 4),
)
VMEM_BYTES = 60 * 2**20
BF16 = jnp.bfloat16
F32 = jnp.float32
SLOTS = 3


def ring_orders(n):
    return RINGS_16 if n == 16 else (tuple(range(n)),) * 3


def lookup(values, index):
    words = []
    for k in range(0, len(values), 8):
        word = sum(v << (4 * j) for j, v in enumerate(values[k : k + 8]))
        words.append(word - (1 << 32) if word >= 1 << 31 else word)
    word = jnp.int32(words[0])
    for k in range(1, len(words)):
        word = jnp.where(index >= 8 * k, jnp.int32(words[k]), word)
    return lax.shift_right_logical(word, 4 * (index & 7)) & 15


def remote(src, dst, send, recv, device):
    return pltpu.make_async_remote_copy(
        src_ref=src,
        dst_ref=dst,
        send_sem=send,
        recv_sem=recv,
        device_id=device,
        device_id_type=pl.DeviceIdType.MESH,
    )


class Place:
    def __init__(self, n):
        self.n, self.half = n, n // 2
        self.me, self.t = lax.axis_index("fsdp"), lax.axis_index("tp")
        self.orders = ring_orders(n)
        self.spot = [
            lookup([order.index(k) for k in range(n)], self.me) for order in self.orders
        ]
        self.near = [[self.owner(r, 1), self.owner(r, n - 1)] for r in range(len(self.orders))]
        self.twin = (self.me, 1 - self.t)

    def owner(self, ring, offset):
        return lookup(self.orders[ring], lax.rem(self.spot[ring] + offset + self.n, self.n))

    def next(self, ring, way):
        return (self.near[ring][way], self.t)

    def enter(self, everyone=False):
        barrier = pltpu.get_barrier_semaphore()
        if everyone:

            def greet(k, _):
                there = lax.rem(self.me + k, self.n)
                pl.semaphore_signal(
                    barrier, 1, device_id=(there, self.t), device_id_type=pl.DeviceIdType.MESH
                )
                return 0

            lax.fori_loop(1, self.n, greet, 0)
            count = self.n - 1
        else:
            count = 0
            for ring in range(len(self.orders)):
                for way in range(2):
                    pl.semaphore_signal(
                        barrier,
                        1,
                        device_id=self.next(ring, way),
                        device_id_type=pl.DeviceIdType.MESH,
                    )
                    count += 1
        pl.semaphore_signal(barrier, 1, device_id=self.twin, device_id_type=pl.DeviceIdType.MESH)
        pl.semaphore_wait(barrier, count + 1)


def gather_sems(n):
    return pltpu.SemaphoreType.DMA((4, 2, n // 2 + 1))


class Gather:
    def __init__(self, place, ring, rows, source, target, sems, shared):
        self.place, self.ring, self.rows = place, ring, rows
        self.source, self.target, self.sems, self.shared = source, target, sems, shared

    def part(self, way, last):
        if not last:
            return 0, self.rows
        half = self.rows // 2
        return (0, half) if way == 0 else (half, self.rows - half)

    def offset(self, way, s):
        return -s if way == 0 else s

    def hop(self, way, s, last=False, first=False, owner=None):
        lo, rows = self.part(way, last)
        place = self.place
        if owner is None:
            owner = place.owner(self.ring, self.offset(way, s - 1))
        there = self.target(owner, lo, rows, place.t)
        here = self.source(lo, rows) if first else there
        return remote(
            here, there, self.sems.at[0, way, s], self.sems.at[1, way, s], place.next(self.ring, way)
        )

    def landed(self, way, s, last=False, owner=None):
        lo, rows = self.part(way, last)
        place = self.place
        if owner is None:
            owner = place.owner(self.ring, self.offset(way, s))
        there = self.target(owner, lo, rows, place.t)
        return remote(
            there, there, self.sems.at[0, way, s], self.sems.at[1, way, s], place.next(self.ring, way)
        )

    def across(self, way, s, t, last=False, first=False, owner=None):
        lo, rows = (0, self.rows) if first else self.part(way, last)
        place = self.place
        if owner is None:
            owner = place.me if first else place.owner(self.ring, self.offset(way, s))
        there = self.target(owner, lo, rows, t)
        here = self.source(lo, rows) if first else there
        return remote(here, there, self.sems.at[2, way, s], self.sems.at[3, way, s], place.twin)

    def own(self):
        return pltpu.make_async_copy(
            self.source(0, self.rows),
            self.target(self.place.me, 0, self.rows, self.place.t),
            self.sems.at[0, 0, 0],
        )

    def begin(self):
        for way in range(2):
            self.hop(way, 1, first=True).start()
        self.own().start()
        if self.shared:
            self.across(0, 0, self.place.t, first=True).start()

    def step(self, s, final=False):
        for way in range(2):
            owner = self.place.owner(self.ring, self.offset(way, s))
            self.landed(way, s, owner=owner).wait_recv()
            self.hop(way, s + 1, last=final, owner=owner).start()
            if self.shared:
                self.across(way, s, self.place.t, owner=owner).start()

    def close(self):
        half = self.place.half
        for way in range(2):
            self.landed(way, half, last=True).wait_recv()
            if self.shared:
                self.across(way, half, self.place.t, last=True).start()

    def settle(self):
        half = self.place.half
        self.own().wait()
        t = self.place.t
        if self.shared:
            self.across(0, 0, t, first=True).wait_send()
            self.across(0, 0, 1 - t, first=True).wait_recv()

        def each(s, _):
            for way in range(2):
                self.hop(way, s).wait_send()
                if self.shared:
                    self.across(way, s, t).wait_send()
                    self.across(way, s, 1 - t).wait_recv()
            return 0

        lax.fori_loop(1, half, each, 0)
        for way in range(2):
            self.hop(way, half, last=True).wait_send()
            if self.shared:
                self.across(way, half, t, last=True).wait_send()
                self.across(way, half, 1 - t, last=True).wait_recv()


def pump_gathers(gathers, half, s):
    if isinstance(s, int):
        s = jnp.int32(s)

    @pl.when(s < half - 1)
    def _():
        for g in gathers:
            g.step(s)

    @pl.when(s == half - 1)
    def _():
        for g in gathers:
            g.step(half - 1, final=True)

    @pl.when(s == half)
    def _():
        for g in gathers:
            g.close()


def pump_all(place, gathers, beside=()):
    for s, work in enumerate(beside):
        pump_gathers(gathers, place.half, s + 1)
        work()

    def each(s, _):
        for g in gathers:
            g.step(s)
        return 0

    lax.fori_loop(1 + len(beside), place.half - 1, each, 0)
    for g in gathers:
        g.step(place.half - 1, final=True)
    for g in gathers:
        g.close()


class Share:
    def __init__(self, place, own, pair, rows, mine, heap, sems, arrived):
        self.place, self.own, self.pair, self.rows = place, own, pair, rows
        self.mine, self.heap, self.sems, self.arrived = mine, heap, sems, arrived

    def keep(self, i, k):
        slot, own = lax.rem(i, 2), self.own
        return pltpu.make_async_copy(
            self.rows.at[slot, k, pl.ds(self.place.t * own, own)],
            self.mine.at[i * self.pair + k],
            self.sems.at[0, slot, k],
        )

    def give(self, i, k):
        slot, own, s = lax.rem(i, 2), self.own, i * self.pair + k
        return remote(
            self.rows.at[slot, k, pl.ds((1 - self.place.t) * own, own)],
            self.heap.at[s],
            self.sems.at[1, slot, k],
            self.arrived.at[s],
            self.place.twin,
        )

    def start(self, i):
        for k in range(self.pair):
            self.give(i, k).start()
            self.keep(i, k).start()

    def left(self, i):
        for k in range(self.pair):
            self.keep(i, k).wait()
            self.give(i, k).wait_send()

    def settle(self, steps):
        self.left(steps - 2)
        self.left(steps - 1)

        def each(i, _):
            for k in range(self.pair):
                self.give(i, k).wait_recv()
            return 0

        lax.fori_loop(0, steps, each, 0)


def share_scratch(n, pair, seq, width):
    return [
        pltpu.VMEM((2, pair, seq, width), BF16),
        pltpu.SemaphoreType.DMA((2, 2, pair)),
        pltpu.SemaphoreType.DMA((n,)),
    ]


class Bring:
    def __init__(self, pairs, sems):
        self.copies = [
            pltpu.make_async_copy(src, dst, sems.at[k]) for k, (src, dst) in enumerate(pairs)
        ]

    def begin(self):
        for copy in self.copies:
            copy.start()

    def wait(self):
        for copy in self.copies:
            copy.wait()


def room_for(arrays):
    return [pltpu.VMEM(a.shape, a.dtype) for a in arrays] + [
        pltpu.SemaphoreType.DMA((len(arrays),))
    ]


def scatter_scratch(n, rows, cols):
    return [
        pltpu.SemaphoreType.DMA((2, 2, n // 2 + 1)),
        pltpu.SemaphoreType.DMA((2, 2, n // 2 + 1)),
        pltpu.SemaphoreType.DMA((2, n)),
        pltpu.VMEM((2, SLOTS, rows, cols), BF16),
        pltpu.VMEM((2, SLOTS, rows, cols), BF16),
        pltpu.VMEM((2, n // 2, rows, cols), BF16),
    ]


def add_rows(target, sources, lo, rows, cols):
    most = max(16, (32768 // cols) // 16 * 16)
    size = min(most, rows)
    while rows % size:
        size -= 16

    def each(i, _):
        at = pl.ds(pl.multiple_of(lo + i * size, 16), size)
        total = sources[0][at, :].astype(F32)
        for source in sources[1:]:
            total = total + source[at, :].astype(F32)
        target[at, :] = total.astype(target.dtype)
        return 0

    lax.fori_loop(0, rows // size, each, 0)


class Scatter:
    def __init__(self, place, ring, shape, source, scratch, heap=None, given=False):
        self.place, self.ring, self.source, self.heap = place, ring, source, heap
        self.giving = heap is not None and not given
        self.rows, self.cols = shape
        self.sems, self.load_sems, self.give_sems, self.term, self.other, self.land = scratch

    def owner(self, way, s):
        half = self.place.half
        return self.place.owner(self.ring, half - s if way == 0 else half + s)

    def loads(self, way, s):
        slot = lax.rem(s, SLOTS)
        owner = self.owner(way, s)
        out = [
            pltpu.make_async_copy(
                self.source(owner, self.place.t),
                self.term.at[way, slot],
                self.load_sems.at[0, way, s],
            )
        ]
        if self.heap is not None:
            out.append(
                pltpu.make_async_copy(
                    self.heap(owner), self.other.at[way, slot], self.load_sems.at[1, way, s]
                )
            )
        return out

    def give(self, owner):
        return remote(
            self.source(owner, 1 - self.place.t),
            self.heap(owner),
            self.give_sems.at[0, owner],
            self.give_sems.at[1, owner],
            self.place.twin,
        )

    def push(self, s):
        if self.giving:
            for way in range(2):

                @pl.when((s <= self.place.half) if way == 0 else ((s > 0) & (s < self.place.half)))
                def _(way=way):
                    self.give(self.owner(way, s)).start()

    def fetch(self, s, ways=(0, 1), fresh=True):
        for way in ways:
            if self.giving and fresh:
                self.give(self.owner(way, s)).wait_recv()
            for copy in self.loads(way, s):
                copy.start()

    def part(self, way, first):
        if not first:
            return 0, self.rows
        half = self.rows // 2
        return (0, half) if way == 0 else (half, self.rows - half)

    def hop(self, way, s, first=False):
        lo, rows = self.part(way, first)
        at = pl.ds(lo, rows)
        return remote(
            self.term.at[way, lax.rem(s - 1, SLOTS), at, :],
            self.land.at[way, s - 1, at, :],
            self.sems.at[0, way, s],
            self.sems.at[1, way, s],
            self.place.next(self.ring, way),
        )

    def sources(self, way, s, *more):
        slot = lax.rem(s, SLOTS)
        out = [self.term.at[way, slot]]
        if self.heap is not None:
            out.append(self.other.at[way, slot])
        return out + list(more)

    def begin(self):
        if self.giving:
            self.push(0)
            self.push(1)
        self.fetch(0, ways=(0,))
        self.fetch(0, ways=(1,), fresh=False)

    def open(self):
        for way in range(2):
            for copy in self.loads(way, 0):
                copy.wait()
            if self.heap is not None:
                lo, rows = self.part(way, True)
                add_rows(self.term.at[way, 0], self.sources(way, 0), lo, rows, self.cols)
            self.hop(way, 1, first=True).start()

    def follow(self):
        if self.giving:

            def each(s, _):
                self.push(s)
                return 0

            lax.fori_loop(2, self.place.half + 1, each, 0)
        self.fetch(1)

    def step(self, s, first=False, second=False, final=False):
        for way in range(2):
            for copy in self.loads(way, s):
                copy.wait()
            self.hop(way, s, first=first).wait_recv()
            lo, rows = self.part(way, first)
            target = self.term.at[way, lax.rem(s, SLOTS)]
            landed = self.land.at[way, s - 1]
            add_rows(target, self.sources(way, s, landed), lo, rows, self.cols)
            if first and self.heap is not None:
                lo, rows = self.part(1 - way, first)
                add_rows(target, self.sources(way, s), lo, rows, self.cols)
            self.hop(way, s + 1).start()
        for way in range(2):
            if not first:
                self.hop(way, s - 1, first=second).wait_send()
            if not final or way == 0:
                self.fetch(s + 1, ways=(way,))

    def middle(self, s):
        half = self.place.half

        @pl.when(s == 2)
        def _():
            self.step(s, second=True)

        @pl.when((s > 2) & (s < half - 1))
        def _():
            self.step(s)

        @pl.when(s == half - 1)
        def _():
            self.step(s, final=True)

    def close(self, out):
        half = self.place.half
        for copy in self.loads(0, half):
            copy.wait()
        for way in range(2):
            self.hop(way, half).wait_recv()
        last = [self.land.at[way, half - 1] for way in range(2)]
        add_rows(out, self.sources(0, half, *last), 0, self.rows, self.cols)
        for way in range(2):
            self.hop(way, half - 1).wait_send()
            self.hop(way, half).wait_send()
        if self.giving:

            def given(k, _):
                self.give(k).wait_send()
                return 0

            lax.fori_loop(0, self.place.n, given, 0)


def open_scatters(scatters):
    for s in scatters:
        s.begin()
    for s in scatters:
        s.open()
    for s in scatters:
        s.follow()


def step_scatters(place, scatters, s):
    if isinstance(s, int):
        s = jnp.int32(s)

    @pl.when(s == 1)
    def _():
        for one in scatters:
            one.step(1, first=True)

    @pl.when((s > 1) & (s < place.half))
    def _():
        for one in scatters:
            one.middle(s)


def run_scatters(place, scatters, outs, beside=()):
    open_scatters(scatters)
    for s, work in enumerate(beside):
        step_scatters(place, scatters, s + 1)
        work()

    def each(s, _):
        step_scatters(place, scatters, s)
        return 0

    lax.fori_loop(1 + len(beside), place.half, each, 0)
    for s, out in zip(scatters, outs):
        s.close(out)


class Trade:
    def __init__(self, place, sources, targets, sems):
        self.place, self.sources, self.targets, self.sems = place, sources, targets, sems

    def copies(self, k, coming=False):
        place = self.place
        there = lax.rem(place.me + k, place.n)
        back = lax.rem(place.me + place.n - k, place.n)
        return [
            remote(
                source(there),
                target(back if coming else place.me),
                self.sems.at[0, k, j],
                self.sems.at[1, k, j],
                (there, place.t),
            )
            for j, (source, target) in enumerate(zip(self.sources, self.targets))
        ]

    def own(self):
        me = self.place.me
        return [
            pltpu.make_async_copy(source(me), target(me), self.sems.at[0, 0, j])
            for j, (source, target) in enumerate(zip(self.sources, self.targets))
        ]

    def begin(self):
        def each(k, _):
            for copy in self.copies(k):
                copy.start()
            return 0

        lax.fori_loop(1, self.place.n, each, 0)
        for copy in self.own():
            copy.start()

    def settle(self):
        def each(k, _):
            for copy in self.copies(k):
                copy.wait_send()
            for copy in self.copies(k, coming=True):
                copy.wait_recv()
            return 0

        lax.fori_loop(1, self.place.n, each, 0)
        for copy in self.own():
            copy.wait()


def comm_call(kernel, out_shape, out_specs, in_specs, scratch, ident, name):
    return pl.pallas_call(
        kernel,
        out_shape=out_shape,
        in_specs=in_specs,
        out_specs=out_specs,
        scratch_shapes=scratch,
        compiler_params=pltpu.CompilerParams(
            collective_id=ident, has_side_effects=True, vmem_limit_bytes=VMEM_BYTES
        ),
        name=name,
    )


IN_HBM = pl.BlockSpec(memory_space=pl.ANY)
IN_VMEM = pl.BlockSpec(memory_space=pltpu.VMEM)


def thirds(width):
    tiles = width // 128
    cuts = [0, tiles // 3, 2 * tiles // 3, tiles]
    return [(128 * lo, 128 * (hi - lo)) for lo, hi in zip(cuts, cuts[1:])]


def pick(flat):
    flat = list(flat)

    def take(count):
        head, flat[:] = flat[:count], flat[count:]
        return head

    return take


def dot_tn(left, right):
    return lax.dot_general(left, right, (((0,), (0,)), ((), ())), preferred_element_type=F32)


def dot_nt(left, right):
    return lax.dot_general(left, right, (((1,), (1,)), ((), ())), preferred_element_type=F32)


def whole(array):
    zeros = (0,) * array.ndim
    return pl.BlockSpec(array.shape, lambda i: zeros, pipeline_mode=pl.Buffered(1))


def by_cols(rows, cols):
    return pl.BlockSpec((rows, cols), lambda i: (0, i))


def by_rows(rows, cols):
    return pl.BlockSpec((rows, cols), lambda i: (i, 0))


def by_seq(*block):
    rest = (0,) * (len(block) - 1)
    return pl.BlockSpec(block, lambda i: (i,) + rest)


def eye(size):
    same = lax.broadcasted_iota(jnp.int32, (size, size), 0) == lax.broadcasted_iota(
        jnp.int32, (size, size), 1
    )
    return same.astype(F32).astype(BF16)


def sds(shape, dtype):
    return jax.ShapeDtypeStruct(shape, dtype)


def grid_call(kernel, steps, in_specs, out, scratch, ident, name):
    return pl.pallas_call(
        kernel,
        grid=(steps,),
        in_specs=in_specs,
        out_specs=tuple(spec for spec, _, _ in out),
        out_shape=tuple(sds(shape, dtype) for _, shape, dtype in out),
        scratch_shapes=scratch,
        compiler_params=pltpu.CompilerParams(
            collective_id=ident, has_side_effects=True, vmem_limit_bytes=63 * 2**20
        ),
        name=name,
    )


GAIN_ATTN, GAIN_FFN, GAIN_KV, TABLES = 16, 17, 18, 32


def row_gathers(place, chunks, sems, source, target, own):
    t = place.t
    return [
        Gather(
            place, ring, rows,
            lambda lo, r, b=b, c0=c0, w=w: source(pl.ds(b + lo, r), pl.ds(c0, w)),
            lambda o, lo, r, u, b=b, c0=c0, w=w: target(
                o, pl.ds(u * own + b + lo, r), pl.ds(c0, w)
            ),
            sems[k], True,
        )
        for k, (ring, b, rows, c0, w) in enumerate(chunks)
    ]


def row_scatters(place, chunks, scratch, mine, heap):
    return [
        Scatter(
            place, ring, (rows, w),
            lambda o, u, c0=c0, w=w: mine.at[o, :, pl.ds(c0, w)],
            scratch[k],
            lambda o, c0=c0, w=w: heap.at[o, :, pl.ds(c0, w)],
            given=True,
        )
        for k, (ring, _, rows, c0, w) in enumerate(chunks)
    ]


def row_cuts(rows, width):
    return [(ring, 0, rows, c0, w) for ring, (c0, w) in enumerate(thirds(width))]


def collect_inputs(
    n, query, kvd, kvu, outp, x, norm_attn, norm_ffn, kv_norm, router, routes, s_gate, s_up, s_down
):
    own, width = x.shape
    seq = 2 * own
    q_rows, q_cols = query.shape
    cut = q_cols // 4 * 3
    d_rows, cols = kvd.shape[0] // 2, kvd.shape[1]
    o_rows = outp.shape[0]
    u_rows = kvu.shape[0]
    hidden = s_down.shape[0] // n
    padded = -(-hidden // 16) * 16
    small_rows = TABLES + 2 * n

    def kernel(*refs):
        take = pick(refs)
        q, kd, ku, wo, xin, na, nf, nk, ro, rt, sg, su, sd = take(13)
        q_all, kd_all, ku_all, wo_all, sm_all, x_all, blocks = take(7)
        sems = take(6)
        x_sems, sm, turned = take(3)
        place = Place(n)
        t = place.t
        place.enter()

        def of_q(ring, c0, w):
            return Gather(
                place, ring, q_rows,
                lambda lo, r: q.at[pl.ds(lo, r), pl.ds(c0, w)],
                lambda o, lo, r, _: q_all.at[pl.ds(o * q_rows + lo, r), pl.ds(c0, w)],
                sems[ring], False,
            )

        gathers = [
            of_q(0, 0, cut),
            of_q(1, cut, q_cols - cut),
            Gather(
                place, 2, o_rows,
                lambda lo, r: wo.at[pl.ds(lo, r)],
                lambda o, lo, r, _: wo_all.at[pl.ds(lo, r), pl.ds(o * cols, cols)],
                sems[5], False,
            ),
            Gather(
                place, 1, u_rows,
                lambda lo, r: ku.at[pl.ds(lo, r)],
                lambda o, lo, r, _: ku_all.at[pl.ds(o * u_rows + lo, r)],
                sems[2], False,
            ),
            Gather(
                place, 1, d_rows,
                lambda lo, r: kd.at[pl.ds(t * d_rows + lo, r)],
                lambda o, lo, r, u: kd_all.at[pl.ds(u * d_rows + lo, r), pl.ds(o * cols, cols)],
                sems[3], True,
            ),
            Gather(
                place, 2, small_rows,
                lambda lo, r: sm.at[pl.ds(lo, r)],
                lambda o, lo, r, _: sm_all.at[o, pl.ds(lo, r)],
                sems[4], False,
            ),
        ]
        for g in gathers[:-1]:
            g.begin()
        mine = x_all.at[pl.ds(t * own, own)]
        x_own = pltpu.make_async_copy(xin, mine, x_sems.at[0])
        x_give = remote(xin, mine, x_sems.at[1], x_sems.at[2], place.twin)
        theirs = x_all.at[pl.ds((1 - t) * own, own)]
        x_take = remote(xin, theirs, x_sems.at[1], x_sems.at[2], place.twin)
        x_own.start()
        x_give.start()

        sm[...] = jnp.zeros_like(sm)
        sm[0:n, :] = ro[...]
        gains = jnp.concatenate(
            [
                na[...].astype(F32),
                nf[...].astype(F32),
                nk[...].astype(F32),
                jnp.zeros((TABLES - GAIN_KV - 1, cols), F32),
            ],
            0,
        )
        sm[GAIN_ATTN:TABLES, :] = gains.astype(BF16)
        ids = lax.broadcasted_iota(jnp.int32, (n, seq), 0)
        chosen = jnp.zeros((n, seq), F32)
        for k in range(TOP):
            chosen = jnp.where(ids == rt[k : k + 1, :], 1.0, chosen)
        table = chosen.astype(BF16)
        sm[TABLES : TABLES + n, :] = table[:, :own]
        sm[TABLES + n : TABLES + 2 * n, :] = table[:, own:]
        gathers[-1].begin()

        def cut_slices(j, w):
            if j < 2:
                turned[...] = dot_tn(w[...], eye(cols))
            else:
                turned[...] = w[...].astype(F32)
            for k in range(n):
                blocks[k, j, 0:hidden, :] = turned[k * hidden : (k + 1) * hidden, :].astype(BF16)
                if padded > hidden:
                    blocks[k, j, hidden:padded, :] = jnp.zeros((padded - hidden, cols), BF16)

        beside = [lambda j=j, w=w: cut_slices(j, w) for j, w in enumerate((sg, su, sd))]
        pump_all(place, gathers, beside)
        x_own.wait()
        x_give.wait_send()
        x_take.wait_recv()
        for g in gathers:
            g.settle()

    return comm_call(
        kernel,
        (
            sds((n * q_rows, q_cols), BF16),
            sds((kvd.shape[0], n * cols), BF16),
            sds((n * u_rows, kvu.shape[1]), BF16),
            sds((o_rows, n * cols), BF16),
            sds((n, small_rows, cols), BF16),
            sds((seq, width), BF16),
            sds((n, 3, padded, cols), BF16),
        ),
        (IN_HBM,) * 6 + (IN_VMEM,),
        [IN_HBM] * 5 + [IN_VMEM] * 8,
        [gather_sems(n)] * 6
        + [
            pltpu.SemaphoreType.DMA((3,)),
            pltpu.VMEM((small_rows, cols), BF16),
            pltpu.VMEM((n * hidden, cols), F32),
        ],
        1,
        "collect_inputs",
    )(query, kvd, kvu, outp, x, norm_attn, norm_ffn, kv_norm, router, routes, s_gate, s_up, s_down)


def swapped(v):
    half_width = v.shape[1] // 2
    return jnp.concatenate([v[:, half_width:], v[:, :half_width]], 1)


def causal_weights(q_n, q_r, k_n, k_r, factor):
    raw = (dot_nt(q_n, k_n) + dot_nt(q_r, k_r)) * factor
    length = raw.shape[0]
    ahead = lax.broadcasted_iota(jnp.int32, (length, length), 0) >= lax.broadcasted_iota(
        jnp.int32, (length, length), 1
    )
    raw = jnp.where(ahead, raw, -1e30)
    top = jnp.max(raw, axis=1, keepdims=True)
    up = jnp.exp(raw - top)
    return up / jnp.sum(up, axis=1, keepdims=True)


def attend(n, x_seq, x_own, small_all, w_kvd, cos2, sin2, w_q, w_kvu, w_out, blocks):
    seq, width = x_seq.shape
    own = seq // 2
    head = DN + DR
    pairs = w_q.shape[1] // (2 * head)
    factor = 1.0 / math.sqrt(head)
    cols = width // n
    padded = blocks.shape[2]
    kv_cols = KVR // n
    part_rows = 128

    def kernel(*refs):
        take = pick(refs)
        x, xo, sm, wd, co, si, wq, wu, wo, bl = take(10)
        resid, sel_out, g2, wr, h_own, gates, h1, g1, gk, lat, cn, kpe, sw, qn, qr, kv, ctx = take(17)
        trade_sems, got, part, theirs, swap_sems = take(5)
        place = Place(n)
        t, me = place.t, place.me
        i = pl.program_id(0)
        trade = Trade(place, [lambda k: bl.at[k]], [lambda k: got.at[k]], trade_sems)

        @pl.when(i == 0)
        def _():
            place.enter(everyone=True)
            trade.begin()
            for o in range(n):
                at = slice(o * cols, (o + 1) * cols)
                g1[:, at] = sm[o, GAIN_ATTN : GAIN_ATTN + 1, :].astype(F32)
                g2[:, at] = sm[o, GAIN_FFN : GAIN_FFN + 1, :].astype(F32)
                wr[:, at] = sm[o, 0:n, :]
                gk[:, o * kv_cols : (o + 1) * kv_cols] = sm[
                    o, GAIN_KV : GAIN_KV + 1, 0:kv_cols
                ].astype(F32)
            size = 16

            def norm_rows(j, _):
                at = pl.ds(pl.multiple_of(j * size, size), size)
                v = x[at, :].astype(F32)
                h1[at, :] = (v * inv_rms(v) * g1[...]).astype(BF16)
                return 0

            lax.fori_loop(0, seq // size, norm_rows, 0)
            first = dot_nt(h1[...], wd[...])
            latent = first[:, :KVR]
            lat[...] = latent
            cn[...] = (latent * inv_rms(latent) * gk[...]).astype(BF16)
            rope = first[:, KVR:]
            kpe[...] = (rope * co[...] + swapped(rope) * si[...]).astype(BF16)

        q_raw = dot_single_float(h1[...], wq[...])
        kv[...] = dot_single_float(cn[...], wu[...]).astype(BF16)
        for k in range(2):
            q_n = q_raw[:, k * head : k * head + DN].astype(BF16)
            rope = q_raw[:, k * head + DN : (k + 1) * head]
            q_r = (rope * co[...] + swapped(rope) * si[...]).astype(BF16)
            qn[:, k * DN : (k + 1) * DN] = q_n
            qr[:, k * DR : (k + 1) * DR] = q_r
            base = k * (DN + DV)
            weights = causal_weights(q_n, q_r, kv[:, base : base + DN], kpe[...], factor)
            one = dot_single_float(weights.astype(BF16), kv[:, base + DN : base + DN + DV])
            ctx[:, k * DV : (k + 1) * DV] = one.astype(BF16)
        more = dot_single_float(ctx[...], wo[...])

        @pl.when(i == 0)
        def _():
            part[...] = more

        @pl.when(i > 0)
        def _():
            part[...] += more

        @pl.when(i == pairs - 1)
        def _():
            swap = remote(
                part.at[pl.ds((1 - t) * own, own)],
                theirs,
                swap_sems.at[0],
                swap_sems.at[1],
                place.twin,
            )
            swap.start()
            swap.wait_recv()
            size = 16

            def norm_rows(j, _):
                at = pl.ds(pl.multiple_of(j * size, size), size)
                mine = pl.ds(pl.multiple_of(t * own + j * size, size), size)
                v = xo[at, :].astype(F32) + (part[mine, :] + theirs[at, :])
                resid[at, :] = v
                h_own[at, :] = (v * inv_rms(v) * g2[...]).astype(BF16)
                return 0

            lax.fori_loop(0, own // size, norm_rows, 0)
            logits = dot_nt(wr[...], h_own[...])
            chosen = sm[me, pl.ds(pl.multiple_of(TABLES + t * n, 16), n), :].astype(F32)
            sel = jnp.where(chosen > 0.5, 1.0 / (1.0 + jnp.exp(-logits)), 0.0)
            sel_out[...] = sel
            gate = ROUTE_SCALE * sel / jnp.sum(sel, axis=0, keepdims=True)
            high = gate.astype(BF16)
            gates[0:n, :] = high
            gates[n : 2 * n, :] = (gate - high.astype(F32)).astype(BF16)
            swap.wait_send()
            trade.settle()
            sw[...] = jnp.zeros_like(sw)
            for o in range(n):
                for j in range(3):
                    sw[j * part_rows : j * part_rows + padded, o * cols : (o + 1) * cols] = got[o, j]

    heads = 2 * pairs
    return grid_call(
        kernel,
        pairs,
        [whole(a) for a in (x_seq, x_own, small_all, w_kvd, cos2, sin2)]
        + [by_cols(width, 2 * head), by_cols(KVR, 2 * (DN + DV)), by_rows(2 * DV, width), IN_HBM],
        (
            (IN_VMEM, (own, width), F32),
            (IN_VMEM, (n, own), F32),
            (IN_VMEM, (1, width), F32),
            (IN_VMEM, (n, width), BF16),
            (IN_VMEM, (own, width), BF16),
            (IN_VMEM, (2 * n, own), BF16),
            (IN_VMEM, (seq, width), BF16),
            (IN_VMEM, (1, width), F32),
            (IN_VMEM, (1, KVR), F32),
            (IN_VMEM, (seq, KVR), F32),
            (IN_VMEM, (seq, KVR), BF16),
            (IN_VMEM, (seq, DR), BF16),
            (IN_VMEM, (3 * part_rows, width), BF16),
            (by_cols(seq, 2 * DN), (seq, heads * DN), BF16),
            (by_cols(seq, 2 * DR), (seq, heads * DR), BF16),
            (by_cols(seq, 2 * (DN + DV)), (seq, heads * (DN + DV)), BF16),
            (by_cols(seq, 2 * DV), (seq, heads * DV), BF16),
        ),
        [
            pltpu.SemaphoreType.DMA((2, n, 1)),
            pltpu.VMEM(blocks.shape, BF16),
            pltpu.VMEM((seq, width), F32),
            pltpu.VMEM((own, width), F32),
            pltpu.SemaphoreType.DMA((2,)),
        ],
        2,
        "attend",
    )(x_seq, x_own, small_all, w_kvd, cos2, sin2, w_q, w_kvu, w_out, blocks)


def spread_rows(n, h_own, gates, small_all, cap):
    own, width = h_own.shape
    seq = 2 * own
    chunks = row_cuts(own, width)

    def kernel(*refs):
        take = pick(refs)
        h, ga, sm = take(3)
        table, h_all, gate_all = take(3)
        (named,) = take(1)
        sems = take(1 + len(chunks))
        place = Place(n)
        me = place.me
        place.enter()
        gathers = row_gathers(
            place, chunks, sems,
            lambda r, c: h.at[r, c], lambda o, r, c: h_all.at[o, r, c], own,
        )
        gathers.append(
            Gather(
                place, 0, 2 * n,
                lambda lo, r: ga.at[pl.ds(lo, r)],
                lambda o, lo, r, u: gate_all.at[o, u, pl.ds(lo, r)],
                sems[len(chunks)], True,
            )
        )
        for one in gathers:
            one.begin()

        mine = lax.broadcasted_iota(jnp.int32, (n, own), 0) == me
        for s in range(n):
            for u in range(2):
                one = sm[s, TABLES + u * n : TABLES + (u + 1) * n, :].astype(F32)
                one = jnp.sum(jnp.where(mine, one, 0.0), axis=0, keepdims=True)
                named[s : s + 1, u * own : (u + 1) * own] = one
        below = lax.broadcasted_iota(jnp.int32, (seq, seq), 0) <= lax.broadcasted_iota(
            jnp.int32, (seq, seq), 1
        )
        count = dot_single_float(named[...].astype(BF16), below.astype(F32).astype(BF16)) - 1.0
        slots = lax.broadcasted_iota(jnp.int32, (cap, seq), 0).astype(F32)

        def fill(first, last):
            for s in range(first, last):
                here = (count[s : s + 1, :] == slots) & (named[s : s + 1, :] > 0.5)
                table[s] = here.astype(F32).astype(BF16)

        quarter = n // 4
        beside = [
            lambda k=k: fill(k * quarter, (k + 1) * quarter if k < 3 else n) for k in range(4)
        ]
        pump_all(place, gathers, beside)
        for one in gathers:
            one.settle()

    return comm_call(
        kernel,
        (
            sds((n, cap, seq), BF16),
            sds((n, seq, width), BF16),
            sds((n, 2, 2 * n, own), BF16),
        ),
        (IN_VMEM, IN_HBM, IN_HBM),
        [IN_HBM, IN_HBM, IN_VMEM],
        [pltpu.VMEM((n, seq), F32)] + [gather_sems(n)] * (1 + len(chunks)),
        3,
        "spread_rows",
    )(h_own, gates, small_all)


PAIR = 2


def expert_forward(h_all, place_table, gates_all, w_gate, w_up, w_down, shared_w, cot):
    n, seq, width = h_all.shape
    own = seq // 2
    cap, hidden, part = place_table.shape[1], w_gate.shape[0], shared_w.shape[0] // 3
    steps = n // PAIR
    chunks = row_cuts(own, width)

    def kernel(*refs):
        take = pick(refs)
        h, pm, ga, *far, ct = take(8)
        rows, act, act_gate, on_up, on_gate, s_act, s_on, gate, out_mine, out_heap, ct_all = take(11)
        sems = take(len(chunks))
        orows, *near, bring_sems = take(6)
        out_rows, share_sems, arrived = take(3)
        wg, wu, wd, sw = near
        place = Place(n)
        t, me = place.t, place.me
        i = pl.program_id(0)
        gathers = row_gathers(
            place, chunks, sems,
            lambda r, c: ct.at[pl.ds(t * own + r.start, r.size), c],
            lambda o, r, c: ct_all.at[o, r, c], own,
        )

        bring = Bring(list(zip(far, near)), bring_sems)
        share = Share(place, own, PAIR, out_rows, out_mine, out_heap, share_sems, arrived)

        @pl.when(i == 0)
        def _():
            place.enter()
            for one in gathers:
                one.begin()
            bring.begin()

        @pl.when(i > 1)
        def _():
            share.left(i - 2)

        @pl.when(i > 0)
        def _():
            pump_gathers(gathers, place.half, i)

        slots = []
        line = lax.broadcasted_iota(jnp.int32, (2 * n, own), 0)
        mine = (line == me) | (line == me + n)
        for k in range(PAIR):
            halves = [
                jnp.sum(jnp.where(mine, ga[k, u].astype(F32), 0.0), axis=0, keepdims=True)
                for u in range(2)
            ]
            gate[k] = jnp.concatenate(halves, 1)
            rows[pl.ds(k * cap, cap), :] = dot_single_float(pm[k], h[k]).astype(BF16)
            slots.append(jnp.sum(pm[k].astype(F32) * gate[k], axis=1, keepdims=True))
        pl.when(i == 0)(bring.wait)
        pre = dot_nt(rows[...], wg[...])
        up = dot_nt(rows[...], wu[...])
        sigm = jax.nn.sigmoid(pre)
        silu = pre * sigm
        gs = jnp.concatenate(slots, 0)
        plain = silu * up
        act[...] = plain.astype(BF16)
        act_gate[...] = (plain * gs).astype(BF16)
        on_up[...] = silu.astype(BF16)
        on_gate[...] = (up * (sigm * (1.0 + pre * (1.0 - sigm)))).astype(BF16)
        orows[...] = dot_single_float(act_gate[...], wd[...]).astype(BF16)
        for k in range(PAIR):
            at = pl.ds(k * seq, seq)
            both = dot_nt(h[k], sw[0 : 2 * part, :])
            s_pre, s_up = both[:, :part], both[:, part:]
            sigm = jax.nn.sigmoid(s_pre)
            silu = s_pre * sigm
            s_act[at, :] = (silu * s_up).astype(BF16)
            s_on[at, 0:part] = (s_up * (sigm * (1.0 + s_pre * (1.0 - sigm)))).astype(BF16)
            s_on[at, part:] = silu.astype(BF16)
            out_rows[lax.rem(i, 2), k] = (
                dot_tn(pm[k], orows[pl.ds(k * cap, cap), :])
                + dot_single_float(s_act[at, :], sw[2 * part :, :])
            ).astype(BF16)
        share.start(i)

        @pl.when(i == steps - 1)
        def _():
            for one in gathers:
                one.close()
            for one in gathers:
                one.settle()
            share.settle(steps)

    return grid_call(
        kernel,
        steps,
        [by_seq(PAIR, seq, width), by_seq(PAIR, cap, seq), by_seq(PAIR, 2, 2 * n, own)]
        + [IN_HBM] * 5,
        (
            (by_rows(PAIR * cap, width), (n * cap, width), BF16),
            (by_rows(PAIR * cap, hidden), (n * cap, hidden), BF16),
            (by_rows(PAIR * cap, hidden), (n * cap, hidden), BF16),
            (by_rows(PAIR * cap, hidden), (n * cap, hidden), BF16),
            (by_rows(PAIR * cap, hidden), (n * cap, hidden), BF16),
            (by_rows(PAIR * seq, part), (n * seq, part), BF16),
            (by_rows(PAIR * seq, 2 * part), (n * seq, 2 * part), BF16),
            (by_seq(PAIR, 1, seq), (n, 1, seq), F32),
            (IN_HBM, (n, own, width), BF16),
            (IN_HBM, (n, own, width), BF16),
            (IN_HBM, (n, seq, width), BF16),
        ),
        [gather_sems(n)] * len(chunks)
        + [pltpu.VMEM((PAIR * cap, width), BF16)]
        + room_for((w_gate, w_up, w_down, shared_w))
        + share_scratch(n, PAIR, seq, width),
        4,
        "expert_forward",
    )(h_all, place_table, gates_all, w_gate, w_up, w_down, shared_w, cot)


def expert_back(
    out_mine, out_heap, resid, cot_all, place_table, gate, act, on_up, on_gate, s_on,
    w_gate, w_up, w_down, shared_w,
):
    n, seq, width = cot_all.shape
    own = seq // 2
    cap, hidden, part = place_table.shape[1], w_gate.shape[0], shared_w.shape[0] // 3
    steps = n // PAIR
    chunks = row_cuts(own, width)

    def kernel(*refs):
        take = pick(refs)
        p, heap, res, ct, pm, gt, ac, ou, og, so, *far = take(14)
        out, dh_mine, dh_heap, cr, dge, due, d_spre, dgt = take(8)
        scratch = [take(6) for _ in chunks]
        total, dr, *near, bring_sems = take(7)
        wg, wu, wd, sw = near
        dh_rows, share_sems, arrived = take(3)
        place = Place(n)
        me = place.me
        i = pl.program_id(0)
        scatters = row_scatters(place, chunks, scratch, p, heap)
        share = Share(place, own, PAIR, dh_rows, dh_mine, dh_heap, share_sems, arrived)

        bring = Bring(list(zip(far, near)), bring_sems)

        @pl.when(i == 0)
        def _():
            place.enter()
            bring.begin()
            open_scatters(scatters)

        @pl.when(i > 0)
        def _():
            step_scatters(place, scatters, i)

        @pl.when(i > 1)
        def _():
            share.left(i - 2)

        slots = []
        for k in range(PAIR):
            cr[pl.ds(k * cap, cap), :] = dot_single_float(pm[k], ct[k]).astype(BF16)
            slots.append(jnp.sum(pm[k].astype(F32) * gt[k], axis=1, keepdims=True))
        gs = jnp.concatenate(slots, 0)
        pl.when(i == 0)(bring.wait)
        plain_da = dot_nt(cr[...], wd[...])
        dgs = jnp.sum(plain_da * ac[...].astype(F32), axis=1, keepdims=True)
        da = plain_da * gs
        dge[...] = (da * og[...].astype(F32)).astype(BF16)
        due[...] = (da * ou[...].astype(F32)).astype(BF16)
        dr[...] = (
            dot_single_float(dge[...], wg[...]) + dot_single_float(due[...], wu[...])
        ).astype(BF16)
        line = lax.broadcasted_iota(jnp.int32, (2 * n, own), 0)
        for k in range(PAIR):
            at = pl.ds(k * cap, cap)
            s_at = pl.ds(k * seq, seq)
            ds = dot_nt(ct[k], sw[2 * part :, :])
            d_spre[s_at, 0:part] = (ds * so[s_at, 0:part].astype(F32)).astype(BF16)
            d_spre[s_at, part:] = (ds * so[s_at, part:].astype(F32)).astype(BF16)
            dh_rows[lax.rem(i, 2), k] = (
                dot_tn(pm[k], dr[at, :])
                + dot_single_float(d_spre[s_at, :], sw[0 : 2 * part, :])
            ).astype(BF16)
            dg = jnp.sum(pm[k].astype(F32) * dgs[k * cap : (k + 1) * cap], axis=0, keepdims=True)
            for u in range(2):
                one = dg[:, u * own : (u + 1) * own]
                high = one.astype(BF16).astype(F32)
                both = jnp.where(line == me, high, jnp.where(line == me + n, one - high, 0.0))
                dgt[k, u] = both.astype(BF16)
        share.start(i)

        @pl.when(i == steps - 1)
        def _():
            share.settle(steps)
            for s, (_, b, rows, c0, w) in zip(scatters, chunks):
                s.close(total.at[pl.ds(b, rows), pl.ds(c0, w)])
            add_rows(out, [total, res], 0, own, width)

    scratch = []
    for _, _, size, _, w in chunks:
        scratch += scatter_scratch(n, size, w)
    scratch += [
        pltpu.VMEM((own, width), F32),
        pltpu.VMEM((PAIR * cap, width), BF16),
    ] + room_for((w_gate, w_up, w_down, shared_w))
    scratch += share_scratch(n, PAIR, seq, width)
    return grid_call(
        kernel,
        steps,
        [IN_HBM, IN_HBM, whole(resid), by_seq(PAIR, seq, width), by_seq(PAIR, cap, seq)]
        + [by_seq(PAIR, 1, seq)]
        + [by_rows(PAIR * cap, hidden)] * 3
        + [by_rows(PAIR * seq, 2 * part)]
        + [IN_HBM] * 4,
        (
            (IN_VMEM, (own, width), BF16),
            (IN_HBM, (n, own, width), BF16),
            (IN_HBM, (n, own, width), BF16),
            (by_rows(PAIR * cap, width), (n * cap, width), BF16),
            (by_rows(PAIR * cap, hidden), (n * cap, hidden), BF16),
            (by_rows(PAIR * cap, hidden), (n * cap, hidden), BF16),
            (by_rows(PAIR * seq, 2 * part), (n * seq, 2 * part), BF16),
            (by_seq(PAIR, 2, 2 * n, own), (n, 2, 2 * n, own), BF16),
        ),
        scratch,
        5,
        "expert_back",
    )(
        out_mine, out_heap, resid, cot_all, place_table, gate, act, on_up, on_gate, s_on,
        w_gate, w_up, w_down, shared_w,
    )


def sum_rows(
    dh_mine, dh_heap, gate_parts, sel, router_t, resid, gain, cot, normed_own,
    rows, dy, act, dge, due, s_act, d_spre, h_all, cot_all,
):
    n, seq, width = cot_all.shape
    own = seq // 2
    chunks = row_cuts(own, width)
    hidden, part = act.shape[1], s_act.shape[1]
    steps = n // 2
    cols = width // steps
    slots = rows.shape[0]

    def kernel(*refs):
        take = pick(refs)
        p, heap, gp, se, wr, res, g, gr, hn = take(9)
        r_in, y_in, *far, h_in, c_in = take(9)
        g2_out, wr_out, d_resid, d_attn, gate_heap = take(5)
        g_gate, g_up, g_down, g_shared = take(4)
        scratch = [take(6) for _ in range(len(chunks) + 1)]
        dg, ex_sems, dh, swap, gr_own, hn_own, *near, bring_sems = take(12)
        a_in, ge_in, ue_in, sa_in, sp_in = near
        place = Place(n)
        t = place.t
        i = pl.program_id(0)
        scatters = row_scatters(place, chunks, scratch, p, heap)
        gates = Scatter(
            place, 1, (2 * n, own), lambda o, u: gp.at[o, u], scratch[-1],
            lambda o: gate_heap.at[o],
        )
        bring = Bring(
            list(zip(far, near)) + [(gr.at[pl.ds(t * own, own)], gr_own), (hn, hn_own)], bring_sems
        )

        @pl.when(i == 0)
        def _():
            place.enter()
            bring.begin()
            open_scatters(scatters + [gates])
            bring.wait()

        @pl.when(i > 0)
        def _():
            step_scatters(place, scatters + [gates], i)

        g_gate[...] = dot_tn(ge_in[...], r_in[...]).astype(g_gate.dtype)
        g_up[...] = dot_tn(ue_in[...], r_in[...]).astype(g_up.dtype)

        g_down[...] = dot_tn(a_in[...], y_in[...]).astype(g_down.dtype)
        g_shared[0 : 2 * part, :] = dot_tn(sp_in[...], h_in[...]).astype(BF16)
        g_shared[2 * part :, :] = dot_tn(sa_in[...], c_in[...]).astype(BF16)

        @pl.when(i == steps - 1)
        def _():
            for s, (_, b, r, c0, w) in zip(scatters, chunks):
                s.close(dh.at[pl.ds(b, r), pl.ds(c0, w)])
            gates.close(dg)
            dgate = dg[0:n, :] + dg[n : 2 * n, :]
            s = se[...]
            total = jnp.sum(s, axis=0, keepdims=True)
            dsel = ROUTE_SCALE * (
                dgate / total - jnp.sum(dgate * s, axis=0, keepdims=True) / (total * total)
            )
            dl = (dsel * s * (1.0 - s)).astype(BF16)
            wr_out[...] = dot_single_float(dl, hn_own[...])
            dh[...] += dot_tn(dl, wr[...])
            size = 16

            def rows_back(j, acc):
                at = pl.ds(pl.multiple_of(j * size, size), size)
                mine = pl.ds(pl.multiple_of(t * own + j * size, size), size)
                v = res[at, :]
                r, one = inv_rms(v), dh[at, :]
                out = gr_own[at, :].astype(F32) + norm_back(v, r, g[...], one)
                d_resid[at, :] = out
                d_attn[mine, :] = out.astype(BF16)
                swap[0, at, :] = out.astype(BF16)
                return acc + jnp.sum(one * (v * r), axis=0, keepdims=True)

            g2_out[...] = lax.fori_loop(0, own // size, rows_back, jnp.zeros((1, width), F32))
            give = remote(swap.at[0], swap.at[1], ex_sems.at[0], ex_sems.at[1], place.twin)
            give.start()
            give.wait_recv()
            d_attn[pl.ds(pl.multiple_of((1 - t) * own, own), own), :] = swap[1]
            give.wait_send()

    scratch = []
    for _, _, size, _, w in chunks:
        scratch += scatter_scratch(n, size, w)
    scratch += scatter_scratch(n, 2 * n, own)
    scratch += [
        pltpu.VMEM((2 * n, own), F32),
        pltpu.SemaphoreType.DMA((2,)),
        pltpu.VMEM((own, width), F32),
        pltpu.VMEM((2, own, width), BF16),
        pltpu.VMEM((own, width), BF16),
        pltpu.VMEM((own, width), BF16),
        *[pltpu.VMEM(a.shape, a.dtype) for a in (act, dge, due, s_act, d_spre)],
        pltpu.SemaphoreType.DMA((7,)),
    ]
    return grid_call(
        kernel,
        steps,
        [IN_HBM] * 3
        + [whole(a) for a in (sel, router_t, resid, gain)]
        + [IN_HBM] * 2
        + [by_cols(slots, cols)] * 2
        + [IN_HBM] * 5
        + [by_cols(n * seq, cols)] * 2,
        (
            (IN_VMEM, (1, width), F32),
            (IN_VMEM, (n, width), F32),
            (IN_VMEM, (own, width), F32),
            (IN_VMEM, (seq, width), BF16),
            (IN_HBM, (n, 2 * n, own), BF16),
            (by_cols(hidden, cols), (hidden, width), EXPERT_GRADS),
            (by_cols(hidden, cols), (hidden, width), EXPERT_GRADS),
            (by_cols(hidden, cols), (hidden, width), EXPERT_GRADS),
            (by_cols(3 * part, cols), (3 * part, width), BF16),
        ),
        scratch,
        6,
        "sum_row_gradients",
    )(
        dh_mine, dh_heap, gate_parts, sel, router_t, resid, gain, cot, normed_own,
        rows, dy, act, dge, due, s_act, d_spre,
        h_all.reshape(n * seq, width), cot_all.reshape(n * seq, width),
    )


EXPERT_GRADS = BF16


def attend_back(
    n, d_attn, x_seq, h1, latent, cn, gain_kv, k_rope, cos2, sin2, w_kvd,
    q_n, q_r, kv, ctx, w_q, w_kvu, w_out, g2_small, wr_small, g_shared, padded,
):
    seq, width = x_seq.shape
    head = DN + DR
    pairs = w_q.shape[1] // (2 * head)
    factor = 1.0 / math.sqrt(head)
    cols = width // n
    part_rows = g_shared.shape[0] // 3

    def kernel(*refs):
        take = pick(refs)
        da, x, h, lat, c_n, gk, kpe, co, si, wd, g2s, wrs = take(12)
        gsh, qn, qr, kvb, cx, wq, wu, wo = take(8)
        dh_out, g_kvd, small, sh_got = take(4)
        g_wq, g_wu, g_wo = take(3)
        trade_sems, dh, dcn, dkr, dq, dkv, dctx = take(7)
        place = Place(n)
        i = pl.program_id(0)
        trade = Trade(
            place,
            [
                lambda k, j=j: gsh.at[pl.ds(j * part_rows, padded), pl.ds(k * cols, cols)]
                for j in range(3)
            ],
            [lambda k, j=j: sh_got.at[k, j] for j in range(3)],
            trade_sems,
        )

        @pl.when(i == 0)
        def _():
            place.enter(everyone=True)
            trade.begin()
            dh[...] = jnp.zeros_like(dh)
            dcn[...] = jnp.zeros_like(dcn)
            dkr[...] = jnp.zeros_like(dkr)

        dctx[...] = dot_nt(da[...], wo[...]).astype(BF16)
        g_wo[...] = dot_tn(cx[...], da[...]).astype(BF16)
        for k in range(2):
            base = k * (DN + DV)
            keys, values = kvb[:, base : base + DN], kvb[:, base + DN : base + DN + DV]
            one_n, one_r = qn[:, k * DN : (k + 1) * DN], qr[:, k * DR : (k + 1) * DR]
            d_one = dctx[:, k * DV : (k + 1) * DV]
            weights = causal_weights(one_n, one_r, keys, kpe[...], factor)
            dw = dot_nt(d_one, values)
            ds = (weights * (dw - jnp.sum(weights * dw, axis=1, keepdims=True))).astype(BF16)
            dq[:, k * head : k * head + DN] = (dot_single_float(ds, keys) * factor).astype(BF16)
            d_rope = dot_single_float(ds, kpe[...]) * factor
            dq[:, k * head + DN : (k + 1) * head] = (
                d_rope * co[...] - swapped(d_rope) * si[...]
            ).astype(BF16)
            dkv[:, base : base + DN] = (dot_tn(ds, one_n) * factor).astype(BF16)
            dkr[...] += dot_tn(ds, one_r) * factor
            dkv[:, base + DN : base + DN + DV] = dot_tn(weights.astype(BF16), d_one).astype(BF16)
        g_wq[...] = dot_tn(h[...], dq[...]).astype(BF16)
        g_wu[...] = dot_tn(c_n[...], dkv[...]).astype(BF16)
        dcn[...] += dot_nt(dkv[...], wu[...])
        dh[...] += dot_nt(dq[...], wq[...])

        @pl.when(i == pairs - 1)
        def _():
            lt = lat[...]
            factor_kv = inv_rms(lt)
            back = dcn[...]
            g_gain = jnp.sum(back * lt * factor_kv, axis=0, keepdims=True)
            d_lat = norm_back(lt, factor_kv, gk[...], back)
            d_rope = dkr[...]
            d_rope = d_rope * co[...] - swapped(d_rope) * si[...]
            d_first = jnp.concatenate([d_lat, d_rope], 1).astype(BF16)
            g_kvd[...] = dot_tn(h[...], d_first).astype(BF16)
            dh[...] += dot_single_float(d_first, wd[...])
            size = 16

            def finish(j, acc):
                at = pl.ds(pl.multiple_of(j * size, size), size)
                v = x[at, :].astype(F32)
                one = dh[at, :]
                dh_out[at, :] = one.astype(BF16)
                return acc + jnp.sum(one * (v * inv_rms(v)), axis=0, keepdims=True)

            g_one = lax.fori_loop(0, seq // size, finish, jnp.zeros((1, width), F32))
            small[...] = jnp.zeros_like(small)
            kv_cols = KVR // n
            for o in range(n):
                at = slice(o * cols, (o + 1) * cols)
                small[o, 0:1, :] = g_one[:, at].astype(BF16)
                small[o, 1:2, :] = g2s[:, at].astype(BF16)
                small[o, 2:3, 0:kv_cols] = g_gain[:, o * kv_cols : (o + 1) * kv_cols].astype(BF16)
                small[o, 16 : 16 + n, :] = wrs[:, at].astype(BF16)
            trade.settle()

    scratch = [
        pltpu.SemaphoreType.DMA((2, n, 3)),
        pltpu.VMEM((seq, width), F32),
        pltpu.VMEM((seq, KVR), F32),
        pltpu.VMEM((seq, DR), F32),
        pltpu.VMEM((seq, 2 * head), BF16),
        pltpu.VMEM((seq, 2 * (DN + DV)), BF16),
        pltpu.VMEM((seq, 2 * DV), BF16),
    ]
    resident = (
        d_attn, x_seq, h1, latent, cn, gain_kv, k_rope, cos2, sin2, w_kvd, g2_small, wr_small,
    )
    return grid_call(
        kernel,
        pairs,
        [whole(a) for a in resident]
        + [
            IN_HBM,
            by_cols(seq, 2 * DN),
            by_cols(seq, 2 * DR),
            by_cols(seq, 2 * (DN + DV)),
            by_cols(seq, 2 * DV),
            by_cols(width, 2 * head),
            by_cols(KVR, 2 * (DN + DV)),
            by_rows(2 * DV, width),
        ],
        (
            (IN_VMEM, (seq, width), BF16),
            (IN_VMEM, (width, KVR + DR), BF16),
            (IN_VMEM, (n, 32, cols), BF16),
            (IN_HBM, (n, 3, padded, cols), BF16),
            (by_cols(width, 2 * head), w_q.shape, BF16),
            (by_cols(KVR, 2 * (DN + DV)), w_kvu.shape, BF16),
            (by_rows(2 * DV, width), w_out.shape, BF16),
        ),
        scratch,
        7,
        "attend_back",
    )(*resident, g_shared, q_n, q_r, kv, ctx, w_q, w_kvu, w_out)


def sum_weights(n, g_query, g_kvu, g_out, g_kvd, g_small, dh1, x_own, d_resid, gain, g_shared, hidden):
    q_rows, q_cols = g_query.shape[0] // n, g_query.shape[1]
    cut = q_cols // 4 * 3
    o_rows, o_cols = g_out.shape[0], g_out.shape[1] // n
    u_rows, u_cols = g_kvu.shape[0] // n, g_kvu.shape[1]
    d_rows, d_cols = g_kvd.shape[0] // (2 * n), g_kvd.shape[1]
    s_rows, s_cols = g_small.shape[1:]
    seq, width = dh1.shape
    own = seq // 2
    specs = [
        (0, (q_rows, cut)),
        (1, (q_rows, q_cols - cut)),
        (2, (o_rows, o_cols)),
        (1, (u_rows, u_cols)),
        (1, (d_rows, d_cols)),
        (2, (s_rows, s_cols)),
    ]

    def kernel(*refs):
        take = pick(refs)
        q, ku, wo, kd, sm, dh, x, dr, g, sh = take(10)
        q_out, ku_out, wo_out, kd_out, sm_out, in_out, sg_out, su_out, sd_out = take(9)
        kd_heap, sm_heap = take(2)
        scratch = [take(6) for _ in specs]
        got, swap_sems, turned = take(3)
        place = Place(n)
        t = place.t
        place.enter()
        swap = remote(
            dh.at[pl.ds((1 - t) * own, own)], got, swap_sems.at[0], swap_sems.at[1], place.twin
        )
        swap.start()
        views = [
            lambda o, u: q.at[pl.ds(o * q_rows, q_rows), pl.ds(0, cut)],
            lambda o, u: q.at[pl.ds(o * q_rows, q_rows), pl.ds(cut, q_cols - cut)],
            lambda o, u: wo.at[:, pl.ds(o * o_cols, o_cols)],
            lambda o, u: ku.at[pl.ds(o * u_rows, u_rows)],
            lambda o, u: kd.at[pl.ds((o * 2 + u) * d_rows, d_rows)],
            lambda o, u: sm.at[o],
        ]
        heaps = [None] * 4 + [lambda o: kd_heap.at[o], lambda o: sm_heap.at[o]]
        scatters = [
            Scatter(place, ring, shape, view, more, heap)
            for (ring, shape), view, more, heap in zip(specs, views, scratch, heaps)
        ]
        outs = [
            q_out.at[:, pl.ds(0, cut)],
            q_out.at[:, pl.ds(cut, q_cols - cut)],
            wo_out,
            ku_out,
            kd_out,
            sm_out,
        ]

        def grad_in():
            swap.wait_recv()
            size = 16

            def rows_back(j, _):
                at = pl.ds(pl.multiple_of(j * size, size), size)
                mine = pl.ds(pl.multiple_of(t * own + j * size, size), size)
                v = x[at, :].astype(F32)
                one = dh[mine, :].astype(F32) + got[at, :].astype(F32)
                in_out[at, :] = (dr[at, :] + norm_back(v, inv_rms(v), g[...], one)).astype(BF16)
                return 0

            lax.fori_loop(0, own // size, rows_back, 0)

        def put_together(j, out):
            for k in range(n):
                turned[k * hidden : (k + 1) * hidden, :] = sh[k, j, 0:hidden, :].astype(F32)
            if j < 2:
                out[...] = dot_nt(eye(q_rows), turned[...].astype(BF16))
            else:
                out[...] = turned[...]

        beside = [grad_in] + [
            lambda j=j, out=out: put_together(j, out)
            for j, out in enumerate((sg_out, su_out, sd_out))
        ]
        run_scatters(place, scatters, outs, beside)
        swap.wait_send()

    scratch = []
    for _, shape in specs:
        scratch += scatter_scratch(n, *shape)
    scratch += [
        pltpu.VMEM((own, width), BF16),
        pltpu.SemaphoreType.DMA((2,)),
        pltpu.VMEM((n * hidden, q_rows), F32),
    ]
    return comm_call(
        kernel,
        (
            sds((q_rows, q_cols), F32),
            sds((u_rows, u_cols), F32),
            sds((o_rows, o_cols), F32),
            sds((d_rows, d_cols), F32),
            sds((s_rows, s_cols), F32),
            sds((own, width), BF16),
            sds((q_rows, n * hidden), F32),
            sds((q_rows, n * hidden), F32),
            sds((n * hidden, q_rows), F32),
            sds((n, d_rows, d_cols), BF16),
            sds((n, s_rows, s_cols), BF16),
        ),
        (IN_VMEM,) * 9 + (IN_HBM,) * 2,
        [IN_HBM] * 5 + [IN_VMEM] * 5,
        scratch,
        8,
        "sum_weights",
    )(g_query, g_kvu, g_out, g_kvd, g_small, dh1, x_own, d_resid, gain, g_shared)[:9]


def finish(results, small, kept, experts):
    t_cols = small.shape[1] // 2
    n = small.shape[0] - 16
    hidden, width = experts[0].shape
    steps = 4
    rows = hidden // steps
    count = len(results)

    def kernel(*refs):
        take = pick(refs)
        came, (sm,), parts = take(count), take(1), take(3)
        outs, (g1, g2, gk, gr), wide = take(count), take(4), take(3)

        @pl.when(pl.program_id(0) == 0)
        def _():
            lower = lax.axis_index("tp") == 0
            mine = jnp.where(lower, sm[:, :t_cols], sm[:, t_cols:])
            g1[...] = mine[0:1, :]
            g2[...] = mine[1:2, :]
            gk[...] = jnp.where(lower, sm[2:3, :kept], sm[2:3, kept : 2 * kept])
            gr[...] = mine[16 : 16 + n, :]

        for one, out in zip(came, outs):
            out[...] = one[...]
        for part, out in zip(parts, wide):
            out[...] = part[...].astype(F32)

    def spec(*shape):
        return pl.BlockSpec(shape, lambda i: (0, 0))

    blocks = [by_rows(a.shape[0] // steps, a.shape[1]) for a in results]
    return pl.pallas_call(
        kernel,
        grid=(steps,),
        in_specs=blocks + [spec(*small.shape)] + [by_rows(rows, width)] * 3,
        out_specs=tuple(blocks)
        + (spec(1, t_cols), spec(1, t_cols), spec(1, kept), spec(n, t_cols))
        + (by_rows(rows, width),) * 3,
        out_shape=tuple(sds(a.shape, a.dtype) for a in results)
        + (sds((1, t_cols), F32), sds((1, t_cols), F32), sds((1, kept), F32), sds((n, t_cols), F32))
        + (sds((hidden, width), F32),) * 3,
        compiler_params=pltpu.CompilerParams(vmem_limit_bytes=VMEM_BYTES),
        name="finish",
    )(*results, small, *experts)


def fast(
    hidden_in,
    routes,
    cotangent,
    norm_attn,
    query_proj,
    kv_down,
    kv_norm,
    kv_up,
    out_proj,
    norm_ffn,
    router_proj,
    shared_gate,
    shared_up,
    shared_down,
    expert_gate,
    expert_up_weight,
    expert_down,
):
    n = lax.axis_size("fsdp")
    own, width = hidden_in.shape
    seq = 2 * own
    cap = 4 * seq * TOP // (3 * n)
    cos_table, sin_table = rope_tables(seq, DR)
    cos2 = jnp.concatenate([cos_table, cos_table], 1)
    sin2 = jnp.concatenate([-sin_table, sin_table], 1)
    model_rows, latent_rows = norm_attn.shape[0], kv_norm.shape[0]
    hidden = shared_gate.shape[1] // n

    full_wq, full_wkva, full_wkvb, full_wo, small_all, x_seq, blocks = collect_inputs(
        n,
        query_proj,
        kv_down.T,
        kv_up,
        out_proj,
        hidden_in,
        norm_attn[None],
        norm_ffn[None],
        jnp.pad(kv_norm, (0, model_rows - latent_rows))[None],
        router_proj.T,
        routes.T,
        shared_gate,
        shared_up,
        shared_down,
    )
    (
        resid, sel, full_g2, router_t, normed_own, gates_own, h1, full_g1, full_gkv, latent,
        latent_normed, key_rope, shared_w, q_n, q_r, kv, context,
    ) = attend(
        n, x_seq, hidden_in, small_all, full_wkva, cos2, sin2, full_wq, full_wkvb, full_wo, blocks
    )
    place_table, h_all, gates_all = spread_rows(n, normed_own, gates_own, small_all, cap)
    w_gate, w_up, w_down = expert_gate[0].T, expert_up_weight[0].T, expert_down[0]
    (
        rows, act, act_gate, on_up, on_gate, sh_act, sh_on, gate, out_mine, out_heap, cot_all,
    ) = expert_forward(
        h_all, place_table, gates_all, w_gate, w_up, w_down, shared_w, cotangent
    )
    (
        hidden_out, dh_mine, dh_heap, cot_rows, d_pre_gate, d_pre_up, d_sh_pre, d_gates,
    ) = expert_back(
        out_mine, out_heap, resid, cot_all, place_table, gate, act, on_up, on_gate, sh_on,
        w_gate, w_up, w_down, shared_w,
    )
    (
        grad_g2, grad_wr, d_resid, d_attn, _, grad_egate, grad_eup, grad_edown, grad_shared,
    ) = sum_rows(
        dh_mine, dh_heap, d_gates, sel, router_t, resid, full_g2, cotangent, normed_own,
        rows, cot_rows, act_gate, d_pre_gate, d_pre_up, sh_act, d_sh_pre, h_all, cot_all,
    )
    dh1_part, grad_wkva, grad_small, out_shared, grad_wq, grad_wkvb, grad_wo = attend_back(
        n, d_attn, x_seq, h1, latent, latent_normed, full_gkv, key_rope, cos2, sin2, full_wkva,
        q_n, q_r, kv, context, full_wq, full_wkvb, full_wo, grad_g2, grad_wr, grad_shared,
        blocks.shape[2],
    )
    (
        out_wq, out_wkvb, out_wo, out_wkva, out_small, grad_in, out_sgate, out_sup, out_sdown,
    ) = sum_weights(
        n, grad_wq, grad_wkvb, grad_wo, grad_wkva, grad_small, dh1_part, hidden_in, d_resid,
        full_g1, out_shared, hidden,
    )
    (
        hidden_out, grad_in, out_wq, out_wkva, out_wkvb, out_wo, out_sgate, out_sup, out_sdown,
        out_g1, out_g2, out_gkv, out_wr, grad_egate, grad_eup, grad_edown,
    ) = finish(
        (hidden_out, grad_in, out_wq, out_wkva, out_wkvb, out_wo, out_sgate, out_sup, out_sdown),
        out_small, latent_rows // 2, (grad_egate, grad_eup, grad_edown),
    )
    return (
        hidden_out,
        grad_in,
        out_g1[0],
        out_wq,
        out_wkva,
        out_gkv[0],
        out_wkvb,
        out_wo,
        out_g2[0],
        out_wr.T,
        out_sgate,
        out_sup,
        out_sdown,
        grad_egate.T[None],
        grad_eup.T[None],
        grad_edown[None],
    )


def suits(mesh):
    return mesh.shape["tp"] == 2 and mesh.shape["fsdp"] * 128 == MODEL_WIDTH


def solution(mesh):
    return jax.shard_map(
        fast if suits(mesh) else plain,
        mesh=mesh,
        in_specs=(
            P(("fsdp", "tp"), None),
            P("fsdp", None),
            P("fsdp", None),
            P("fsdp"),
            P("fsdp", "tp"),
            P("fsdp", None),
            P("fsdp"),
            P("fsdp", "tp"),
            P("tp", "fsdp"),
            P("fsdp"),
            P("fsdp", None),
            P("fsdp", "tp"),
            P("fsdp", "tp"),
            P("tp", "fsdp"),
            P("fsdp", None, "tp"),
            P("fsdp", None, "tp"),
            P("fsdp", "tp", None),
        ),
        out_specs=(
            P(("fsdp", "tp"), None),
            P(("fsdp", "tp"), None),
            P(("fsdp", "tp")),
            P("fsdp", "tp"),
            P(("fsdp", "tp"), None),
            P(("fsdp", "tp")),
            P("fsdp", "tp"),
            P("tp", "fsdp"),
            P(("fsdp", "tp")),
            P(("fsdp", "tp"), None),
            P("fsdp", "tp"),
            P("fsdp", "tp"),
            P("tp", "fsdp"),
            P("fsdp", None, "tp"),
            P("fsdp", None, "tp"),
            P("fsdp", "tp", None),
        ),
        check_vma=False,
    )
```

```python
import math

import jax
import jax.numpy as jnp
import numpy as np
from jax import lax
from jax.experimental import pallas as pl
from jax.experimental.pallas import tpu as pltpu
from jax.sharding import PartitionSpec as P

MODEL_WIDTH = 2048
DN = 128
DR = 64
DV = 128
KVR = 512
TOP = 6


NORM_EPS = 1e-06
ROPE_THETA = 50000.0
ROUTE_SCALE = 2.446


def dot_single_float(left, right):
    return jnp.dot(left, right, preferred_element_type=jnp.float32)


def dot_high(left, right):
    return jnp.dot(left, right, precision=lax.Precision.HIGHEST, preferred_element_type=jnp.float32)


def inv_rms(value):
    return lax.rsqrt(jnp.mean(value * value, axis=-1, keepdims=True) + NORM_EPS)


def norm_back(value, factor, gain, grad):
    scaled = grad * gain
    return factor * scaled - value * factor**3 * jnp.mean(scaled * value, axis=-1, keepdims=True)


def silu_grad(value):
    sigm = jax.nn.sigmoid(value)
    return sigm * (1.0 + value * (1.0 - sigm))


def rope_tables(length, width):
    half_width = width // 2
    freq = ROPE_THETA ** (-(jnp.arange(half_width, dtype=jnp.float32) * 2.0 / width))
    angle = jnp.arange(length, dtype=jnp.float32)[:, None] * freq[None, :]
    return (jnp.cos(angle), jnp.sin(angle))


def rotate(value, cos_table, sin_table):
    half_width = value.shape[-1] // 2
    first, second = (value[..., :half_width], value[..., half_width:])
    return jnp.concatenate(
        [first * cos_table - second * sin_table, second * cos_table + first * sin_table], -1
    )


def unrotate(grad, cos_table, sin_table):
    half_width = grad.shape[-1] // 2
    first, second = (grad[..., :half_width], grad[..., half_width:])
    return jnp.concatenate(
        [first * cos_table + second * sin_table, second * cos_table - first * sin_table], -1
    )


def scores_of(query, keys, factor):
    length = query.shape[0]
    raw_scores = (
        jnp.einsum("qhd,khd->hqk", query, keys, preferred_element_type=jnp.float32) * factor
    )
    causal = jnp.arange(length)[:, None] >= jnp.arange(length)[None, :]
    return jnp.where(causal[None], raw_scores, -1e30)


def plain(
    hidden_in,
    routes,
    cotangent,
    norm_attn,
    query_proj,
    kv_down,
    kv_norm,
    kv_up,
    out_proj,
    norm_ffn,
    router_proj,
    shared_gate,
    shared_up,
    shared_down,
    expert_gate,
    expert_up_weight,
    expert_down,
):
    n_tp = lax.axis_size("tp")
    sharded_parts_count = lax.axis_size("fsdp")
    own_rows = hidden_in.shape[0]
    seq_len = own_rows * n_tp
    head_width = DN + DR
    heads_here = query_proj.shape[1] // head_width
    expert_capacity = 4 * seq_len * TOP // (3 * sharded_parts_count)
    tp_index = lax.axis_index("tp")
    factor = 1.0 / math.sqrt(head_width)
    cos_table, sin_table = rope_tables(seq_len, DR)

    def arrange(grad):
        rest = grad.shape[1:]
        block = grad.shape[0] // (sharded_parts_count * n_tp)
        split = grad.reshape((sharded_parts_count, n_tp, block) + rest)
        return jnp.swapaxes(split, 0, 1).reshape((grad.shape[0],) + rest)

    x_group = lax.all_gather(hidden_in, "tp", axis=0, tiled=True).astype(jnp.float32)
    full_g1, full_wq, full_wkva, full_gkv, full_wkvb, full_wo = (
        lax.all_gather(norm_attn, "fsdp", axis=0, tiled=True),
        lax.all_gather(query_proj, "fsdp", axis=0, tiled=True),
        lax.all_gather(kv_down, "fsdp", axis=0, tiled=True),
        lax.all_gather(kv_norm, "fsdp", axis=0, tiled=True),
        lax.all_gather(kv_up, "fsdp", axis=0, tiled=True),
        lax.all_gather(out_proj, "fsdp", axis=1, tiled=True),
    )
    factor_one = inv_rms(x_group)
    x_normed = x_group * factor_one
    normed_in = (x_normed * full_g1.astype(jnp.float32)).astype(jnp.bfloat16)
    query_raw = dot_single_float(normed_in, full_wq).reshape(seq_len, heads_here, head_width)
    query = jnp.concatenate(
        [query_raw[..., :DN], rotate(query_raw[..., DN:], cos_table[:, None], sin_table[:, None])],
        -1,
    ).astype(jnp.bfloat16)
    kv_first = dot_single_float(normed_in, full_wkva)
    latent = kv_first[:, :KVR]
    latent_factor = inv_rms(latent)
    latent_normed = (latent * latent_factor * full_gkv.astype(jnp.float32)).astype(jnp.bfloat16)
    key_rope = rotate(kv_first[:, KVR:], cos_table, sin_table).astype(jnp.bfloat16)
    kv_full = (
        dot_single_float(latent_normed, full_wkvb)
        .astype(jnp.bfloat16)
        .reshape(seq_len, heads_here, DN + DV)
    )
    keys = jnp.concatenate(
        [kv_full[..., :DN], jnp.broadcast_to(key_rope[:, None, :], (seq_len, heads_here, DR))], -1
    )
    values = kv_full[..., DN:]
    scores = scores_of(query, keys, factor)
    top_score = jnp.max(scores, axis=-1, keepdims=True)
    log_total = top_score + jnp.log(jnp.sum(jnp.exp(scores - top_score), axis=-1, keepdims=True))
    weights_bf = jnp.exp(scores - log_total).astype(jnp.bfloat16)
    context = jnp.einsum("hqk,khd->qhd", weights_bf, values, preferred_element_type=jnp.float32)
    context = context.reshape(seq_len, heads_here * DV).astype(jnp.bfloat16)
    attn_own = lax.psum_scatter(
        dot_single_float(context, full_wo), "tp", scatter_dimension=0, tiled=True
    )
    x_own = hidden_in.astype(jnp.float32)
    resid = x_own + attn_own
    full_g2, full_wr, full_sg, full_su, full_sd = (
        lax.all_gather(norm_ffn, "fsdp", axis=0, tiled=True),
        lax.all_gather(router_proj, "fsdp", axis=0, tiled=True),
        lax.all_gather(shared_gate, "fsdp", axis=0, tiled=True),
        lax.all_gather(shared_up, "fsdp", axis=0, tiled=True),
        lax.all_gather(shared_down, "fsdp", axis=1, tiled=True),
    )
    factor_two = inv_rms(resid)
    resid_normed = resid * factor_two
    normed_own = (resid_normed * full_g2.astype(jnp.float32)).astype(jnp.bfloat16)
    normed_ffn = lax.all_gather(normed_own, "tp", axis=0, tiled=True)
    logits = dot_single_float(normed_ffn, full_wr)
    sigmoids = jax.nn.sigmoid(logits)
    chosen = jnp.take_along_axis(sigmoids, routes, axis=1)
    chosen_sum = jnp.sum(chosen, axis=-1, keepdims=True)
    gate_values = ROUTE_SCALE * chosen / chosen_sum
    flat_routes = routes.reshape(-1)
    one_hot = (
        flat_routes[:, None] == jnp.arange(sharded_parts_count, dtype=jnp.int32)[None, :]
    ).astype(jnp.int32)
    slot_num = jnp.sum((jnp.cumsum(one_hot, axis=0) - one_hot) * one_hot, axis=-1)
    target = flat_routes * expert_capacity + slot_num
    token_of = jnp.arange(seq_len * TOP, dtype=jnp.int32) // TOP
    send_rows = (
        jnp.zeros((sharded_parts_count * expert_capacity, MODEL_WIDTH), jnp.bfloat16)
        .at[target]
        .set(normed_ffn[token_of])
    )
    send_rows = send_rows.reshape(sharded_parts_count, expert_capacity, MODEL_WIDTH)
    expert_gate_weight = expert_gate[0]
    routed_up_weight = expert_up_weight[0]
    w_edown = expert_down[0]
    arrived = lax.all_to_all(send_rows, "fsdp", split_axis=0, concat_axis=0, tiled=True)
    sources = arrived.shape[0]
    items = arrived.shape[1]
    flattened_input = arrived.reshape(sources * items, MODEL_WIDTH)
    pre_gate = dot_single_float(flattened_input, expert_gate_weight)
    up_projected = dot_single_float(flattened_input, routed_up_weight)
    activ = (jax.nn.silu(pre_gate) * up_projected).astype(jnp.bfloat16)
    output = (
        dot_single_float(activ, w_edown).astype(jnp.bfloat16).reshape(sources, items, MODEL_WIDTH)
    )
    returned = lax.all_to_all(output, "fsdp", split_axis=0, concat_axis=0, tiled=True)
    hidden_shape = (sources, items, pre_gate.shape[-1])
    returned, arrived, pre_gate, up_projected, activ = (
        returned,
        arrived,
        pre_gate.reshape(hidden_shape),
        up_projected.reshape(hidden_shape),
        activ.reshape(hidden_shape),
    )
    pair_rows = returned.reshape(sharded_parts_count * expert_capacity, MODEL_WIDTH)[
        target
    ].reshape(seq_len, TOP, MODEL_WIDTH)
    routed_rows = jnp.sum(gate_values[..., None] * pair_rows, axis=1)
    shared_pre_gate = dot_single_float(normed_ffn, full_sg)
    shared_pre_up = dot_single_float(normed_ffn, full_su)
    shared_act = (jax.nn.silu(shared_pre_gate) * shared_pre_up).astype(jnp.bfloat16)
    ffn_own = lax.psum_scatter(
        (routed_rows + dot_single_float(shared_act, full_sd)).astype(jnp.bfloat16),
        "tp",
        scatter_dimension=0,
        tiled=True,
    ).astype(jnp.float32)
    hidden_out = (resid + ffn_own).astype(jnp.bfloat16)
    grad_own = lax.dynamic_slice_in_dim(cotangent, tp_index * own_rows, own_rows, 0).astype(
        jnp.float32
    )
    d_shared = dot_single_float(cotangent, full_sd.T)
    d_sgate = (d_shared * shared_pre_up * silu_grad(shared_pre_gate)).astype(jnp.bfloat16)
    d_sup = (d_shared * jax.nn.silu(shared_pre_gate)).astype(jnp.bfloat16)
    dh2_part = dot_single_float(d_sgate, full_sg.T) + dot_single_float(d_sup, full_su.T)
    grad_sdown = dot_single_float(shared_act.T, cotangent)
    grad_sgate = dot_single_float(normed_ffn.T, d_sgate)
    grad_sup = dot_single_float(normed_ffn.T, d_sup)
    cot_pairs = cotangent[token_of]
    d_output = (gate_values.reshape(-1)[:, None] * cot_pairs).astype(jnp.bfloat16)
    d_gate_part = jnp.einsum("td,tkd->tk", cotangent, pair_rows, preferred_element_type=jnp.float32)
    grad_send = (
        jnp.zeros((sharded_parts_count * expert_capacity, MODEL_WIDTH), jnp.bfloat16)
        .at[target]
        .set(d_output)
    )
    grad_arrived = lax.all_to_all(
        grad_send.reshape(sharded_parts_count, expert_capacity, MODEL_WIDTH),
        "fsdp",
        split_axis=0,
        concat_axis=0,
        tiled=True,
    )
    grad_flat = grad_arrived.reshape(-1, MODEL_WIDTH)
    flattened_gate = pre_gate.reshape(grad_flat.shape[0], -1)
    up_flat = up_projected.reshape(grad_flat.shape[0], -1)
    activ_flat = activ.reshape(grad_flat.shape[0], -1)
    flattened_rows = arrived.reshape(-1, MODEL_WIDTH)
    activation_gradient = dot_single_float(grad_flat, w_edown.T)
    expert_gate_gradient = (activation_gradient * up_flat * silu_grad(flattened_gate)).astype(
        jnp.bfloat16
    )
    expert_up_gradient = (activation_gradient * jax.nn.silu(flattened_gate)).astype(jnp.bfloat16)
    grad_edown = dot_single_float(activ_flat.T, grad_flat)
    grad_egate = dot_single_float(flattened_rows.T, expert_gate_gradient)
    expert_up_weight_gradient = dot_single_float(flattened_rows.T, expert_up_gradient)
    row_gradients = (
        dot_single_float(expert_gate_gradient, expert_gate_weight.T)
        + dot_single_float(expert_up_gradient, routed_up_weight.T)
    ).reshape(sharded_parts_count, expert_capacity, MODEL_WIDTH)
    d_back = lax.all_to_all(
        row_gradients.astype(jnp.bfloat16), "fsdp", split_axis=0, concat_axis=0, tiled=True
    ).astype(row_gradients.dtype)
    dh2_part = dh2_part + jnp.sum(
        d_back.reshape(sharded_parts_count * expert_capacity, MODEL_WIDTH)[target].reshape(
            seq_len, TOP, MODEL_WIDTH
        ),
        axis=1,
    )
    dh2_own, dgate_own = (
        lax.psum_scatter(
            dh2_part.astype(jnp.bfloat16), "tp", scatter_dimension=0, tiled=True
        ).astype(jnp.float32),
        lax.psum_scatter(
            d_gate_part.astype(jnp.bfloat16), "tp", scatter_dimension=0, tiled=True
        ).astype(jnp.float32),
    )
    own_routes = lax.dynamic_slice_in_dim(routes, tp_index * own_rows, own_rows, 0)
    own_chosen = lax.dynamic_slice_in_dim(chosen, tp_index * own_rows, own_rows, 0)
    own_sum = lax.dynamic_slice_in_dim(chosen_sum, tp_index * own_rows, own_rows, 0)
    d_chosen = ROUTE_SCALE * (
        dgate_own / own_sum
        - jnp.sum(dgate_own * own_chosen, axis=-1, keepdims=True) / (own_sum * own_sum)
    )
    d_select = d_chosen * own_chosen * (1.0 - own_chosen)
    expert_ids = jnp.arange(sharded_parts_count, dtype=jnp.int32)
    d_logits = jnp.sum(
        jnp.where(own_routes[..., None] == expert_ids, d_select[..., None], 0.0), axis=1
    ).astype(jnp.bfloat16)
    dh2_own = dh2_own + dot_single_float(d_logits, full_wr.T)
    grad_wr = dot_single_float(normed_own.T, d_logits)
    grad_g2 = jnp.sum(dh2_own * resid_normed, axis=0)
    d_resid = grad_own + norm_back(resid, factor_two, full_g2.astype(jnp.float32), dh2_own)
    d_attn = lax.all_gather(d_resid.astype(jnp.bfloat16), "tp", axis=0, tiled=True)
    grad_wo = dot_single_float(context.T, d_attn)
    d_context = (
        dot_single_float(d_attn, full_wo.T).astype(jnp.bfloat16).reshape(seq_len, heads_here, DV)
    )
    weights_f = jnp.exp(scores_of(query, keys, factor) - log_total)
    d_weights = jnp.einsum("qhd,khd->hqk", d_context, values, preferred_element_type=jnp.float32)
    d_scores = (
        weights_f * (d_weights - jnp.sum(weights_f * d_weights, axis=-1, keepdims=True))
    ).astype(jnp.bfloat16)
    d_query = (
        jnp.einsum("hqk,khd->qhd", d_scores, keys, preferred_element_type=jnp.float32) * factor
    )
    d_keys = (
        jnp.einsum("hqk,qhd->khd", d_scores, query, preferred_element_type=jnp.float32) * factor
    )
    d_values = jnp.einsum(
        "hqk,qhd->khd",
        weights_f.astype(jnp.bfloat16),
        d_context,
        preferred_element_type=jnp.float32,
    )
    d_qraw = jnp.concatenate(
        [d_query[..., :DN], unrotate(d_query[..., DN:], cos_table[:, None], sin_table[:, None])], -1
    )
    d_qraw = d_qraw.reshape(seq_len, heads_here * head_width).astype(jnp.bfloat16)
    d_kv = (
        jnp.concatenate([d_keys[..., :DN], d_values], -1)
        .reshape(seq_len, heads_here * (DN + DV))
        .astype(jnp.bfloat16)
    )
    d_krope = unrotate(jnp.sum(d_keys[..., DN:], axis=1), cos_table, sin_table)
    grad_wq = dot_single_float(normed_in.T, d_qraw)
    grad_wkvb = dot_single_float(latent_normed.T, d_kv)
    d_latent_normed = dot_single_float(d_kv, full_wkvb.T)
    gkv_f = full_gkv.astype(jnp.float32)
    grad_gkv = jnp.sum(d_latent_normed * latent * latent_factor, axis=0)
    d_latent = norm_back(latent, latent_factor, gkv_f, d_latent_normed)
    d_kvfirst = jnp.concatenate([d_latent, d_krope], -1)
    grad_wkva = dot_high(normed_in.astype(jnp.float32).T, d_kvfirst)
    dh1_part = dot_single_float(d_qraw, full_wq.T) + dot_high(
        d_kvfirst, full_wkva.astype(jnp.float32).T
    )
    grad_g1 = jnp.sum(dh1_part * x_normed, axis=0)
    dh1_own, sum_g1, sum_wkva, sum_gkv, sum_g2, sum_wr = (
        lax.psum_scatter(
            dh1_part.astype(jnp.bfloat16), "tp", scatter_dimension=0, tiled=True
        ).astype(jnp.float32),
        lax.psum_scatter(
            arrange(grad_g1).astype(jnp.bfloat16), "tp", scatter_dimension=0, tiled=True
        ).astype(jnp.float32),
        lax.psum_scatter(
            arrange(grad_wkva).astype(jnp.bfloat16), "tp", scatter_dimension=0, tiled=True
        ).astype(jnp.float32),
        lax.psum_scatter(
            arrange(grad_gkv).astype(jnp.bfloat16), "tp", scatter_dimension=0, tiled=True
        ).astype(jnp.float32),
        lax.psum_scatter(
            arrange(grad_g2).astype(jnp.bfloat16), "tp", scatter_dimension=0, tiled=True
        ).astype(jnp.float32),
        lax.psum_scatter(
            arrange(grad_wr).astype(jnp.bfloat16), "tp", scatter_dimension=0, tiled=True
        ).astype(jnp.float32),
    )
    g1_f = full_g1.astype(jnp.float32)
    grad_in = (d_resid + norm_back(x_own, inv_rms(x_own), g1_f, dh1_own)).astype(jnp.bfloat16)
    summed = (
        lax.psum_scatter(grad_wq, "fsdp", scatter_dimension=0, tiled=True),
        lax.psum_scatter(grad_wkvb, "fsdp", scatter_dimension=0, tiled=True),
        lax.psum_scatter(grad_wo, "fsdp", scatter_dimension=1, tiled=True),
        lax.psum_scatter(grad_sgate, "fsdp", scatter_dimension=0, tiled=True),
        lax.psum_scatter(grad_sup, "fsdp", scatter_dimension=0, tiled=True),
        lax.psum_scatter(grad_sdown, "fsdp", scatter_dimension=1, tiled=True),
        lax.psum_scatter(sum_g1, "fsdp", scatter_dimension=0, tiled=True),
        lax.psum_scatter(sum_wkva, "fsdp", scatter_dimension=0, tiled=True),
        lax.psum_scatter(sum_gkv, "fsdp", scatter_dimension=0, tiled=True),
        lax.psum_scatter(sum_g2, "fsdp", scatter_dimension=0, tiled=True),
        lax.psum_scatter(sum_wr, "fsdp", scatter_dimension=0, tiled=True),
    )
    (
        out_wq,
        out_wkvb,
        out_wo,
        out_sgate,
        out_sup,
        out_sdown,
        out_g1,
        out_wkva,
        out_gkv,
        out_g2,
        out_wr,
    ) = summed
    return (
        hidden_out,
        grad_in,
        out_g1,
        out_wq,
        out_wkva,
        out_gkv,
        out_wkvb,
        out_wo,
        out_g2,
        out_wr,
        out_sgate,
        out_sup,
        out_sdown,
        grad_egate[None],
        expert_up_weight_gradient[None],
        grad_edown[None],
    )


RINGS_16 = (
    (0, 1, 3, 2, 6, 7, 5, 9, 13, 12, 14, 15, 11, 10, 8, 4),
    (0, 1, 5, 4, 6, 10, 14, 15, 13, 12, 8, 9, 11, 7, 3, 2),
    (0, 2, 6, 7, 3, 1, 5, 9, 13, 15, 11, 10, 14, 12, 8, 4),
)
VMEM_BYTES = 60 * 2**20
BF16 = jnp.bfloat16
F32 = jnp.float32
SLOTS = 3


def ring_orders(n):
    return RINGS_16 if n == 16 else (tuple(range(n)),) * 3


def lookup(values, index):
    words = []
    for k in range(0, len(values), 8):
        word = sum(v << (4 * j) for j, v in enumerate(values[k : k + 8]))
        words.append(word - (1 << 32) if word >= 1 << 31 else word)
    word = jnp.int32(words[0])
    for k in range(1, len(words)):
        word = jnp.where(index >= 8 * k, jnp.int32(words[k]), word)
    return lax.shift_right_logical(word, 4 * (index & 7)) & 15


def remote(src, dst, send, recv, device):
    return pltpu.make_async_remote_copy(
        src_ref=src,
        dst_ref=dst,
        send_sem=send,
        recv_sem=recv,
        device_id=device,
        device_id_type=pl.DeviceIdType.MESH,
    )


class Place:
    def __init__(self, n):
        self.n, self.half = n, n // 2
        self.me, self.t = lax.axis_index("fsdp"), lax.axis_index("tp")
        self.orders = ring_orders(n)
        self.spot = [
            lookup([order.index(k) for k in range(n)], self.me) for order in self.orders
        ]
        self.near = [[self.owner(r, 1), self.owner(r, n - 1)] for r in range(len(self.orders))]
        self.twin = (self.me, 1 - self.t)

    def owner(self, ring, offset):
        return lookup(self.orders[ring], lax.rem(self.spot[ring] + offset + self.n, self.n))

    def next(self, ring, way):
        return (self.near[ring][way], self.t)

    def enter(self, everyone=False):
        barrier = pltpu.get_barrier_semaphore()
        if everyone:

            def greet(k, _):
                there = lax.rem(self.me + k, self.n)
                pl.semaphore_signal(
                    barrier, 1, device_id=(there, self.t), device_id_type=pl.DeviceIdType.MESH
                )
                return 0

            lax.fori_loop(1, self.n, greet, 0)
            count = self.n - 1
        else:
            count = 0
            for ring in range(len(self.orders)):
                for way in range(2):
                    pl.semaphore_signal(
                        barrier,
                        1,
                        device_id=self.next(ring, way),
                        device_id_type=pl.DeviceIdType.MESH,
                    )
                    count += 1
        pl.semaphore_signal(barrier, 1, device_id=self.twin, device_id_type=pl.DeviceIdType.MESH)
        pl.semaphore_wait(barrier, count + 1)


def gather_sems(n):
    return pltpu.SemaphoreType.DMA((4, 2, n // 2 + 1))


class Gather:
    def __init__(self, place, ring, rows, source, target, sems, shared):
        self.place, self.ring, self.rows = place, ring, rows
        self.source, self.target, self.sems, self.shared = source, target, sems, shared

    def part(self, way, last):
        if not last:
            return 0, self.rows
        half = self.rows // 2
        return (0, half) if way == 0 else (half, self.rows - half)

    def offset(self, way, s):
        return -s if way == 0 else s

    def hop(self, way, s, last=False, first=False, owner=None):
        lo, rows = self.part(way, last)
        place = self.place
        if owner is None:
            owner = place.owner(self.ring, self.offset(way, s - 1))
        there = self.target(owner, lo, rows, place.t)
        here = self.source(lo, rows) if first else there
        return remote(
            here, there, self.sems.at[0, way, s], self.sems.at[1, way, s], place.next(self.ring, way)
        )

    def landed(self, way, s, last=False, owner=None):
        lo, rows = self.part(way, last)
        place = self.place
        if owner is None:
            owner = place.owner(self.ring, self.offset(way, s))
        there = self.target(owner, lo, rows, place.t)
        return remote(
            there, there, self.sems.at[0, way, s], self.sems.at[1, way, s], place.next(self.ring, way)
        )

    def across(self, way, s, t, last=False, first=False, owner=None):
        lo, rows = (0, self.rows) if first else self.part(way, last)
        place = self.place
        if owner is None:
            owner = place.me if first else place.owner(self.ring, self.offset(way, s))
        there = self.target(owner, lo, rows, t)
        here = self.source(lo, rows) if first else there
        return remote(here, there, self.sems.at[2, way, s], self.sems.at[3, way, s], place.twin)

    def own(self):
        return pltpu.make_async_copy(
            self.source(0, self.rows),
            self.target(self.place.me, 0, self.rows, self.place.t),
            self.sems.at[0, 0, 0],
        )

    def begin(self):
        for way in range(2):
            self.hop(way, 1, first=True).start()
        self.own().start()
        if self.shared:
            self.across(0, 0, self.place.t, first=True).start()

    def step(self, s, final=False):
        for way in range(2):
            owner = self.place.owner(self.ring, self.offset(way, s))
            self.landed(way, s, owner=owner).wait_recv()
            self.hop(way, s + 1, last=final, owner=owner).start()
            if self.shared:
                self.across(way, s, self.place.t, owner=owner).start()

    def close(self):
        half = self.place.half
        for way in range(2):
            self.landed(way, half, last=True).wait_recv()
            if self.shared:
                self.across(way, half, self.place.t, last=True).start()

    def settle(self):
        half = self.place.half
        self.own().wait()
        t = self.place.t
        if self.shared:
            self.across(0, 0, t, first=True).wait_send()
            self.across(0, 0, 1 - t, first=True).wait_recv()

        def each(s, _):
            for way in range(2):
                self.hop(way, s).wait_send()
                if self.shared:
                    self.across(way, s, t).wait_send()
                    self.across(way, s, 1 - t).wait_recv()
            return 0

        lax.fori_loop(1, half, each, 0)
        for way in range(2):
            self.hop(way, half, last=True).wait_send()
            if self.shared:
                self.across(way, half, t, last=True).wait_send()
                self.across(way, half, 1 - t, last=True).wait_recv()


def pump_gathers(gathers, half, s):
    if isinstance(s, int):
        s = jnp.int32(s)

    @pl.when(s < half - 1)
    def _():
        for g in gathers:
            g.step(s)

    @pl.when(s == half - 1)
    def _():
        for g in gathers:
            g.step(half - 1, final=True)

    @pl.when(s == half)
    def _():
        for g in gathers:
            g.close()


def pump_all(place, gathers, beside=(), late=None):
    for s, work in enumerate(beside):
        pump_gathers(gathers, place.half, s + 1)
        work()

    def each(s, _):
        for g in gathers:
            g.step(s)
        return 0

    lax.fori_loop(1 + len(beside), place.half - 1, each, 0)
    for g in gathers:
        g.step(place.half - 1, final=True)
    if late is not None:
        late()
    for g in gathers:
        g.close()


class Share:
    def __init__(self, place, own, pair, rows, mine, heap, sems, arrived):
        self.place, self.own, self.pair, self.rows = place, own, pair, rows
        self.mine, self.heap, self.sems, self.arrived = mine, heap, sems, arrived

    def keep(self, i, k):
        slot, own = lax.rem(i, 2), self.own
        return pltpu.make_async_copy(
            self.rows.at[slot, k, pl.ds(self.place.t * own, own)],
            self.mine.at[i * self.pair + k],
            self.sems.at[0, slot, k],
        )

    def give(self, i, k):
        slot, own, s = lax.rem(i, 2), self.own, i * self.pair + k
        return remote(
            self.rows.at[slot, k, pl.ds((1 - self.place.t) * own, own)],
            self.heap.at[s],
            self.sems.at[1, slot, k],
            self.arrived.at[s],
            self.place.twin,
        )

    def start(self, i):
        for k in range(self.pair):
            self.give(i, k).start()
            self.keep(i, k).start()

    def left(self, i):
        for k in range(self.pair):
            self.keep(i, k).wait()
            self.give(i, k).wait_send()

    def settle(self, steps):
        self.left(steps - 2)
        self.left(steps - 1)

        def each(i, _):
            for k in range(self.pair):
                self.give(i, k).wait_recv()
            return 0

        lax.fori_loop(0, steps, each, 0)


def share_scratch(n, pair, seq, width):
    return [
        pltpu.VMEM((2, pair, seq, width), BF16),
        pltpu.SemaphoreType.DMA((2, 2, pair)),
        pltpu.SemaphoreType.DMA((n,)),
    ]


class Bring:
    def __init__(self, pairs, sems):
        self.copies = [
            pltpu.make_async_copy(src, dst, sems.at[k]) for k, (src, dst) in enumerate(pairs)
        ]

    def begin(self):
        for copy in self.copies:
            copy.start()

    def wait(self):
        for copy in self.copies:
            copy.wait()


def room_for(arrays):
    return [pltpu.VMEM(a.shape, a.dtype) for a in arrays] + [
        pltpu.SemaphoreType.DMA((len(arrays),))
    ]


def scatter_scratch(n, rows, cols):
    return [
        pltpu.SemaphoreType.DMA((2, 2, n // 2 + 1)),
        pltpu.SemaphoreType.DMA((2, 2, n // 2 + 1)),
        pltpu.SemaphoreType.DMA((2, n)),
        pltpu.VMEM((2, SLOTS, rows, cols), BF16),
        pltpu.VMEM((2, SLOTS, rows, cols), BF16),
        pltpu.VMEM((2, n // 2, rows, cols), BF16),
    ]


def add_rows(target, sources, lo, rows, cols):
    most = max(16, (32768 // cols) // 16 * 16)
    size = min(most, rows)
    while rows % size:
        size -= 16

    def each(i, _):
        at = pl.ds(pl.multiple_of(lo + i * size, 16), size)
        total = sources[0][at, :].astype(F32)
        for source in sources[1:]:
            total = total + source[at, :].astype(F32)
        target[at, :] = total.astype(target.dtype)
        return 0

    lax.fori_loop(0, rows // size, each, 0)


class Scatter:
    def __init__(self, place, ring, shape, source, scratch, heap=None, given=False):
        self.place, self.ring, self.source, self.heap = place, ring, source, heap
        self.giving = heap is not None and not given
        self.rows, self.cols = shape
        self.sems, self.load_sems, self.give_sems, self.term, self.other, self.land = scratch

    def owner(self, way, s):
        half = self.place.half
        return self.place.owner(self.ring, half - s if way == 0 else half + s)

    def loads(self, way, s):
        slot = lax.rem(s, SLOTS)
        owner = self.owner(way, s)
        out = [
            pltpu.make_async_copy(
                self.source(owner, self.place.t),
                self.term.at[way, slot],
                self.load_sems.at[0, way, s],
            )
        ]
        if self.heap is not None:
            out.append(
                pltpu.make_async_copy(
                    self.heap(owner), self.other.at[way, slot], self.load_sems.at[1, way, s]
                )
            )
        return out

    def give(self, owner):
        return remote(
            self.source(owner, 1 - self.place.t),
            self.heap(owner),
            self.give_sems.at[0, owner],
            self.give_sems.at[1, owner],
            self.place.twin,
        )

    def push(self, s):
        if self.giving:
            for way in range(2):

                @pl.when((s <= self.place.half) if way == 0 else ((s > 0) & (s < self.place.half)))
                def _(way=way):
                    self.give(self.owner(way, s)).start()

    def fetch(self, s, ways=(0, 1), fresh=True):
        for way in ways:
            if self.giving and fresh:
                self.give(self.owner(way, s)).wait_recv()
            for copy in self.loads(way, s):
                copy.start()

    def part(self, way, first):
        if not first:
            return 0, self.rows
        half = self.rows // 2
        return (0, half) if way == 0 else (half, self.rows - half)

    def hop(self, way, s, first=False):
        lo, rows = self.part(way, first)
        at = pl.ds(lo, rows)
        return remote(
            self.term.at[way, lax.rem(s - 1, SLOTS), at, :],
            self.land.at[way, s - 1, at, :],
            self.sems.at[0, way, s],
            self.sems.at[1, way, s],
            self.place.next(self.ring, way),
        )

    def sources(self, way, s, *more):
        slot = lax.rem(s, SLOTS)
        out = [self.term.at[way, slot]]
        if self.heap is not None:
            out.append(self.other.at[way, slot])
        return out + list(more)

    def begin(self):
        if self.giving:
            self.push(0)
            self.push(1)
        self.fetch(0, ways=(0,))
        self.fetch(0, ways=(1,), fresh=False)

    def open(self):
        for way in range(2):
            for copy in self.loads(way, 0):
                copy.wait()
            if self.heap is not None:
                lo, rows = self.part(way, True)
                add_rows(self.term.at[way, 0], self.sources(way, 0), lo, rows, self.cols)
            self.hop(way, 1, first=True).start()

    def follow(self):
        if self.giving:

            def each(s, _):
                self.push(s)
                return 0

            lax.fori_loop(2, self.place.half + 1, each, 0)
        self.fetch(1)

    def step(self, s, first=False, second=False, final=False):
        for way in range(2):
            for copy in self.loads(way, s):
                copy.wait()
            self.hop(way, s, first=first).wait_recv()
            lo, rows = self.part(way, first)
            target = self.term.at[way, lax.rem(s, SLOTS)]
            landed = self.land.at[way, s - 1]
            add_rows(target, self.sources(way, s, landed), lo, rows, self.cols)
            if first and self.heap is not None:
                lo, rows = self.part(1 - way, first)
                add_rows(target, self.sources(way, s), lo, rows, self.cols)
            self.hop(way, s + 1).start()
        for way in range(2):
            if not first:
                self.hop(way, s - 1, first=second).wait_send()
            if not final or way == 0:
                self.fetch(s + 1, ways=(way,))

    def middle(self, s):
        half = self.place.half

        @pl.when(s == 2)
        def _():
            self.step(s, second=True)

        @pl.when((s > 2) & (s < half - 1))
        def _():
            self.step(s)

        @pl.when(s == half - 1)
        def _():
            self.step(s, final=True)

    def close(self, out):
        half = self.place.half
        for copy in self.loads(0, half):
            copy.wait()
        for way in range(2):
            self.hop(way, half).wait_recv()
        last = [self.land.at[way, half - 1] for way in range(2)]
        add_rows(out, self.sources(0, half, *last), 0, self.rows, self.cols)
        for way in range(2):
            self.hop(way, half - 1).wait_send()
            self.hop(way, half).wait_send()
        if self.giving:

            def given(k, _):
                self.give(k).wait_send()
                return 0

            lax.fori_loop(0, self.place.n, given, 0)


def open_scatters(scatters):
    for s in scatters:
        s.begin()
    for s in scatters:
        s.open()
    for s in scatters:
        s.follow()


def step_scatters(place, scatters, s):
    if isinstance(s, int):
        s = jnp.int32(s)

    @pl.when(s == 1)
    def _():
        for one in scatters:
            one.step(1, first=True)

    @pl.when((s > 1) & (s < place.half))
    def _():
        for one in scatters:
            one.middle(s)


def run_scatters(place, scatters, outs, beside=()):
    open_scatters(scatters)
    for s, work in enumerate(beside):
        step_scatters(place, scatters, s + 1)
        work()

    def each(s, _):
        step_scatters(place, scatters, s)
        return 0

    lax.fori_loop(1 + len(beside), place.half, each, 0)
    for s, out in zip(scatters, outs):
        s.close(out)


class Trade:
    def __init__(self, place, sources, targets, sems):
        self.place, self.sources, self.targets, self.sems = place, sources, targets, sems

    def copies(self, k, coming=False):
        place = self.place
        there = lax.rem(place.me + k, place.n)
        back = lax.rem(place.me + place.n - k, place.n)
        return [
            remote(
                source(there),
                target(back if coming else place.me),
                self.sems.at[0, k, j],
                self.sems.at[1, k, j],
                (there, place.t),
            )
            for j, (source, target) in enumerate(zip(self.sources, self.targets))
        ]

    def own(self):
        me = self.place.me
        return [
            pltpu.make_async_copy(source(me), target(me), self.sems.at[0, 0, j])
            for j, (source, target) in enumerate(zip(self.sources, self.targets))
        ]

    def begin(self):
        def each(k, _):
            for copy in self.copies(k):
                copy.start()
            return 0

        lax.fori_loop(1, self.place.n, each, 0)
        for copy in self.own():
            copy.start()

    def settle(self):
        def each(k, _):
            for copy in self.copies(k):
                copy.wait_send()
            for copy in self.copies(k, coming=True):
                copy.wait_recv()
            return 0

        lax.fori_loop(1, self.place.n, each, 0)
        for copy in self.own():
            copy.wait()


def comm_call(kernel, out_shape, out_specs, in_specs, scratch, ident, name):
    return pl.pallas_call(
        kernel,
        out_shape=out_shape,
        in_specs=in_specs,
        out_specs=out_specs,
        scratch_shapes=scratch,
        compiler_params=pltpu.CompilerParams(
            collective_id=ident, has_side_effects=True, vmem_limit_bytes=VMEM_BYTES
        ),
        name=name,
    )


IN_HBM = pl.BlockSpec(memory_space=pl.ANY)
IN_VMEM = pl.BlockSpec(memory_space=pltpu.VMEM)


def thirds(width):
    tiles = width // 128
    cuts = [0, tiles // 3, 2 * tiles // 3, tiles]
    return [(128 * lo, 128 * (hi - lo)) for lo, hi in zip(cuts, cuts[1:])]


def pick(flat):
    flat = list(flat)

    def take(count):
        head, flat[:] = flat[:count], flat[count:]
        return head

    return take


def dot_tn(left, right):
    return lax.dot_general(left, right, (((0,), (0,)), ((), ())), preferred_element_type=F32)


def dot_nt(left, right):
    return lax.dot_general(left, right, (((1,), (1,)), ((), ())), preferred_element_type=F32)


def whole(array):
    zeros = (0,) * array.ndim
    return pl.BlockSpec(array.shape, lambda i: zeros, pipeline_mode=pl.Buffered(1))


def by_cols(rows, cols):
    return pl.BlockSpec((rows, cols), lambda i: (0, i))


def by_rows(rows, cols):
    return pl.BlockSpec((rows, cols), lambda i: (i, 0))


def by_seq(*block):
    rest = (0,) * (len(block) - 1)
    return pl.BlockSpec(block, lambda i: (i,) + rest)


def eye(size):
    same = lax.broadcasted_iota(jnp.int32, (size, size), 0) == lax.broadcasted_iota(
        jnp.int32, (size, size), 1
    )
    return same.astype(F32).astype(BF16)


def sds(shape, dtype):
    return jax.ShapeDtypeStruct(shape, dtype)


def grid_call(kernel, steps, in_specs, out, scratch, ident, name):
    return pl.pallas_call(
        kernel,
        grid=(steps,),
        in_specs=in_specs,
        out_specs=tuple(spec for spec, _, _ in out),
        out_shape=tuple(sds(shape, dtype) for _, shape, dtype in out),
        scratch_shapes=scratch,
        compiler_params=pltpu.CompilerParams(
            collective_id=ident, has_side_effects=True, vmem_limit_bytes=63 * 2**20
        ),
        name=name,
    )


GAIN_ATTN, GAIN_FFN, GAIN_KV, TABLES = 16, 17, 18, 32


def row_gathers(place, chunks, sems, source, target, own):
    t = place.t
    return [
        Gather(
            place, ring, rows,
            lambda lo, r, b=b, c0=c0, w=w: source(pl.ds(b + lo, r), pl.ds(c0, w)),
            lambda o, lo, r, u, b=b, c0=c0, w=w: target(
                o, pl.ds(u * own + b + lo, r), pl.ds(c0, w)
            ),
            sems[k], True,
        )
        for k, (ring, b, rows, c0, w) in enumerate(chunks)
    ]


def row_scatters(place, chunks, scratch, mine, heap):
    return [
        Scatter(
            place, ring, (rows, w),
            lambda o, u, c0=c0, w=w: mine.at[o, :, pl.ds(c0, w)],
            scratch[k],
            lambda o, c0=c0, w=w: heap.at[o, :, pl.ds(c0, w)],
            given=True,
        )
        for k, (ring, _, rows, c0, w) in enumerate(chunks)
    ]


def row_cuts(rows, width):
    return [(ring, 0, rows, c0, w) for ring, (c0, w) in enumerate(thirds(width))]


def collect_inputs(
    n, query, kvd, kvu, outp, x, norm_attn, norm_ffn, kv_norm, router, routes, s_gate, s_up, s_down
):
    own, width = x.shape
    seq = 2 * own
    q_rows, q_cols = query.shape
    cut = q_cols // 4 * 3
    d_rows, cols = kvd.shape[0] // 2, kvd.shape[1]
    o_rows = outp.shape[0]
    u_rows = kvu.shape[0]
    hidden = s_down.shape[0] // n
    padded = -(-hidden // 16) * 16
    small_rows = TABLES + 2 * n

    def kernel(*refs):
        take = pick(refs)
        q, kd, ku, wo, xin, na, nf, nk, ro, rt, sg, su, sd = take(13)
        q_all, kd_all, ku_all, wo_all, sm_all, x_all, blocks = take(7)
        sems = take(6)
        x_sems, sm, turned = take(3)
        place = Place(n)
        t = place.t
        place.enter()

        def of_q(ring, c0, w):
            return Gather(
                place, ring, q_rows,
                lambda lo, r: q.at[pl.ds(lo, r), pl.ds(c0, w)],
                lambda o, lo, r, _: q_all.at[pl.ds(o * q_rows + lo, r), pl.ds(c0, w)],
                sems[ring], False,
            )

        gathers = [
            of_q(0, 0, cut),
            of_q(1, cut, q_cols - cut),
            Gather(
                place, 2, o_rows,
                lambda lo, r: wo.at[pl.ds(lo, r)],
                lambda o, lo, r, _: wo_all.at[pl.ds(lo, r), pl.ds(o * cols, cols)],
                sems[5], False,
            ),
            Gather(
                place, 1, u_rows,
                lambda lo, r: ku.at[pl.ds(lo, r)],
                lambda o, lo, r, _: ku_all.at[pl.ds(o * u_rows + lo, r)],
                sems[2], False,
            ),
            Gather(
                place, 1, d_rows,
                lambda lo, r: kd.at[pl.ds(t * d_rows + lo, r)],
                lambda o, lo, r, u: kd_all.at[pl.ds(u * d_rows + lo, r), pl.ds(o * cols, cols)],
                sems[3], True,
            ),
            Gather(
                place, 2, small_rows,
                lambda lo, r: sm.at[pl.ds(lo, r)],
                lambda o, lo, r, _: sm_all.at[o, pl.ds(lo, r)],
                sems[4], False,
            ),
        ]
        for g in gathers[:-1]:
            g.begin()
        mine = x_all.at[pl.ds(t * own, own)]
        x_own = pltpu.make_async_copy(xin, mine, x_sems.at[0])
        x_give = remote(xin, mine, x_sems.at[1], x_sems.at[2], place.twin)
        theirs = x_all.at[pl.ds((1 - t) * own, own)]
        x_take = remote(xin, theirs, x_sems.at[1], x_sems.at[2], place.twin)
        x_own.start()
        x_give.start()

        sm[...] = jnp.zeros_like(sm)
        sm[0:n, :] = ro[...]
        gains = jnp.concatenate(
            [
                na[...].astype(F32),
                nf[...].astype(F32),
                jnp.concatenate(
                    [nk[...].astype(F32), jnp.zeros((1, cols - nk.shape[1]), F32)], 1
                ),
                jnp.zeros((TABLES - GAIN_KV - 1, cols), F32),
            ],
            0,
        )
        sm[GAIN_ATTN:TABLES, :] = gains.astype(BF16)
        ids = lax.broadcasted_iota(jnp.int32, (n, seq), 0)
        chosen = jnp.zeros((n, seq), F32)
        for k in range(TOP):
            chosen = jnp.where(ids == rt[k : k + 1, :], 1.0, chosen)
        table = chosen.astype(BF16)
        sm[TABLES : TABLES + n, :] = table[:, :own]
        sm[TABLES + n : TABLES + 2 * n, :] = table[:, own:]
        gathers[-1].begin()

        def cut_slices(j, w):
            if j < 2:
                turned[...] = dot_tn(w[...], eye(cols))
            else:
                turned[...] = w[...].astype(F32)
            for k in range(n):
                blocks[k, j, 0:hidden, :] = turned[k * hidden : (k + 1) * hidden, :].astype(BF16)
                if padded > hidden:
                    blocks[k, j, hidden:padded, :] = jnp.zeros((padded - hidden, cols), BF16)

        beside = [lambda j=j, w=w: cut_slices(j, w) for j, w in enumerate((sg, su, sd))]
        pump_all(place, gathers, beside)
        x_own.wait()
        x_give.wait_send()
        x_take.wait_recv()
        for g in gathers:
            g.settle()

    return comm_call(
        kernel,
        (
            sds((n * q_rows, q_cols), BF16),
            sds((kvd.shape[0], n * cols), BF16),
            sds((n * u_rows, kvu.shape[1]), BF16),
            sds((o_rows, n * cols), BF16),
            sds((n, small_rows, cols), BF16),
            sds((seq, width), BF16),
            sds((n, 3, padded, cols), BF16),
        ),
        (IN_HBM,) * 6 + (IN_VMEM,),
        [IN_HBM] * 5 + [IN_VMEM] * 8,
        [gather_sems(n)] * 6
        + [
            pltpu.SemaphoreType.DMA((3,)),
            pltpu.VMEM((small_rows, cols), BF16),
            pltpu.VMEM((n * hidden, cols), F32),
        ],
        1,
        "collect_inputs",
    )(query, kvd, kvu, outp, x, norm_attn, norm_ffn, kv_norm, router, routes, s_gate, s_up, s_down)


def swapped(v):
    half_width = v.shape[1] // 2
    return jnp.concatenate([v[:, half_width:], v[:, :half_width]], 1)


def causal_weights(q_n, q_r, k_n, k_r, factor):
    raw = (dot_nt(q_n, k_n) + dot_nt(q_r, k_r)) * factor
    length = raw.shape[0]
    ahead = lax.broadcasted_iota(jnp.int32, (length, length), 0) >= lax.broadcasted_iota(
        jnp.int32, (length, length), 1
    )
    raw = jnp.where(ahead, raw, -1e30)
    top = jnp.max(raw, axis=1, keepdims=True)
    up = jnp.exp(raw - top)
    return up / jnp.sum(up, axis=1, keepdims=True)


def attend(n, x_seq, x_own, small_all, w_kvd, cos2, sin2, w_q, w_kvu, w_out, blocks):
    seq, width = x_seq.shape
    own = seq // 2
    head = DN + DR
    pairs = w_q.shape[1] // (2 * head)
    factor = 1.0 / math.sqrt(head)
    cols = width // n
    padded = blocks.shape[2]
    kv_cols = KVR // n
    part_rows = 128

    def kernel(*refs):
        take = pick(refs)
        x, xo, sm, wd, co, si, wq, wu, wo, bl = take(10)
        resid, sel_out, g2, wr, h_own, gates, h1, g1, gk, lat, cn, kpe, sw, qn, qr, kv, ctx = take(17)
        trade_sems, got, part, theirs, swap_sems = take(5)
        place = Place(n)
        t, me = place.t, place.me
        i = pl.program_id(0)
        trade = Trade(place, [lambda k: bl.at[k]], [lambda k: got.at[k]], trade_sems)

        @pl.when(i == 0)
        def _():
            place.enter(everyone=True)
            trade.begin()
            for o in range(n):
                at = slice(o * cols, (o + 1) * cols)
                g1[:, at] = sm[o, GAIN_ATTN : GAIN_ATTN + 1, :].astype(F32)
                g2[:, at] = sm[o, GAIN_FFN : GAIN_FFN + 1, :].astype(F32)
                wr[:, at] = sm[o, 0:n, :]
                gk[:, o * kv_cols : (o + 1) * kv_cols] = sm[
                    o, GAIN_KV : GAIN_KV + 1, 0:kv_cols
                ].astype(F32)
            size = 16

            def norm_rows(j, _):
                at = pl.ds(pl.multiple_of(j * size, size), size)
                v = x[at, :].astype(F32)
                h1[at, :] = (v * inv_rms(v) * g1[...]).astype(BF16)
                return 0

            lax.fori_loop(0, seq // size, norm_rows, 0)
            first = dot_nt(h1[...], wd[...])
            latent = first[:, :KVR]
            lat[...] = latent
            cn[...] = (latent * inv_rms(latent) * gk[...]).astype(BF16)
            rope = first[:, KVR:]
            kpe[...] = (rope * co[...] + swapped(rope) * si[...]).astype(BF16)

        q_raw = dot_single_float(h1[...], wq[...])
        kv[...] = dot_single_float(cn[...], wu[...]).astype(BF16)
        for k in range(2):
            q_n = q_raw[:, k * head : k * head + DN].astype(BF16)
            rope = q_raw[:, k * head + DN : (k + 1) * head]
            q_r = (rope * co[...] + swapped(rope) * si[...]).astype(BF16)
            qn[:, k * DN : (k + 1) * DN] = q_n
            qr[:, k * DR : (k + 1) * DR] = q_r
            base = k * (DN + DV)
            weights = causal_weights(q_n, q_r, kv[:, base : base + DN], kpe[...], factor)
            one = dot_single_float(weights.astype(BF16), kv[:, base + DN : base + DN + DV])
            ctx[:, k * DV : (k + 1) * DV] = one.astype(BF16)
        more = dot_single_float(ctx[...], wo[...])

        @pl.when(i == 0)
        def _():
            part[...] = more

        @pl.when(i > 0)
        def _():
            part[...] += more

        @pl.when(i == pairs - 1)
        def _():
            swap = remote(
                part.at[pl.ds((1 - t) * own, own)],
                theirs,
                swap_sems.at[0],
                swap_sems.at[1],
                place.twin,
            )
            swap.start()
            swap.wait_recv()
            size = 16

            def norm_rows(j, _):
                at = pl.ds(pl.multiple_of(j * size, size), size)
                mine = pl.ds(pl.multiple_of(t * own + j * size, size), size)
                v = xo[at, :].astype(F32) + (part[mine, :] + theirs[at, :])
                resid[at, :] = v
                h_own[at, :] = (v * inv_rms(v) * g2[...]).astype(BF16)
                return 0

            lax.fori_loop(0, own // size, norm_rows, 0)
            logits = dot_nt(wr[...], h_own[...])
            chosen = sm[me, pl.ds(pl.multiple_of(TABLES + t * n, 16), n), :].astype(F32)
            sel = jnp.where(chosen > 0.5, 1.0 / (1.0 + jnp.exp(-logits)), 0.0)
            sel_out[...] = sel
            gate = ROUTE_SCALE * sel / jnp.sum(sel, axis=0, keepdims=True)
            high = gate.astype(BF16)
            gates[0:n, :] = high
            gates[n : 2 * n, :] = (gate - high.astype(F32)).astype(BF16)
            swap.wait_send()
            trade.settle()
            sw[...] = jnp.zeros_like(sw)
            for o in range(n):
                for j in range(3):
                    sw[j * part_rows : j * part_rows + padded, o * cols : (o + 1) * cols] = got[o, j]

    heads = 2 * pairs
    return grid_call(
        kernel,
        pairs,
        [whole(a) for a in (x_seq, x_own, small_all, w_kvd, cos2, sin2)]
        + [by_cols(width, 2 * head), by_cols(KVR, 2 * (DN + DV)), by_rows(2 * DV, width), IN_HBM],
        (
            (IN_VMEM, (own, width), F32),
            (IN_VMEM, (n, own), F32),
            (IN_VMEM, (1, width), F32),
            (IN_VMEM, (n, width), BF16),
            (IN_VMEM, (own, width), BF16),
            (IN_VMEM, (2 * n, own), BF16),
            (IN_VMEM, (seq, width), BF16),
            (IN_VMEM, (1, width), F32),
            (IN_VMEM, (1, KVR), F32),
            (IN_VMEM, (seq, KVR), F32),
            (IN_VMEM, (seq, KVR), BF16),
            (IN_VMEM, (seq, DR), BF16),
            (IN_VMEM, (3 * part_rows, width), BF16),
            (by_cols(seq, 2 * DN), (seq, heads * DN), BF16),
            (by_cols(seq, 2 * DR), (seq, heads * DR), BF16),
            (by_cols(seq, 2 * (DN + DV)), (seq, heads * (DN + DV)), BF16),
            (by_cols(seq, 2 * DV), (seq, heads * DV), BF16),
        ),
        [
            pltpu.SemaphoreType.DMA((2, n, 1)),
            pltpu.VMEM(blocks.shape, BF16),
            pltpu.VMEM((seq, width), F32),
            pltpu.VMEM((own, width), F32),
            pltpu.SemaphoreType.DMA((2,)),
        ],
        2,
        "attend",
    )(x_seq, x_own, small_all, w_kvd, cos2, sin2, w_q, w_kvu, w_out, blocks)


PAIR = 2


def expert_forward(n, h_own, gates, small_all, cap, w_gate, w_up, w_down, shared_w, cot):
    own, width = h_own.shape
    seq = 2 * own
    hidden, part = w_gate.shape[0], shared_w.shape[0] // 3
    steps = n // PAIR
    chunks = row_cuts(own, width)

    def kernel(*refs):
        take = pick(refs)
        ho, go, sm, *far, ct = take(8)
        rows, act, act_gate, on_up, on_gate, s_act, s_on, gate = take(8)
        pm, out_mine, out_heap, ct_all, h_all, gate_all = take(6)
        sems, row_sems = take(len(chunks)), take(len(chunks) + 1)
        named, h, ga, h_sems, ga_sem = take(5)
        orows, *near, bring_sems = take(6)
        out_rows, share_sems, arrived = take(3)
        wg, wu, wd, sw = near
        place = Place(n)
        t, me = place.t, place.me
        i = pl.program_id(0)
        gathers = row_gathers(
            place, chunks, sems,
            lambda r, c: ct.at[pl.ds(t * own + r.start, r.size), c],
            lambda o, r, c: ct_all.at[o, r, c], own,
        )

        spread = row_gathers(
            place, chunks, row_sems,
            lambda r, c: ho.at[r, c], lambda o, r, c: h_all.at[o, r, c], own,
        )
        spread.append(
            Gather(
                place, 0, 2 * n,
                lambda lo, r: go.at[pl.ds(lo, r)],
                lambda o, lo, r, u: gate_all.at[o, u, pl.ds(lo, r)],
                row_sems[len(chunks)], True,
            )
        )

        def fetch(step):
            slot = lax.rem(step, 2)
            return pltpu.make_async_copy(
                h_all.at[pl.ds(step * PAIR, PAIR)], h.at[slot], h_sems.at[slot]
            )

        def lay_table():
            mine = lax.broadcasted_iota(jnp.int32, (n, own), 0) == me
            for s in range(n):
                for u in range(2):
                    one = sm[s, TABLES + u * n : TABLES + (u + 1) * n, :].astype(F32)
                    one = jnp.sum(jnp.where(mine, one, 0.0), axis=0, keepdims=True)
                    named[s : s + 1, u * own : (u + 1) * own] = one

        def fill(first, last):
            below = lax.broadcasted_iota(jnp.int32, (seq, seq), 0) <= lax.broadcasted_iota(
                jnp.int32, (seq, seq), 1
            )
            below = below.astype(F32).astype(BF16)
            count = dot_single_float(named[...].astype(BF16), below) - 1.0
            slots = lax.broadcasted_iota(jnp.int32, (cap, seq), 0).astype(F32)
            for s in range(first, last):
                here = (count[s : s + 1, :] == slots) & (named[s : s + 1, :] > 0.5)
                pm[s] = here.astype(F32).astype(BF16)

        bring = Bring(list(zip(far, near)), bring_sems)
        share = Share(place, own, PAIR, out_rows, out_mine, out_heap, share_sems, arrived)

        @pl.when(i == 0)
        def _():
            place.enter()
            for one in spread:
                one.begin()
            bring.begin()
            quarter = n // 4
            beside = [lay_table] + [
                lambda q=q: fill(q * quarter, (q + 1) * quarter if q < 3 else n) for q in range(4)
            ]
            pump_all(place, spread, beside, lambda: [one.begin() for one in gathers])
            for one in spread:
                one.settle()
            copy = pltpu.make_async_copy(gate_all, ga, ga_sem)
            copy.start()
            fetch(0).start()
            copy.wait()

        fetch(i).wait()

        @pl.when(i + 1 < steps)
        def _():
            fetch(i + 1).start()

        @pl.when(i > 1)
        def _():
            share.left(i - 2)

        @pl.when(i > 0)
        def _():
            pump_gathers(gathers[:1], place.half, i)

        turn = lax.rem(i, 2)
        slots = []
        line = lax.broadcasted_iota(jnp.int32, (2 * n, own), 0)
        mine = (line == me) | (line == me + n)
        for k in range(PAIR):
            halves = [
                jnp.sum(jnp.where(mine, ga[i * PAIR + k, u].astype(F32), 0.0), axis=0, keepdims=True)
                for u in range(2)
            ]
            gate[k] = jnp.concatenate(halves, 1)
            rows[pl.ds(k * cap, cap), :] = dot_single_float(pm[i * PAIR + k], h[turn, k]).astype(BF16)
            slots.append(jnp.sum(pm[i * PAIR + k].astype(F32) * gate[k], axis=1, keepdims=True))
        pl.when(i == 0)(bring.wait)
        pre = dot_nt(rows[...], wg[...])

        @pl.when(i > 0)
        def _():
            pump_gathers(gathers[1:2], place.half, i)

        up = dot_nt(rows[...], wu[...])
        sigm = jax.nn.sigmoid(pre)
        silu = pre * sigm
        gs = jnp.concatenate(slots, 0)
        plain = silu * up
        act[...] = plain.astype(BF16)
        act_gate[...] = (plain * gs).astype(BF16)
        on_up[...] = silu.astype(BF16)
        on_gate[...] = (up * (sigm * (1.0 + pre * (1.0 - sigm)))).astype(BF16)
        orows[...] = dot_single_float(act_gate[...], wd[...]).astype(BF16)

        @pl.when(i > 0)
        def _():
            pump_gathers(gathers[2:], place.half, i)

        for k in range(PAIR):
            at = pl.ds(k * seq, seq)
            both = dot_nt(h[turn, k], sw[0 : 2 * part, :])
            s_pre, s_up = both[:, :part], both[:, part:]
            sigm = jax.nn.sigmoid(s_pre)
            silu = s_pre * sigm
            s_act[at, :] = (silu * s_up).astype(BF16)
            s_on[at, 0:part] = (s_up * (sigm * (1.0 + s_pre * (1.0 - sigm)))).astype(BF16)
            s_on[at, part:] = silu.astype(BF16)
            out_rows[turn, k] = (
                dot_tn(pm[i * PAIR + k], orows[pl.ds(k * cap, cap), :])
                + dot_single_float(s_act[at, :], sw[2 * part :, :])
            ).astype(BF16)
        share.start(i)

        @pl.when(i == steps - 1)
        def _():
            for one in gathers:
                one.close()
            for one in gathers:
                one.settle()
            share.settle(steps)

    return grid_call(
        kernel,
        steps,
        [IN_HBM, IN_HBM, whole(small_all)] + [IN_HBM] * 5,
        (
            (by_rows(PAIR * cap, width), (n * cap, width), BF16),
            (by_rows(PAIR * cap, hidden), (n * cap, hidden), BF16),
            (by_rows(PAIR * cap, hidden), (n * cap, hidden), BF16),
            (by_rows(PAIR * cap, hidden), (n * cap, hidden), BF16),
            (by_rows(PAIR * cap, hidden), (n * cap, hidden), BF16),
            (by_rows(PAIR * seq, part), (n * seq, part), BF16),
            (by_rows(PAIR * seq, 2 * part), (n * seq, 2 * part), BF16),
            (by_seq(PAIR, 1, seq), (n, 1, seq), F32),
            (IN_VMEM, (n, cap, seq), BF16),
            (IN_HBM, (n, own, width), BF16),
            (IN_HBM, (n, own, width), BF16),
            (IN_HBM, (n, seq, width), BF16),
            (IN_HBM, (n, seq, width), BF16),
            (IN_HBM, (n, 2, 2 * n, own), BF16),
        ),
        [gather_sems(n)] * (2 * len(chunks) + 1)
        + [
            pltpu.VMEM((n, seq), F32),
            pltpu.VMEM((2, PAIR, seq, width), BF16),
            pltpu.VMEM((n, 2, 2 * n, own), BF16),
            pltpu.SemaphoreType.DMA((2,)),
            pltpu.SemaphoreType.DMA,
        ]
        + [pltpu.VMEM((PAIR * cap, width), BF16)]
        + room_for((w_gate, w_up, w_down, shared_w))
        + share_scratch(n, PAIR, seq, width),
        4,
        "expert_forward",
    )(h_own, gates, small_all, w_gate, w_up, w_down, shared_w, cot)


def expert_back(
    out_mine, out_heap, resid, cot_all, place_table, gate, act, on_up, on_gate, s_on,
    w_gate, w_up, w_down, shared_w,
):
    n, seq, width = cot_all.shape
    own = seq // 2
    cap, hidden, part = place_table.shape[1], w_gate.shape[0], shared_w.shape[0] // 3
    steps = n // PAIR
    chunks = row_cuts(own, width)

    def kernel(*refs):
        take = pick(refs)
        p, heap, res, ct, pm, gt, ac, ou, og, so, *far = take(14)
        out, dh_mine, dh_heap, cr, dge, due, d_spre, dgt = take(8)
        scratch = [take(6) for _ in chunks]
        total, dr, *near, bring_sems = take(7)
        wg, wu, wd, sw = near
        dh_rows, share_sems, arrived = take(3)
        place = Place(n)
        me = place.me
        i = pl.program_id(0)
        scatters = row_scatters(place, chunks, scratch, p, heap)
        share = Share(place, own, PAIR, dh_rows, dh_mine, dh_heap, share_sems, arrived)

        bring = Bring(list(zip(far, near)), bring_sems)

        @pl.when(i == 0)
        def _():
            place.enter()
            bring.begin()
            open_scatters(scatters)

        @pl.when(i > 0)
        def _():
            step_scatters(place, scatters, i)

        @pl.when(i > 1)
        def _():
            share.left(i - 2)

        slots = []
        for k in range(PAIR):
            cr[pl.ds(k * cap, cap), :] = dot_single_float(pm[k], ct[k]).astype(BF16)
            slots.append(jnp.sum(pm[k].astype(F32) * gt[k], axis=1, keepdims=True))
        gs = jnp.concatenate(slots, 0)
        pl.when(i == 0)(bring.wait)
        plain_da = dot_nt(cr[...], wd[...])
        dgs = jnp.sum(plain_da * ac[...].astype(F32), axis=1, keepdims=True)
        da = plain_da * gs
        dge[...] = (da * og[...].astype(F32)).astype(BF16)
        due[...] = (da * ou[...].astype(F32)).astype(BF16)
        dr[...] = (
            dot_single_float(dge[...], wg[...]) + dot_single_float(due[...], wu[...])
        ).astype(BF16)
        line = lax.broadcasted_iota(jnp.int32, (2 * n, own), 0)
        for k in range(PAIR):
            at = pl.ds(k * cap, cap)
            s_at = pl.ds(k * seq, seq)
            ds = dot_nt(ct[k], sw[2 * part :, :])
            d_spre[s_at, 0:part] = (ds * so[s_at, 0:part].astype(F32)).astype(BF16)
            d_spre[s_at, part:] = (ds * so[s_at, part:].astype(F32)).astype(BF16)
            dh_rows[lax.rem(i, 2), k] = (
                dot_tn(pm[k], dr[at, :])
                + dot_single_float(d_spre[s_at, :], sw[0 : 2 * part, :])
            ).astype(BF16)
            dg = jnp.sum(pm[k].astype(F32) * dgs[k * cap : (k + 1) * cap], axis=0, keepdims=True)
            for u in range(2):
                one = dg[:, u * own : (u + 1) * own]
                high = one.astype(BF16).astype(F32)
                both = jnp.where(line == me, high, jnp.where(line == me + n, one - high, 0.0))
                dgt[k, u] = both.astype(BF16)
        share.start(i)

        @pl.when(i == steps - 1)
        def _():
            share.settle(steps)
            for s, (_, b, rows, c0, w) in zip(scatters, chunks):
                s.close(total.at[pl.ds(b, rows), pl.ds(c0, w)])
            add_rows(out, [total, res], 0, own, width)

    scratch = []
    for _, _, size, _, w in chunks:
        scratch += scatter_scratch(n, size, w)
    scratch += [
        pltpu.VMEM((own, width), F32),
        pltpu.VMEM((PAIR * cap, width), BF16),
    ] + room_for((w_gate, w_up, w_down, shared_w))
    scratch += share_scratch(n, PAIR, seq, width)
    return grid_call(
        kernel,
        steps,
        [IN_HBM, IN_HBM, whole(resid), by_seq(PAIR, seq, width), by_seq(PAIR, cap, seq)]
        + [by_seq(PAIR, 1, seq)]
        + [by_rows(PAIR * cap, hidden)] * 3
        + [by_rows(PAIR * seq, 2 * part)]
        + [IN_HBM] * 4,
        (
            (IN_VMEM, (own, width), BF16),
            (IN_HBM, (n, own, width), BF16),
            (IN_HBM, (n, own, width), BF16),
            (by_rows(PAIR * cap, width), (n * cap, width), BF16),
            (by_rows(PAIR * cap, hidden), (n * cap, hidden), BF16),
            (by_rows(PAIR * cap, hidden), (n * cap, hidden), BF16),
            (by_rows(PAIR * seq, 2 * part), (n * seq, 2 * part), BF16),
            (by_seq(PAIR, 2, 2 * n, own), (n, 2, 2 * n, own), BF16),
        ),
        scratch,
        5,
        "expert_back",
    )(
        out_mine, out_heap, resid, cot_all, place_table, gate, act, on_up, on_gate, s_on,
        w_gate, w_up, w_down, shared_w,
    )


def sum_rows(
    dh_mine, dh_heap, gate_parts, sel, router_t, resid, gain, cot, normed_own,
    rows, dy, act, dge, due, s_act, d_spre, h_all, cot_all,
):
    n, seq, width = cot_all.shape
    own = seq // 2
    chunks = row_cuts(own, width)
    hidden, part = act.shape[1], s_act.shape[1]
    steps = n // 2
    cols = width // steps
    slots = rows.shape[0]

    def kernel(*refs):
        take = pick(refs)
        p, heap, gp, se, wr, res, g, gr, hn = take(9)
        r_in, y_in, *far, h_in, c_in = take(9)
        g2_out, wr_out, d_resid, d_attn, gate_heap = take(5)
        g_gate, g_up, g_down, g_shared = take(4)
        scratch = [take(6) for _ in range(len(chunks) + 1)]
        dg, ex_sems, dh, swap, gr_own, hn_own, *near, bring_sems = take(12)
        a_in, ge_in, ue_in, sa_in, sp_in = near
        place = Place(n)
        t = place.t
        i = pl.program_id(0)
        scatters = row_scatters(place, chunks, scratch, p, heap)
        gates = Scatter(
            place, 1, (2 * n, own), lambda o, u: gp.at[o, u], scratch[-1],
            lambda o: gate_heap.at[o],
        )
        bring = Bring(
            list(zip(far, near)) + [(gr.at[pl.ds(t * own, own)], gr_own), (hn, hn_own)], bring_sems
        )

        @pl.when(i == 0)
        def _():
            place.enter()
            bring.begin()
            open_scatters(scatters + [gates])
            bring.wait()

        @pl.when(i > 0)
        def _():
            step_scatters(place, scatters + [gates], i)

        g_gate[...] = dot_tn(ge_in[...], r_in[...]).astype(g_gate.dtype)
        g_up[...] = dot_tn(ue_in[...], r_in[...]).astype(g_up.dtype)

        g_down[...] = dot_tn(a_in[...], y_in[...]).astype(g_down.dtype)
        g_shared[0 : 2 * part, :] = dot_tn(sp_in[...], h_in[...]).astype(BF16)
        g_shared[2 * part :, :] = dot_tn(sa_in[...], c_in[...]).astype(BF16)

        @pl.when(i == steps - 1)
        def _():
            for s, (_, b, r, c0, w) in zip(scatters, chunks):
                s.close(dh.at[pl.ds(b, r), pl.ds(c0, w)])
            gates.close(dg)
            dgate = dg[0:n, :] + dg[n : 2 * n, :]
            s = se[...]
            total = jnp.sum(s, axis=0, keepdims=True)
            dsel = ROUTE_SCALE * (
                dgate / total - jnp.sum(dgate * s, axis=0, keepdims=True) / (total * total)
            )
            dl = (dsel * s * (1.0 - s)).astype(BF16)
            wr_out[...] = dot_single_float(dl, hn_own[...])
            dh[...] += dot_tn(dl, wr[...])
            size = 16

            def rows_back(j, acc):
                at = pl.ds(pl.multiple_of(j * size, size), size)
                mine = pl.ds(pl.multiple_of(t * own + j * size, size), size)
                v = res[at, :]
                r, one = inv_rms(v), dh[at, :]
                out = gr_own[at, :].astype(F32) + norm_back(v, r, g[...], one)
                d_resid[at, :] = out
                d_attn[mine, :] = out.astype(BF16)
                swap[0, at, :] = out.astype(BF16)
                return acc + jnp.sum(one * (v * r), axis=0, keepdims=True)

            g2_out[...] = lax.fori_loop(0, own // size, rows_back, jnp.zeros((1, width), F32))
            give = remote(swap.at[0], swap.at[1], ex_sems.at[0], ex_sems.at[1], place.twin)
            give.start()
            give.wait_recv()
            d_attn[pl.ds(pl.multiple_of((1 - t) * own, own), own), :] = swap[1]
            give.wait_send()

    scratch = []
    for _, _, size, _, w in chunks:
        scratch += scatter_scratch(n, size, w)
    scratch += scatter_scratch(n, 2 * n, own)
    scratch += [
        pltpu.VMEM((2 * n, own), F32),
        pltpu.SemaphoreType.DMA((2,)),
        pltpu.VMEM((own, width), F32),
        pltpu.VMEM((2, own, width), BF16),
        pltpu.VMEM((own, width), BF16),
        pltpu.VMEM((own, width), BF16),
        *[pltpu.VMEM(a.shape, a.dtype) for a in (act, dge, due, s_act, d_spre)],
        pltpu.SemaphoreType.DMA((7,)),
    ]
    return grid_call(
        kernel,
        steps,
        [IN_HBM] * 3
        + [whole(a) for a in (sel, router_t, resid, gain)]
        + [IN_HBM] * 2
        + [by_cols(slots, cols)] * 2
        + [IN_HBM] * 5
        + [by_cols(n * seq, cols)] * 2,
        (
            (IN_VMEM, (1, width), F32),
            (IN_VMEM, (n, width), F32),
            (IN_VMEM, (own, width), F32),
            (IN_VMEM, (seq, width), BF16),
            (IN_HBM, (n, 2 * n, own), BF16),
            (by_cols(hidden, cols), (hidden, width), EXPERT_GRADS),
            (by_cols(hidden, cols), (hidden, width), EXPERT_GRADS),
            (by_cols(hidden, cols), (hidden, width), EXPERT_GRADS),
            (by_cols(3 * part, cols), (3 * part, width), BF16),
        ),
        scratch,
        6,
        "sum_row_gradients",
    )(
        dh_mine, dh_heap, gate_parts, sel, router_t, resid, gain, cot, normed_own,
        rows, dy, act, dge, due, s_act, d_spre,
        h_all.reshape(n * seq, width), cot_all.reshape(n * seq, width),
    )


EXPERT_GRADS = BF16


def attend_back(
    n, d_attn, x_seq, h1, latent, cn, gain_kv, k_rope, cos2, sin2, w_kvd,
    q_n, q_r, kv, ctx, w_q, w_kvu, w_out, g2_small, wr_small, g_shared, padded,
):
    seq, width = x_seq.shape
    head = DN + DR
    pairs = w_q.shape[1] // (2 * head)
    factor = 1.0 / math.sqrt(head)
    cols = width // n
    part_rows = g_shared.shape[0] // 3

    def kernel(*refs):
        take = pick(refs)
        da, x, h, lat, c_n, gk, kpe, co, si, wd, g2s, wrs = take(12)
        gsh, qn, qr, kvb, cx, wq, wu, wo = take(8)
        dh_out, g_kvd, small, sh_got = take(4)
        g_wq, g_wu, g_wo = take(3)
        trade_sems, dh, dcn, dkr, dq, dkv, dctx = take(7)
        place = Place(n)
        i = pl.program_id(0)
        trade = Trade(
            place,
            [
                lambda k, j=j: gsh.at[pl.ds(j * part_rows, padded), pl.ds(k * cols, cols)]
                for j in range(3)
            ],
            [lambda k, j=j: sh_got.at[k, j] for j in range(3)],
            trade_sems,
        )

        @pl.when(i == 0)
        def _():
            place.enter(everyone=True)
            trade.begin()
            dh[...] = jnp.zeros_like(dh)
            dcn[...] = jnp.zeros_like(dcn)
            dkr[...] = jnp.zeros_like(dkr)

        dctx[...] = dot_nt(da[...], wo[...]).astype(BF16)
        g_wo[...] = dot_tn(cx[...], da[...]).astype(BF16)
        for k in range(2):
            base = k * (DN + DV)
            keys, values = kvb[:, base : base + DN], kvb[:, base + DN : base + DN + DV]
            one_n, one_r = qn[:, k * DN : (k + 1) * DN], qr[:, k * DR : (k + 1) * DR]
            d_one = dctx[:, k * DV : (k + 1) * DV]
            weights = causal_weights(one_n, one_r, keys, kpe[...], factor)
            dw = dot_nt(d_one, values)
            ds = (weights * (dw - jnp.sum(weights * dw, axis=1, keepdims=True))).astype(BF16)
            dq[:, k * head : k * head + DN] = (dot_single_float(ds, keys) * factor).astype(BF16)
            d_rope = dot_single_float(ds, kpe[...]) * factor
            dq[:, k * head + DN : (k + 1) * head] = (
                d_rope * co[...] - swapped(d_rope) * si[...]
            ).astype(BF16)
            dkv[:, base : base + DN] = (dot_tn(ds, one_n) * factor).astype(BF16)
            dkr[...] += dot_tn(ds, one_r) * factor
            dkv[:, base + DN : base + DN + DV] = dot_tn(weights.astype(BF16), d_one).astype(BF16)
        g_wq[...] = dot_tn(h[...], dq[...]).astype(BF16)
        g_wu[...] = dot_tn(c_n[...], dkv[...]).astype(BF16)
        dcn[...] += dot_nt(dkv[...], wu[...])
        dh[...] += dot_nt(dq[...], wq[...])

        @pl.when(i == pairs - 1)
        def _():
            lt = lat[...]
            factor_kv = inv_rms(lt)
            back = dcn[...]
            g_gain = jnp.sum(back * lt * factor_kv, axis=0, keepdims=True)
            d_lat = norm_back(lt, factor_kv, gk[...], back)
            d_rope = dkr[...]
            d_rope = d_rope * co[...] - swapped(d_rope) * si[...]
            d_first = jnp.concatenate([d_lat, d_rope], 1).astype(BF16)
            g_kvd[...] = dot_tn(h[...], d_first).astype(BF16)
            dh[...] += dot_single_float(d_first, wd[...])
            size = 16

            def finish(j, acc):
                at = pl.ds(pl.multiple_of(j * size, size), size)
                v = x[at, :].astype(F32)
                one = dh[at, :]
                dh_out[at, :] = one.astype(BF16)
                return acc + jnp.sum(one * (v * inv_rms(v)), axis=0, keepdims=True)

            g_one = lax.fori_loop(0, seq // size, finish, jnp.zeros((1, width), F32))
            small[...] = jnp.zeros_like(small)
            kv_cols = KVR // n
            for o in range(n):
                at = slice(o * cols, (o + 1) * cols)
                small[o, 0:1, :] = g_one[:, at].astype(BF16)
                small[o, 1:2, :] = g2s[:, at].astype(BF16)
                small[o, 2:3, 0:kv_cols] = g_gain[:, o * kv_cols : (o + 1) * kv_cols].astype(BF16)
                small[o, 16 : 16 + n, :] = wrs[:, at].astype(BF16)
            trade.settle()

    scratch = [
        pltpu.SemaphoreType.DMA((2, n, 3)),
        pltpu.VMEM((seq, width), F32),
        pltpu.VMEM((seq, KVR), F32),
        pltpu.VMEM((seq, DR), F32),
        pltpu.VMEM((seq, 2 * head), BF16),
        pltpu.VMEM((seq, 2 * (DN + DV)), BF16),
        pltpu.VMEM((seq, 2 * DV), BF16),
    ]
    resident = (
        d_attn, x_seq, h1, latent, cn, gain_kv, k_rope, cos2, sin2, w_kvd, g2_small, wr_small,
    )
    return grid_call(
        kernel,
        pairs,
        [whole(a) for a in resident]
        + [
            IN_HBM,
            by_cols(seq, 2 * DN),
            by_cols(seq, 2 * DR),
            by_cols(seq, 2 * (DN + DV)),
            by_cols(seq, 2 * DV),
            by_cols(width, 2 * head),
            by_cols(KVR, 2 * (DN + DV)),
            by_rows(2 * DV, width),
        ],
        (
            (IN_VMEM, (seq, width), BF16),
            (IN_VMEM, (width, KVR + DR), BF16),
            (IN_VMEM, (n, 32, cols), BF16),
            (IN_HBM, (n, 3, padded, cols), BF16),
            (by_cols(width, 2 * head), w_q.shape, BF16),
            (by_cols(KVR, 2 * (DN + DV)), w_kvu.shape, BF16),
            (by_rows(2 * DV, width), w_out.shape, BF16),
        ),
        scratch,
        7,
        "attend_back",
    )(*resident, g_shared, q_n, q_r, kv, ctx, w_q, w_kvu, w_out)


def sum_weights(n, g_query, g_kvu, g_out, g_kvd, g_small, dh1, x_own, d_resid, gain, g_shared, hidden):
    q_rows, q_cols = g_query.shape[0] // n, g_query.shape[1]
    cut = q_cols // 4 * 3
    o_rows, o_cols = g_out.shape[0], g_out.shape[1] // n
    u_rows, u_cols = g_kvu.shape[0] // n, g_kvu.shape[1]
    d_rows, d_cols = g_kvd.shape[0] // (2 * n), g_kvd.shape[1]
    s_rows, s_cols = g_small.shape[1:]
    seq, width = dh1.shape
    own = seq // 2
    specs = [
        (0, (q_rows, cut)),
        (1, (q_rows, q_cols - cut)),
        (2, (o_rows, o_cols)),
        (1, (u_rows, u_cols)),
        (1, (d_rows, d_cols)),
        (2, (s_rows, s_cols)),
    ]

    def kernel(*refs):
        take = pick(refs)
        q, ku, wo, kd, sm, dh, x, dr, g, sh = take(10)
        q_out, ku_out, wo_out, kd_out, sm_out, in_out, sg_out, su_out, sd_out = take(9)
        kd_heap, sm_heap = take(2)
        scratch = [take(6) for _ in specs]
        got, swap_sems, turned = take(3)
        place = Place(n)
        t = place.t
        place.enter()
        swap = remote(
            dh.at[pl.ds((1 - t) * own, own)], got, swap_sems.at[0], swap_sems.at[1], place.twin
        )
        swap.start()
        views = [
            lambda o, u: q.at[pl.ds(o * q_rows, q_rows), pl.ds(0, cut)],
            lambda o, u: q.at[pl.ds(o * q_rows, q_rows), pl.ds(cut, q_cols - cut)],
            lambda o, u: wo.at[:, pl.ds(o * o_cols, o_cols)],
            lambda o, u: ku.at[pl.ds(o * u_rows, u_rows)],
            lambda o, u: kd.at[pl.ds((o * 2 + u) * d_rows, d_rows)],
            lambda o, u: sm.at[o],
        ]
        heaps = [None] * 4 + [lambda o: kd_heap.at[o], lambda o: sm_heap.at[o]]
        scatters = [
            Scatter(place, ring, shape, view, more, heap)
            for (ring, shape), view, more, heap in zip(specs, views, scratch, heaps)
        ]
        outs = [
            q_out.at[:, pl.ds(0, cut)],
            q_out.at[:, pl.ds(cut, q_cols - cut)],
            wo_out,
            ku_out,
            kd_out,
            sm_out,
        ]

        def grad_in():
            swap.wait_recv()
            size = 16

            def rows_back(j, _):
                at = pl.ds(pl.multiple_of(j * size, size), size)
                mine = pl.ds(pl.multiple_of(t * own + j * size, size), size)
                v = x[at, :].astype(F32)
                one = dh[mine, :].astype(F32) + got[at, :].astype(F32)
                in_out[at, :] = (dr[at, :] + norm_back(v, inv_rms(v), g[...], one)).astype(BF16)
                return 0

            lax.fori_loop(0, own // size, rows_back, 0)

        def put_together(j, out):
            for k in range(n):
                turned[k * hidden : (k + 1) * hidden, :] = sh[k, j, 0:hidden, :].astype(F32)
            if j < 2:
                out[...] = dot_nt(eye(q_rows), turned[...].astype(BF16))
            else:
                out[...] = turned[...]

        beside = [grad_in] + [
            lambda j=j, out=out: put_together(j, out)
            for j, out in enumerate((sg_out, su_out, sd_out))
        ]
        run_scatters(place, scatters, outs, beside)
        swap.wait_send()

    scratch = []
    for _, shape in specs:
        scratch += scatter_scratch(n, *shape)
    scratch += [
        pltpu.VMEM((own, width), BF16),
        pltpu.SemaphoreType.DMA((2,)),
        pltpu.VMEM((n * hidden, q_rows), F32),
    ]
    return comm_call(
        kernel,
        (
            sds((q_rows, q_cols), F32),
            sds((u_rows, u_cols), F32),
            sds((o_rows, o_cols), F32),
            sds((d_rows, d_cols), F32),
            sds((s_rows, s_cols), F32),
            sds((own, width), BF16),
            sds((q_rows, n * hidden), F32),
            sds((q_rows, n * hidden), F32),
            sds((n * hidden, q_rows), F32),
            sds((n, d_rows, d_cols), BF16),
            sds((n, s_rows, s_cols), BF16),
        ),
        (IN_VMEM,) * 9 + (IN_HBM,) * 2,
        [IN_HBM] * 5 + [IN_VMEM] * 5,
        scratch,
        8,
        "sum_weights",
    )(g_query, g_kvu, g_out, g_kvd, g_small, dh1, x_own, d_resid, gain, g_shared)[:9]


def finish(results, small, kept, experts):
    t_cols = small.shape[1] // 2
    n = small.shape[0] - 16
    hidden, width = experts[0].shape
    steps = 4
    rows = hidden // steps
    count = len(results)

    def kernel(*refs):
        take = pick(refs)
        came, (sm,), parts = take(count), take(1), take(3)
        outs, (g1, g2, gk, gr), wide = take(count), take(4), take(3)

        @pl.when(pl.program_id(0) == 0)
        def _():
            lower = lax.axis_index("tp") == 0
            mine = jnp.where(lower, sm[:, :t_cols], sm[:, t_cols:])
            g1[...] = mine[0:1, :]
            g2[...] = mine[1:2, :]
            gk[...] = jnp.where(lower, sm[2:3, :kept], sm[2:3, kept : 2 * kept])
            gr[...] = mine[16 : 16 + n, :]

        for one, out in zip(came, outs):
            out[...] = one[...]
        for part, out in zip(parts, wide):
            out[...] = part[...].astype(F32)

    def spec(*shape):
        return pl.BlockSpec(shape, lambda i: (0, 0))

    blocks = [by_rows(a.shape[0] // steps, a.shape[1]) for a in results]
    return pl.pallas_call(
        kernel,
        grid=(steps,),
        in_specs=blocks + [spec(*small.shape)] + [by_rows(rows, width)] * 3,
        out_specs=tuple(blocks)
        + (spec(1, t_cols), spec(1, t_cols), spec(1, kept), spec(n, t_cols))
        + (by_rows(rows, width),) * 3,
        out_shape=tuple(sds(a.shape, a.dtype) for a in results)
        + (sds((1, t_cols), F32), sds((1, t_cols), F32), sds((1, kept), F32), sds((n, t_cols), F32))
        + (sds((hidden, width), F32),) * 3,
        compiler_params=pltpu.CompilerParams(vmem_limit_bytes=VMEM_BYTES),
        name="finish",
    )(*results, small, *experts)


def rope_constants(length):
    half_width = DR // 2
    freq = np.float32(ROPE_THETA) ** -(np.arange(half_width, dtype=np.float32) * 2 / DR)
    angle = np.arange(length, dtype=np.float32)[:, None] * freq.astype(np.float32)[None, :]
    cos_table, sin_table = np.cos(angle), np.sin(angle)
    return (
        jnp.asarray(np.concatenate([cos_table, cos_table], 1), F32),
        jnp.asarray(np.concatenate([-sin_table, sin_table], 1), F32),
    )


def fast(
    hidden_in,
    routes,
    cotangent,
    norm_attn,
    query_proj,
    kv_down,
    kv_norm,
    kv_up,
    out_proj,
    norm_ffn,
    router_proj,
    shared_gate,
    shared_up,
    shared_down,
    expert_gate,
    expert_up_weight,
    expert_down,
):
    n = lax.axis_size("fsdp")
    own, width = hidden_in.shape
    seq = 2 * own
    cap = 4 * seq * TOP // (3 * n)
    cos2, sin2 = rope_constants(seq)
    latent_rows = kv_norm.shape[0]
    hidden = shared_gate.shape[1] // n

    full_wq, full_wkva, full_wkvb, full_wo, small_all, x_seq, blocks = collect_inputs(
        n,
        query_proj,
        kv_down.T,
        kv_up,
        out_proj,
        hidden_in,
        norm_attn[None],
        norm_ffn[None],
        kv_norm[None],
        router_proj.T,
        routes.T,
        shared_gate,
        shared_up,
        shared_down,
    )
    (
        resid, sel, full_g2, router_t, normed_own, gates_own, h1, full_g1, full_gkv, latent,
        latent_normed, key_rope, shared_w, q_n, q_r, kv, context,
    ) = attend(
        n, x_seq, hidden_in, small_all, full_wkva, cos2, sin2, full_wq, full_wkvb, full_wo, blocks
    )
    w_gate, w_up, w_down = expert_gate[0].T, expert_up_weight[0].T, expert_down[0]
    (
        rows, act, act_gate, on_up, on_gate, sh_act, sh_on, gate,
        place_table, out_mine, out_heap, cot_all, h_all, _,
    ) = expert_forward(
        n, normed_own, gates_own, small_all, cap, w_gate, w_up, w_down, shared_w, cotangent
    )
    (
        hidden_out, dh_mine, dh_heap, cot_rows, d_pre_gate, d_pre_up, d_sh_pre, d_gates,
    ) = expert_back(
        out_mine, out_heap, resid, cot_all, place_table, gate, act, on_up, on_gate, sh_on,
        w_gate, w_up, w_down, shared_w,
    )
    (
        grad_g2, grad_wr, d_resid, d_attn, _, grad_egate, grad_eup, grad_edown, grad_shared,
    ) = sum_rows(
        dh_mine, dh_heap, d_gates, sel, router_t, resid, full_g2, cotangent, normed_own,
        rows, cot_rows, act_gate, d_pre_gate, d_pre_up, sh_act, d_sh_pre, h_all, cot_all,
    )
    dh1_part, grad_wkva, grad_small, out_shared, grad_wq, grad_wkvb, grad_wo = attend_back(
        n, d_attn, x_seq, h1, latent, latent_normed, full_gkv, key_rope, cos2, sin2, full_wkva,
        q_n, q_r, kv, context, full_wq, full_wkvb, full_wo, grad_g2, grad_wr, grad_shared,
        blocks.shape[2],
    )
    (
        out_wq, out_wkvb, out_wo, out_wkva, out_small, grad_in, out_sgate, out_sup, out_sdown,
    ) = sum_weights(
        n, grad_wq, grad_wkvb, grad_wo, grad_wkva, grad_small, dh1_part, hidden_in, d_resid,
        full_g1, out_shared, hidden,
    )
    (
        hidden_out, grad_in, out_wq, out_wkva, out_wkvb, out_wo, out_sgate, out_sup, out_sdown,
        out_g1, out_g2, out_gkv, out_wr, grad_egate, grad_eup, grad_edown,
    ) = finish(
        (hidden_out, grad_in, out_wq, out_wkva, out_wkvb, out_wo, out_sgate, out_sup, out_sdown),
        out_small, latent_rows // 2, (grad_egate, grad_eup, grad_edown),
    )
    return (
        hidden_out,
        grad_in,
        out_g1[0],
        out_wq,
        out_wkva,
        out_gkv[0],
        out_wkvb,
        out_wo,
        out_g2[0],
        out_wr.T,
        out_sgate,
        out_sup,
        out_sdown,
        grad_egate.T[None],
        grad_eup.T[None],
        grad_edown[None],
    )


def suits(mesh):
    return mesh.shape["tp"] == 2 and mesh.shape["fsdp"] * 128 == MODEL_WIDTH


def solution(mesh):
    return jax.shard_map(
        fast if suits(mesh) else plain,
        mesh=mesh,
        in_specs=(
            P(("fsdp", "tp"), None),
            P("fsdp", None),
            P("fsdp", None),
            P("fsdp"),
            P("fsdp", "tp"),
            P("fsdp", None),
            P("fsdp"),
            P("fsdp", "tp"),
            P("tp", "fsdp"),
            P("fsdp"),
            P("fsdp", None),
            P("fsdp", "tp"),
            P("fsdp", "tp"),
            P("tp", "fsdp"),
            P("fsdp", None, "tp"),
            P("fsdp", None, "tp"),
            P("fsdp", "tp", None),
        ),
        out_specs=(
            P(("fsdp", "tp"), None),
            P(("fsdp", "tp"), None),
            P(("fsdp", "tp")),
            P("fsdp", "tp"),
            P(("fsdp", "tp"), None),
            P(("fsdp", "tp")),
            P("fsdp", "tp"),
            P("tp", "fsdp"),
            P(("fsdp", "tp")),
            P(("fsdp", "tp"), None),
            P("fsdp", "tp"),
            P("fsdp", "tp"),
            P("tp", "fsdp"),
            P("fsdp", None, "tp"),
            P("fsdp", None, "tp"),
            P("fsdp", "tp", None),
        ),
        check_vma=False,
    )
```
